32 devices in a mesh: path: 4 (over y, x), dev: 8 (over z, core).
Axes of the slice: x: 2, y: 2, z: 4, core: 2. Of those that a mesh axis runs over, the one named last changes fastest.
Arguments:
- inputs: bfloat16 [32, 144, 1024], P(('path', 'dev')), may hold values from -6 to 6
- hires_maps: bfloat16 [32, 24, 24, 1536], P(('path', 'dev')), may hold values from -6 to 6
- target_path: int32 [4, 8], P('path', 'dev'), may hold values from 0 to 3, as said below
- cotangent: bfloat16 [32, 144, 1024], P(('path', 'dev')), may hold values from -6 to 6
- attn_gain: float32 [1024], replicated, may hold values from 0.5 to 1.5
- w_qkv: bfloat16 [1024, 3072], P('dev'), may hold values from -0.1875 to 0.1875
- w_out: bfloat16 [1024, 1024], P('dev'), may hold values from -0.5 to 0.5
- mlp_gain: float32 [1024], replicated, may hold values from 0.5 to 1.5
- w_fc1: bfloat16 [1024, 4096], P('dev'), may hold values from -0.1875 to 0.1875
- w_fc2: bfloat16 [4096, 1024], P('dev'), may hold values from -0.09375 to 0.09375
- w_adapter: bfloat16 [1536, 1024], P('dev'), may hold values from -0.15625 to 0.15625
- adapter_kernel: float32 [9, 1024], replicated, may hold values from -3 to 3
- merge_gate: float32 [1024], replicated, may hold values from 0.5 to 1.5
- section_kernel: float32 [49, 1536], replicated, may hold values from -1 to 1
- section_gain: float32 [1536], replicated, may hold values from 0.5 to 1.5
- w_expand: bfloat16 [1536, 6144], P('dev'), may hold values from -0.15625 to 0.15625
- w_reduce: bfloat16 [6144, 1536], P('dev'), may hold values from -0.078125 to 0.078125
- layer_scale: float32 [1536], replicated, may hold values from 0.5 to 1
Outputs:
- output: bfloat16 [32, 144, 1024], P(('path', 'dev'))
- grad_inputs: float32 [32, 144, 1024], P(('path', 'dev'))
- grad_hires_maps: float32 [32, 24, 24, 1536], P(('path', 'dev'))
- grad_attn_gain: float32 [1024], replicated
- grad_w_qkv: float32 [1024, 3072], P('dev')
- grad_w_out: float32 [1024, 1024], P('dev')
- grad_mlp_gain: float32 [1024], replicated
- grad_w_fc1: float32 [1024, 4096], P('dev')
- grad_w_fc2: float32 [4096, 1024], P('dev')
- grad_w_adapter: float32 [1536, 1024], P('dev')
- grad_adapter_kernel: float32 [9, 1024], replicated
- grad_merge_gate: float32 [1024], replicated
- grad_section_kernel: float32 [49, 1536], replicated
- grad_section_gain: float32 [1536], replicated
- grad_w_expand: float32 [1536, 6144], P('dev')
- grad_w_reduce: float32 [6144, 1536], P('dev')
- grad_layer_scale: float32 [1536], replicated
The draws below stay inside these ranges and needn't reach their ends.
Inputs may be any that keep to these rules, and one draw needn't show every extreme that they name: For every d, the column target_path[:, d] is a permutation of 0 to 3.
All inputs are finite; a program needn't handle non-finite values.
Results may differ from the reference program's by a relative error of at most 0.02.
Values may be sent and summed in bfloat16 or wider, within the bound.
A program may use at most 512 MiB of HBM per device.

```python
from functools import partial
import jax
import jax.numpy as jnp
from jax import lax

D = 1024
HEADS = 16
HEAD_DIM = 64
FF = 4096
C = 1536
CF = 6144
GRID = 12
TOK = 144
HR = 24
IMAGES = 32
N_PATH = 4
N_DEV = 8


def draw_target_path(key, part):
    column_keys = jax.random.split(jax.random.fold_in(key, 17), N_DEV)
    orders = jax.vmap(lambda column_key: jax.random.permutation(column_key, N_PATH))(column_keys)
    return orders.T.astype(jnp.int32)


def level_of(own_key, shape, cuts, least, high):
    level = 1.0
    for position, blocks in cuts:
        steps = jax.random.uniform(jax.random.fold_in(jax.random.fold_in(own_key, 6), position), (blocks,), jnp.float32, least / len(cuts), high / len(cuts))
        level = level * jnp.repeat(jnp.exp(steps), shape[position] // blocks).reshape((-1,) + (1,) * (len(shape) - 1 - position))
    return level


def noise(own_key, dims, scale, reach, cuts=(), kind=jnp.bfloat16):
    loudness = level_of(own_key, dims, cuts, -0.22, 0.18) if cuts else 1.0
    array = jax.random.normal(own_key, dims, jnp.float32) * scale * loudness
    return jnp.minimum(jnp.maximum(array, -reach), reach).astype(kind)


def setup_inputs(seed: int = 0) -> dict:
    streams_of = jax.random.split(jax.random.key(seed), 19)
    inputs = noise(streams_of[0], (IMAGES, TOK, D), 1.0, 6.0, ((0, 32),))
    hires_maps = noise(streams_of[1], (IMAGES, HR, HR, C), 1.0, 6.0, ((0, 32),))
    target_path = draw_target_path(jax.random.fold_in(streams_of[18], 71), 0)
    cotangent = noise(streams_of[3], (IMAGES, TOK, D), 1.0, 6.0, ((0, 32),))
    attn_gain = jnp.clip(1.0 + 0.1 * jax.random.normal(streams_of[4], (D,), jnp.float32), 0.5, 1.5)
    w_qkv = noise(streams_of[5], (D, 3 * D), D ** -0.5, 0.1875, ((0, 8),))
    w_out = noise(streams_of[6], (D, D), (D // 8) ** -0.5, 0.5, ((0, 8),))
    mlp_gain = jnp.clip(1.0 + 0.1 * jax.random.normal(streams_of[7], (D,), jnp.float32), 0.5, 1.5)
    w_fc1 = noise(streams_of[8], (D, FF), D ** -0.5, 0.1875, ((0, 8),))
    w_fc2 = noise(streams_of[9], (FF, D), FF ** -0.5, 0.09375, ((0, 8),))
    w_adapter = noise(streams_of[10], (C, D), C ** -0.5, 0.15625, ((0, 8),))
    adapter_kernel = noise(streams_of[11], (9, D), 0.35, 3.0, (), jnp.float32)
    merge_gate = jnp.clip(jax.random.uniform(streams_of[12], (D,), jnp.float32, 0.5, 1.5), 0.5, 1.5)
    section_kernel = noise(streams_of[13], (49, C), 0.15, 1.0, (), jnp.float32)
    section_gain = jnp.clip(1.0 + 0.1 * jax.random.normal(streams_of[14], (C,), jnp.float32), 0.5, 1.5)
    w_expand = noise(streams_of[15], (C, CF), C ** -0.5, 0.15625, ((0, 8),))
    w_reduce = noise(streams_of[16], (CF, C), CF ** -0.5, 0.078125, ((0, 8),))
    layer_scale = jnp.clip(jax.random.uniform(streams_of[17], (C,), jnp.float32, 0.5, 1.0), 0.5, 1.0)
    return dict(inputs=inputs, hires_maps=hires_maps, target_path=target_path, cotangent=cotangent, attn_gain=attn_gain, w_qkv=w_qkv, w_out=w_out, mlp_gain=mlp_gain, w_fc1=w_fc1, w_fc2=w_fc2, w_adapter=w_adapter, adapter_kernel=adapter_kernel, merge_gate=merge_gate, section_kernel=section_kernel, section_gain=section_gain, w_expand=w_expand, w_reduce=w_reduce, layer_scale=layer_scale)


@jax.custom_vjp
def low(v):
    return lax.optimization_barrier(v.astype(jnp.bfloat16)).astype(jnp.float32)

@jax.custom_vjp
def low_back(v):
    return v

def low_keep(v):
    return (low(v), None)

def low_pass(kept, grad):
    return (grad,)

def back_keep(v):
    return (v, None)

def back_low(kept, grad):
    return (low(grad),)
low.defvjp(low_keep, low_pass)
low_back.defvjp(back_keep, back_low)

def layer_norm(values, gain_vec):
    centred = values - lax.optimization_barrier(jnp.mean(values, axis=-1, keepdims=True))
    spread = lax.optimization_barrier(jnp.mean(centred * centred, axis=-1, keepdims=True))
    return centred * lax.rsqrt(spread + 1e-06) * gain_vec

def depthwise(feature_map, taps_table, kernel_side):
    half_side = kernel_side // 2
    padded = jnp.pad(feature_map, ((0, 0), (half_side, half_side), (half_side, half_side), (0, 0)))
    map_side = feature_map.shape[1]
    accum_sum = jnp.zeros(feature_map.shape, feature_map.dtype)
    for offset_row in range(kernel_side):
        for offset_col in range(kernel_side):
            window = padded[:, offset_row:offset_row + map_side, offset_col:offset_col + map_side, :]
            accum_sum = accum_sum + window * taps_table[offset_row * kernel_side + offset_col]
    return accum_sum

def product(left_rows, right_matrix):
    return jnp.einsum('...i,ij->...j', left_rows, right_matrix, precision=lax.Precision.HIGHEST)

def forward(inputs, maps, weights, inverse):
    attn_gain, w_qkv, w_out, mlp_gain, w_fc1, w_fc2, w_adapter, adapter_kernel, merge_gate, section_kernel, section_gain, w_expand, w_reduce, layer_scale = weights
    section_mixed = depthwise(maps, section_kernel, 7)
    section_rows = low(layer_norm(section_mixed, section_gain))
    expanded = low_back(product(section_rows, w_expand))
    activated = low(jax.nn.gelu(expanded))
    reduced = low_back(product(activated, w_reduce))
    section_out = maps + layer_scale * reduced
    pooled = lax.optimization_barrier(jnp.mean(section_out.reshape(IMAGES, GRID, 2, GRID, 2, C), axis=(2, 4)))
    shipped = low_back(low(pooled)).reshape(IMAGES, TOK, C)
    features = shipped[inverse]
    adapted = low_back(product(features, w_adapter))
    spread_rows = depthwise(adapted.reshape(IMAGES, GRID, GRID, D), adapter_kernel, 3).reshape(IMAGES, TOK, D)
    hidden_in = inputs + jnp.tanh(merge_gate) * spread_rows
    attn_rows = low(layer_norm(hidden_in, attn_gain))
    projected = low(low_back(product(attn_rows, w_qkv)))
    queries = projected[..., :D].reshape(IMAGES, TOK, HEADS, HEAD_DIM)
    key_rows = projected[..., D:2 * D].reshape(IMAGES, TOK, HEADS, HEAD_DIM)
    values = projected[..., 2 * D:].reshape(IMAGES, TOK, HEADS, HEAD_DIM)
    scores = low_back(jnp.einsum('ithd,ishd->ihts', queries, key_rows, precision=lax.Precision.HIGHEST) * HEAD_DIM ** (-0.5))
    probs_low = low(jax.nn.softmax(scores, axis=-1))
    attn_mixed = low(low_back(jnp.einsum('ihts,ishd->ithd', probs_low, values, precision=lax.Precision.HIGHEST)))
    attn_mixed = attn_mixed.reshape(IMAGES, TOK, D)
    hidden_mid = hidden_in + low_back(product(attn_mixed, w_out))
    mlp_rows = low(layer_norm(hidden_mid, mlp_gain))
    raised = low_back(product(mlp_rows, w_fc1))
    lifted = low(jax.nn.gelu(raised))
    return hidden_mid + low_back(product(lifted, w_fc2))

def reference(inputs, hires_maps, target_path, cotangent, attn_gain, w_qkv, w_out, mlp_gain, w_fc1, w_fc2, w_adapter, adapter_kernel, merge_gate, section_kernel, section_gain, w_expand, w_reduce, layer_scale):
    flat_target = target_path.reshape(-1).astype(jnp.int32)
    image_ids = jnp.arange(IMAGES, dtype=jnp.int32)
    destination = flat_target * N_DEV + image_ids % N_DEV
    inverse = jnp.zeros((IMAGES,), jnp.int32).at[destination].set(image_ids)
    weights = (attn_gain.astype(jnp.float32), w_qkv.astype(jnp.float32), w_out.astype(jnp.float32), mlp_gain.astype(jnp.float32), w_fc1.astype(jnp.float32), w_fc2.astype(jnp.float32), w_adapter.astype(jnp.float32), adapter_kernel.astype(jnp.float32), merge_gate.astype(jnp.float32), section_kernel.astype(jnp.float32), section_gain.astype(jnp.float32), w_expand.astype(jnp.float32), w_reduce.astype(jnp.float32), layer_scale.astype(jnp.float32))
    result, backward = jax.vjp(partial(forward, inverse=inverse), inputs.astype(jnp.float32), hires_maps.astype(jnp.float32), weights)
    grad_inputs, grad_maps, grads = backward(cotangent.astype(jnp.float32))
    return (result.astype(jnp.bfloat16), grad_inputs, grad_maps, grads[0], grads[1], grads[2], grads[3], grads[4], grads[5], grads[6], grads[7], grads[8], grads[9], grads[10], grads[11], grads[12], grads[13])
```

```python
import functools

import jax
import jax.numpy as jnp
from jax import lax
from jax.experimental import pallas as pl
from jax.experimental.pallas import tpu as pltpu
from jax.sharding import PartitionSpec as P

HEAD_DIM = 64
MESH = pl.DeviceIdType.MESH

def gather_jobs(shapes):
    jobs = []
    for w, (r, n) in enumerate(shapes):
        q = r // 4
        size = q * n
        parts = max(1, round(size / (16 * 6144)))
        while parts > 1 and (n // 2) % (parts * 128): parts -= 1
        for k in range(parts):
            jobs.append((w, q, k * (n // parts), n // parts))
    return jobs

def gather_kernel(jobs, count, *refs):
    shards = refs[:count]; fulls = refs[count:2*count]
    zs, zr, ps, pr, cs, cr, ls = refs[2*count:]
    p = lax.axis_index("path"); d = lax.axis_index("dev")
    masks = [(0,1),(0,2),(0,4),(0,6),(1,0),(2,0)]
    def at(m): return (p ^ m[0], d ^ m[1])
    bar = pltpu.get_barrier_semaphore()
    for m in masks: pl.semaphore_signal(bar, inc=1, device_id=at(m), device_id_type=MESH)
    pl.semaphore_wait(bar, len(masks))
    def rows(w, owner):
        r = shards[w].shape[0]; return r, owner * r
    def copy(src, dst, ss, rs, m):
        return pltpu.make_async_remote_copy(src, dst, ss, rs, device_id=at(m), device_id_type=MESH)
    def quarter(w, owner, q, nq, c0, nc):
        r = shards[w].shape[0]
        return fulls[w].at[pl.ds(pl.multiple_of(owner * r + q * nq, 16), nq), pl.ds(c0, nc)]
    own = []
    for w in range(count):
        r = shards[w].shape[0]
        place = fulls[w].at[pl.ds(pl.multiple_of(d * r, 16), r)]
        a = pltpu.make_async_copy(shards[w], place, ls.at[w]); a.start()
        b = copy(shards[w], place, cs.at[w, 0], cr.at[w, 0], (0,1)); b.start()
        own.append((a, b))
    J = len(jobs)
    def Z(i, k):
        w, nq, c0, nc = jobs[i]
        return copy(shards[w].at[pl.ds(pl.multiple_of(p * nq, 16), nq), pl.ds(c0, nc)], quarter(w, d, p, nq, c0, nc), zs.at[i,k], zr.at[i,k], (0, 2*(k+1)))
    def XY(i, k, axis):
        w, nq, c0, nc = jobs[i]
        ref = quarter(w, d ^ (2*(k+1)), p, nq, c0, nc)
        return copy(ref, ref, ps.at[i,k,axis], pr.at[i,k,axis], (1+axis, 0))
    def DG(i, k, axis):
        w, nq, c0, nc = jobs[i]
        h = nc // 2
        ref = quarter(w, d ^ (2*(k+1)), p ^ (2 - axis), nq, c0 + axis * h, h)
        return copy(ref, ref, ps.at[i,k,2+axis], pr.at[i,k,2+axis], (1+axis, 0))
    def S(w, k):
        r = shards[w].shape[0]
        ref = fulls[w].at[pl.ds(pl.multiple_of((d ^ (2*(k+1))) * r, 16), r)]
        return copy(ref, ref, cs.at[w,1+k], cr.at[w,1+k], (0,1))
    last = {}
    for i,(w,*_) in enumerate(jobs): last[w] = i
    AHEAD = 2
    for i in range(min(AHEAD, J)):
        for k in range(3): Z(i,k).start()
    sent = []
    for i in range(J + 2):
        if i < J:
            for k in range(3):
                Z(i,k).wait_recv()
                XY(i,k,0).start(); XY(i,k,1).start()
            if i + AHEAD < J:
                for k in range(3): Z(i+AHEAD,k).start()
        if 0 <= i-1 < J:
            for k in range(3):
                XY(i-1,k,0).wait_recv(); DG(i-1,k,1).start()
                XY(i-1,k,1).wait_recv(); DG(i-1,k,0).start()
        if 0 <= i-2 < J:
            for k in range(3):
                DG(i-2,k,0).wait_recv(); DG(i-2,k,1).wait_recv()
            w = jobs[i-2][0]
            if last[w] == i-2:
                for k in range(3): S(w,k).start()
    for w in range(count):
        own[w][0].wait(); own[w][1].wait()
        for k in range(3): S(w,k).wait()
    for i in range(J):
        for k in range(3):
            Z(i,k).wait_send()
            for a in range(2): XY(i,k,a).wait_send(); DG(i,k,a).wait_send()

def gather_weights(shards, collective_id=0):
    shapes = [s.shape for s in shards]
    jobs = gather_jobs(shapes); n = len(shards); J = len(jobs)
    anyspec = pl.BlockSpec(memory_space=pl.ANY)
    return pl.pallas_call(
        functools.partial(gather_kernel, jobs, n),
        out_shape=[jax.ShapeDtypeStruct((8*r, c), jnp.bfloat16) for r, c in shapes],
        in_specs=[anyspec]*n, out_specs=[anyspec]*n,
        scratch_shapes=[pltpu.SemaphoreType.DMA((J,3)),pltpu.SemaphoreType.DMA((J,3)),
            pltpu.SemaphoreType.DMA((J,3,4)),pltpu.SemaphoreType.DMA((J,3,4)),
            pltpu.SemaphoreType.DMA((n,4)),pltpu.SemaphoreType.DMA((n,4)),pltpu.SemaphoreType.DMA((n,))],
        compiler_params=pltpu.CompilerParams(collective_id=collective_id, has_side_effects=True),
    )(*shards)


def layer_norm(values, gain_vec):
    centred = values - jnp.mean(values, axis=-1, keepdims=True)
    spread = jnp.mean(centred * centred, axis=-1, keepdims=True)
    return centred * lax.rsqrt(spread + 1e-06) * gain_vec


def depthwise(feature_map, taps_table, kernel_side):
    half_side = kernel_side // 2
    padded = jnp.pad(feature_map, ((0, 0), (half_side, half_side), (half_side, half_side), (0, 0)))
    map_side = feature_map.shape[1]
    accum_sum = jnp.zeros(feature_map.shape, feature_map.dtype)
    for offset_row in range(kernel_side):
        for offset_col in range(kernel_side):
            window = padded[
                :, offset_row : offset_row + map_side, offset_col : offset_col + map_side, :
            ]
            accum_sum = accum_sum + window * taps_table[offset_row * kernel_side + offset_col]
    return accum_sum


def section_depthwise(grid_field, grid_kernel):
    return depthwise(grid_field, grid_kernel, 7)


def adapter_depthwise(grid_field, grid_kernel):
    return depthwise(grid_field, grid_kernel, 3)


def gather_all(shards, tuned):
    if tuned:
        return gather_weights(shards)
    return [lax.all_gather(shard, "dev", axis=0, tiled=True) for shard in shards]


def swap(value, axis, mask):
    size = lax.axis_size(axis)
    return lax.ppermute(value, axis, [(i, i ^ mask) for i in range(size)])


def pick(value, index, axis):
    return lax.dynamic_index_in_dim(value, index, axis, keepdims=False)


def add_low(left, right):
    return (left.astype(jnp.float32) + right.astype(jnp.float32)).astype(jnp.bfloat16)


def pair_gradient(rows, grads):
    side = lax.rem(lax.axis_index("dev"), 2)
    tokens, depth = rows.shape
    split = rows.reshape(tokens, 4, 2, depth // 8)
    mine = pick(split, side, 2)
    theirs = swap(pick(split, 1 - side, 2), "dev", 1)
    both_rows = jnp.concatenate([mine.reshape(tokens, depth // 2), theirs.reshape(tokens, depth // 2)])
    both_grads = jnp.concatenate([grads, swap(grads, "dev", 1)])
    product = lax.dot_general(
        both_rows, both_grads, (((0,), (0,)), ((), ())), preferred_element_type=jnp.float32
    )
    return product.astype(jnp.bfloat16).reshape(4, depth // 8, grads.shape[1])


def plane_first(share):
    path = lax.axis_index("path")
    up, across = path // 2, lax.rem(path, 2)
    height = lax.axis_index("dev") // 2
    _, rows, columns = share.shape
    view = share.reshape(4, 2, 2, rows // 4, columns)
    left, right = view[..., : columns // 2], view[..., columns // 2 :]
    left = add_low(pick(left, across, 2), swap(pick(left, 1 - across, 2), "path", 1))
    right = add_low(pick(right, up, 1), swap(pick(right, 1 - up, 1), "path", 2))
    left = add_low(pick(left, up, 1), swap(pick(left, 1 - up, 1), "path", 2))
    right = add_low(pick(right, across, 1), swap(pick(right, 1 - across, 1), "path", 1))
    quarter = jnp.concatenate([left, right], axis=-1)
    total = pick(quarter, height, 0).astype(jnp.float32)
    for mask in (1, 2, 3):
        total = total + swap(pick(quarter, height ^ mask, 0), "dev", 2 * mask).astype(jnp.float32)
    low = total.astype(jnp.bfloat16)
    pieces = jnp.stack([low] + [swap(low, "path", mask) for mask in (1, 2, 3)])
    order = jnp.arange(4, dtype=jnp.int32) ^ path
    return jnp.concatenate([pick(pieces, order[i], 0) for i in range(4)]).astype(jnp.float32)


def summed_gradient(rows, grads, tuned, plane):
    if tuned and plane:
        return plane_first(pair_gradient(rows, grads))
    product = lax.dot_general(
        rows, grads, (((0,), (0,)), ((), ())), preferred_element_type=jnp.float32
    ).astype(jnp.bfloat16)
    share = lax.psum_scatter(product, "dev", scatter_dimension=0, tiled=True)
    return lax.psum(share, "path").astype(jnp.float32)


def local(
    inputs,
    hires_maps,
    target_path,
    cotangent,
    attn_gain,
    w_qkv,
    w_out,
    mlp_gain,
    w_fc1,
    w_fc2,
    w_adapter,
    adapter_kernel,
    merge_gate,
    section_kernel,
    section_gain,
    w_expand,
    w_reduce,
    layer_scale,
):
    tuned = lax.axis_size("path") == 4 and lax.axis_size("dev") == 8
    full_expand, full_reduce, full_adapter, full_qkv, full_out, full_fc1, full_fc2 = gather_all(
        (w_expand, w_reduce, w_adapter, w_qkv, w_out, w_fc1, w_fc2), tuned
    )
    path_count = lax.axis_size("path")
    maps_float = hires_maps.astype(jnp.float32)
    map_side = maps_float.shape[1]
    channels = maps_float.shape[3]
    grid_side = map_side // 2
    tokens = grid_side * grid_side
    quarter_rows = tokens // path_count
    model_width = inputs.shape[2]
    head_count = model_width // HEAD_DIM
    score_scale = HEAD_DIM ** (-0.5)
    section_mixed, section_back = jax.vjp(section_depthwise, maps_float, section_kernel)
    section_normed, section_norm_back = jax.vjp(layer_norm, section_mixed, section_gain)
    section_rows = section_normed.reshape(-1, channels).astype(jnp.bfloat16)
    expanded = jnp.dot(section_rows, full_expand, preferred_element_type=jnp.float32)
    activated, section_gelu_back = jax.vjp(jax.nn.gelu, expanded)
    activated_low = activated.astype(jnp.bfloat16)
    reduced = jnp.dot(activated_low, full_reduce, preferred_element_type=jnp.float32).reshape(
        maps_float.shape
    )
    section_out = maps_float + layer_scale * reduced
    pooled = jnp.mean(
        section_out.reshape(grid_side, 2, grid_side, 2, channels), axis=(1, 3)
    ).reshape(tokens, channels)
    pieces = pooled.astype(jnp.bfloat16).reshape(path_count, quarter_rows, channels)
    own_target = jnp.broadcast_to(target_path, (path_count, 1))
    spread_pieces, spread_targets = (
        lax.all_to_all(pieces, "path", split_axis=0, concat_axis=0, tiled=True),
        lax.all_to_all(own_target, "path", split_axis=0, concat_axis=0, tiled=True),
    )
    selector = (
        jnp.arange(path_count, dtype=jnp.int32)[:, None] == spread_targets.reshape(1, path_count)
    ).astype(jnp.float32)
    routed = jnp.einsum("pq,qtc->ptc", selector, spread_pieces.astype(jnp.float32)).astype(
        jnp.bfloat16
    )
    arrived = lax.all_to_all(routed, "path", split_axis=0, concat_axis=0, tiled=True)
    features = arrived.reshape(tokens, channels)
    adapted = jnp.dot(features, full_adapter, preferred_element_type=jnp.float32)
    spread_map, adapter_back = jax.vjp(
        adapter_depthwise, adapted.reshape(1, grid_side, grid_side, model_width), adapter_kernel
    )
    spread_rows = spread_map.reshape(tokens, model_width)
    gate_factor = jnp.tanh(merge_gate)
    hidden_in = inputs[0].astype(jnp.float32) + gate_factor * spread_rows
    normed_one, norm_one_back = jax.vjp(layer_norm, hidden_in, attn_gain)
    attn_rows = normed_one.astype(jnp.bfloat16)
    projected = jnp.dot(attn_rows, full_qkv, preferred_element_type=jnp.float32).astype(
        jnp.bfloat16
    )
    queries = projected[:, :model_width].reshape(tokens, head_count, HEAD_DIM)
    key_rows = projected[:, model_width : 2 * model_width].reshape(tokens, head_count, HEAD_DIM)
    values = projected[:, 2 * model_width :].reshape(tokens, head_count, HEAD_DIM)
    scores = (
        jnp.einsum("thd,shd->hts", queries, key_rows, preferred_element_type=jnp.float32)
        * score_scale
    )
    probs = jax.nn.softmax(scores, axis=-1)
    probs_low = probs.astype(jnp.bfloat16)
    attn_mixed = jnp.einsum("hts,shd->thd", probs_low, values, preferred_element_type=jnp.float32)
    attn_mixed = attn_mixed.astype(jnp.bfloat16).reshape(tokens, model_width)
    attended = jnp.dot(attn_mixed, full_out, preferred_element_type=jnp.float32)
    hidden_mid = hidden_in + attended
    normed_two, norm_two_back = jax.vjp(layer_norm, hidden_mid, mlp_gain)
    mlp_rows = normed_two.astype(jnp.bfloat16)
    raised = jnp.dot(mlp_rows, full_fc1, preferred_element_type=jnp.float32)
    lifted_value, gelu_back = jax.vjp(jax.nn.gelu, raised)
    lifted = lifted_value.astype(jnp.bfloat16)
    lowered = jnp.dot(lifted, full_fc2, preferred_element_type=jnp.float32)
    result = (hidden_mid + lowered)[None].astype(jnp.bfloat16)
    grad_out = cotangent[0].astype(jnp.float32)
    grad_out_low = grad_out.astype(jnp.bfloat16)
    grad_fc2_w = summed_gradient(lifted, grad_out_low, tuned, False)
    grad_lifted = jnp.dot(grad_out_low, full_fc2.T, preferred_element_type=jnp.float32)
    grad_raised = gelu_back(grad_lifted)[0].astype(jnp.bfloat16)
    grad_fc1_w = summed_gradient(mlp_rows, grad_raised, tuned, False)
    grad_normed_two = jnp.dot(grad_raised, full_fc1.T, preferred_element_type=jnp.float32)
    grad_mid_norm, grad_mlp_gain = norm_two_back(grad_normed_two)
    grad_mid = grad_out + grad_mid_norm
    grad_attended = grad_mid.astype(jnp.bfloat16)
    grad_out_w = summed_gradient(attn_mixed, grad_attended, tuned, False)
    grad_mixed = jnp.dot(grad_attended, full_out.T, preferred_element_type=jnp.float32)
    grad_mixed = grad_mixed.astype(jnp.bfloat16).reshape(tokens, head_count, HEAD_DIM)
    grad_probs = jnp.einsum("thd,shd->hts", grad_mixed, values, preferred_element_type=jnp.float32)
    grad_values = jnp.einsum(
        "hts,thd->shd", probs_low, grad_mixed, preferred_element_type=jnp.float32
    )
    grad_scores = probs * (grad_probs - jnp.sum(grad_probs * probs, axis=-1, keepdims=True))
    grad_scores = grad_scores.astype(jnp.bfloat16)
    grad_queries = (
        jnp.einsum("hts,shd->thd", grad_scores, key_rows, preferred_element_type=jnp.float32)
        * score_scale
    )
    grad_keys = (
        jnp.einsum("hts,thd->shd", grad_scores, queries, preferred_element_type=jnp.float32)
        * score_scale
    )
    grad_projected = jnp.concatenate(
        [
            grad_queries.reshape(tokens, model_width),
            grad_keys.reshape(tokens, model_width),
            grad_values.reshape(tokens, model_width),
        ],
        axis=1,
    ).astype(jnp.bfloat16)
    grad_qkv_w = summed_gradient(attn_rows, grad_projected, tuned, False)
    grad_normed_one = jnp.dot(grad_projected, full_qkv.T, preferred_element_type=jnp.float32)
    grad_in_norm, grad_attn_gain = norm_one_back(grad_normed_one)
    grad_in = grad_mid + grad_in_norm
    grad_merge = jnp.sum(grad_in * spread_rows, axis=0) * (1.0 - gate_factor * gate_factor)
    grad_spread = (grad_in * gate_factor).reshape(1, grid_side, grid_side, model_width)
    grad_adapted, grad_adapter_taps = adapter_back(grad_spread)
    grad_adapted_low = grad_adapted.reshape(tokens, model_width).astype(jnp.bfloat16)
    grad_adapter_w = summed_gradient(features, grad_adapted_low, tuned, False)
    grad_features = jnp.dot(grad_adapted_low, full_adapter.T, preferred_element_type=jnp.float32)
    grad_pieces = grad_features.astype(jnp.bfloat16).reshape(path_count, quarter_rows, channels)
    grad_routed = lax.all_to_all(grad_pieces, "path", split_axis=0, concat_axis=0, tiled=True)
    grad_unrouted = jnp.einsum("pq,ptc->qtc", selector, grad_routed.astype(jnp.float32)).astype(
        jnp.bfloat16
    )
    grad_home = lax.all_to_all(grad_unrouted, "path", split_axis=0, concat_axis=0, tiled=True)
    grad_pooled = grad_home.astype(jnp.float32).reshape(tokens, channels)
    quarter = (grad_pooled * 0.25).reshape(1, grid_side, 1, grid_side, 1, channels)
    grad_section_out = jnp.broadcast_to(quarter, (1, grid_side, 2, grid_side, 2, channels)).reshape(
        maps_float.shape
    )
    grad_scale = jnp.sum((grad_section_out * reduced).reshape(-1, channels), axis=0)
    grad_reduced = (grad_section_out * layer_scale).reshape(-1, channels).astype(jnp.bfloat16)
    grad_reduce_w = summed_gradient(activated_low, grad_reduced, tuned, True)
    grad_activated = jnp.dot(grad_reduced, full_reduce.T, preferred_element_type=jnp.float32)
    grad_expanded = section_gelu_back(grad_activated)[0].astype(jnp.bfloat16)
    grad_expand_w = summed_gradient(section_rows, grad_expanded, tuned, True)
    grad_section_normed = jnp.dot(
        grad_expanded, full_expand.T, preferred_element_type=jnp.float32
    ).reshape(maps_float.shape)
    grad_section_mixed, grad_section_gain = section_norm_back(grad_section_normed)
    grad_maps_conv, grad_section_taps = section_back(grad_section_mixed)
    grad_maps = grad_section_out + grad_maps_conv
    summed = (
        grad_qkv_w,
        grad_out_w,
        grad_fc1_w,
        grad_fc2_w,
        grad_adapter_w,
        grad_expand_w,
        grad_reduce_w,
    )
    small_sums = lax.psum(
        (
            grad_attn_gain,
            grad_mlp_gain,
            grad_merge,
            grad_adapter_taps,
            grad_section_gain,
            grad_section_taps,
            grad_scale,
        ),
        ("path", "dev"),
    )
    return (
        result,
        grad_in[None],
        grad_maps,
        small_sums[0],
        summed[0],
        summed[1],
        small_sums[1],
        summed[2],
        summed[3],
        summed[4],
        small_sums[3],
        small_sums[2],
        small_sums[5],
        small_sums[4],
        summed[5],
        summed[6],
        small_sums[6],
    )


def solution(mesh):
    return jax.shard_map(
        local,
        mesh=mesh,
        in_specs=(
            P(("path", "dev"), None, None),
            P(("path", "dev"), None, None, None),
            P("path", "dev"),
            P(("path", "dev"), None, None),
            P(),
            P("dev", None),
            P("dev", None),
            P(),
            P("dev", None),
            P("dev", None),
            P("dev", None),
            P(),
            P(),
            P(),
            P(),
            P("dev", None),
            P("dev", None),
            P(),
        ),
        out_specs=(
            P(("path", "dev"), None, None),
            P(("path", "dev"), None, None),
            P(("path", "dev"), None, None, None),
            P(),
            P("dev", None),
            P("dev", None),
            P(),
            P("dev", None),
            P("dev", None),
            P("dev", None),
            P(),
            P(),
            P(),
            P(),
            P("dev", None),
            P("dev", None),
            P(),
        ),
        check_vma=False,
    )
```

```python
import functools

import jax
import jax.numpy as jnp
from jax import lax
from jax.experimental import pallas as pl
from jax.experimental.pallas import tpu as pltpu
from jax.sharding import PartitionSpec as P

HEAD_DIM = 64
MESH = pl.DeviceIdType.MESH
VMEM = pltpu.VMEM
SIDE, REACH, EDGE, GROUP, LANES = 7, 3, 8, 8, 128


def conv_rows(src, taps, group, flip, side):
    base = group * GROUP
    sums = [None] * GROUP
    for dc in range(SIDE):
        col = [taps((SIDE - 1 - dr) * SIDE + SIDE - 1 - dc if flip else dr * SIDE + dc) for dr in range(SIDE)]
        for j in range(GROUP + SIDE - 1):
            row = src[base + j, EDGE - REACH + dc : EDGE - REACH + dc + side, :]
            for r in range(GROUP):
                if 0 <= j - r < SIDE:
                    term = row * col[j - r]
                    sums[r] = term if sums[r] is None else sums[r] + term
    return sums


def clear_edges(pad, side):
    rows, columns, lanes = pad.shape[-3:]
    pad[:, :EDGE, :] = jnp.zeros((rows, EDGE, lanes), jnp.float32)
    pad[:, EDGE + side :, :] = jnp.zeros((rows, columns - EDGE - side, lanes), jnp.float32)
    pad[:REACH] = jnp.zeros((REACH, columns, lanes), jnp.float32)
    pad[REACH + side :] = jnp.zeros((rows - REACH - side, columns, lanes), jnp.float32)


def lane_block(block):
    return pl.ds(pl.multiple_of(block * LANES, LANES), LANES)


def mix_block(block, maps, taps, mixed, pad):
    side = maps.shape[0]
    at = lane_block(block)
    pad[REACH : REACH + side, EDGE : EDGE + side, :] = maps[:, :, at].astype(jnp.float32)

    def rows(group, carry):
        sums = conv_rows(pad, lambda t: taps[pl.ds(t, 1), at], group, False, side)
        for r in range(GROUP):
            mixed[group * GROUP + r, :, at] = sums[r]
        return carry

    lax.fori_loop(0, side // GROUP, rows, 0)


def norm_rows(h, mixed, gain, rows):
    v = mixed[h]
    centred = v - jnp.mean(v, axis=-1, keepdims=True)
    scale = lax.rsqrt(jnp.mean(centred * centred, axis=-1, keepdims=True) + 1e-06)
    rows[h] = (centred * scale * gain[...]).astype(jnp.bfloat16)


def section_forward_kernel(maps, taps, gain, mixed, rows, pad):
    side, _, channels = maps.shape
    clear_edges(pad, side)

    def blocks(block, carry):
        mix_block(block, maps, taps, mixed, pad)
        return carry

    lax.fori_loop(0, channels // LANES, blocks, 0)

    def norm(h, carry):
        norm_rows(h, mixed, gain, rows)
        return carry

    lax.fori_loop(0, side, norm, 0)


def gather_jobs(shapes):
    jobs = []
    for w, (r, n) in enumerate(shapes):
        q = r // 4
        size = q * n
        parts = max(1, round(size / (16 * 6144)))
        while parts > 1 and (n // 2) % (parts * 128): parts -= 1
        for k in range(parts):
            jobs.append((w, q, k * (n // parts), n // parts))
    return jobs

def gather_kernel(jobs, count, *refs):
    shards = refs[:count]
    maps, taps, gain = refs[count : count + 3]
    fulls = refs[count + 3 : 2 * count + 3]
    mixed, rows_out, pad, zs, zr, ps, pr, cs, cr, ls = refs[2 * count + 3 :]
    p = lax.axis_index("path"); d = lax.axis_index("dev")
    masks = [(0,1),(0,2),(0,4),(0,6),(1,0),(2,0)]
    def at(m): return (p ^ m[0], d ^ m[1])
    bar = pltpu.get_barrier_semaphore()
    for m in masks: pl.semaphore_signal(bar, inc=1, device_id=at(m), device_id_type=MESH)
    pl.semaphore_wait(bar, len(masks))
    def rows(w, owner):
        r = shards[w].shape[0]; return r, owner * r
    def copy(src, dst, ss, rs, m):
        return pltpu.make_async_remote_copy(src, dst, ss, rs, device_id=at(m), device_id_type=MESH)
    def quarter(w, owner, q, nq, c0, nc):
        r = shards[w].shape[0]
        return fulls[w].at[pl.ds(pl.multiple_of(owner * r + q * nq, 16), nq), pl.ds(c0, nc)]
    own = []
    for w in range(count):
        r = shards[w].shape[0]
        place = fulls[w].at[pl.ds(pl.multiple_of(d * r, 16), r)]
        a = pltpu.make_async_copy(shards[w], place, ls.at[w]); a.start()
        b = copy(shards[w], place, cs.at[w, 0], cr.at[w, 0], (0,1)); b.start()
        own.append((a, b))
    J = len(jobs)
    def Z(i, k):
        w, nq, c0, nc = jobs[i]
        return copy(shards[w].at[pl.ds(pl.multiple_of(p * nq, 16), nq), pl.ds(c0, nc)], quarter(w, d, p, nq, c0, nc), zs.at[i,k], zr.at[i,k], (0, 2*(k+1)))
    def XY(i, k, axis):
        w, nq, c0, nc = jobs[i]
        ref = quarter(w, d ^ (2*(k+1)), p, nq, c0, nc)
        return copy(ref, ref, ps.at[i,k,axis], pr.at[i,k,axis], (1+axis, 0))
    def DG(i, k, axis):
        w, nq, c0, nc = jobs[i]
        h = nc // 2
        ref = quarter(w, d ^ (2*(k+1)), p ^ (2 - axis), nq, c0 + axis * h, h)
        return copy(ref, ref, ps.at[i,k,2+axis], pr.at[i,k,2+axis], (1+axis, 0))
    def S(w, k):
        r = shards[w].shape[0]
        ref = fulls[w].at[pl.ds(pl.multiple_of((d ^ (2*(k+1))) * r, 16), r)]
        return copy(ref, ref, cs.at[w,1+k], cr.at[w,1+k], (0,1))
    last = {}
    for i,(w,*_) in enumerate(jobs): last[w] = i
    AHEAD = 3
    for i in range(min(AHEAD, J)):
        for k in range(3): Z(i,k).start()
    section_forward_kernel(maps, taps, gain, mixed, rows_out, pad)
    sent = []
    for i in range(J + 2):
        if i < J:
            for k in range(3):
                Z(i,k).wait_recv()
                XY(i,k,0).start(); XY(i,k,1).start()
            if i + AHEAD < J:
                for k in range(3): Z(i+AHEAD,k).start()
        if 0 <= i-1 < J:
            for k in range(3):
                XY(i-1,k,0).wait_recv(); DG(i-1,k,1).start()
                XY(i-1,k,1).wait_recv(); DG(i-1,k,0).start()
        if 0 <= i-2 < J:
            for k in range(3):
                DG(i-2,k,0).wait_recv(); DG(i-2,k,1).wait_recv()
            w = jobs[i-2][0]
            if last[w] == i-2:
                for k in range(3): S(w,k).start()
    for w in range(count):
        own[w][0].wait(); own[w][1].wait()
        for k in range(3): S(w,k).wait()
    for i in range(J):
        for k in range(3):
            Z(i,k).wait_send()
            for a in range(2): XY(i,k,a).wait_send(); DG(i,k,a).wait_send()

def gather_weights(shards, maps, taps, gain):
    shapes = [s.shape for s in shards]
    jobs = gather_jobs(shapes)
    n, J = len(shards), len(jobs)
    side, _, channels = maps.shape
    anyspec, whole = pl.BlockSpec(memory_space=pl.ANY), pl.BlockSpec(memory_space=VMEM)
    dma = pltpu.SemaphoreType.DMA
    results = pl.pallas_call(
        functools.partial(gather_kernel, jobs, n),
        out_shape=[jax.ShapeDtypeStruct((8 * r, c), jnp.bfloat16) for r, c in shapes]
        + [jax.ShapeDtypeStruct(maps.shape, jnp.float32), jax.ShapeDtypeStruct(maps.shape, jnp.bfloat16)],
        in_specs=[anyspec] * n + [whole] * 3,
        out_specs=[anyspec] * n + [whole] * 2,
        scratch_shapes=[VMEM((side + 2 * REACH, side + 2 * EDGE, LANES), jnp.float32)]
        + [dma((J, 3)), dma((J, 3)), dma((J, 3, 4)), dma((J, 3, 4)), dma((n, 4)), dma((n, 4)), dma((n,))],
        compiler_params=pltpu.CompilerParams(
            collective_id=0, has_side_effects=True, vmem_limit_bytes=40 * 2**20
        ),
    )(*shards, maps, taps, gain.reshape(1, channels))
    return results[:n], results[n], results[n + 1]


def add_block(total, term):
    return (total.astype(jnp.float32) + term.astype(jnp.float32)).astype(jnp.bfloat16)


def scatter_kernel(
    big0, big1, t0, t1, t2, t3, small_in, grad_normed, mixed, maps, taps, gain,
    grad_maps, small_out, o0, o1, o2, o3, o4, o5, land0a, land0b, land1a, land1b,
    acc0a, acc0b, acc1a, acc1b, two0a, two0b, two1a, two1b, tmp0, tmp1,
    own0, own1, own2, own3, two0, two1, two2, two3,
    zr0, zr1, zr2, zr3, zr4, zr5, low0, low1, low2, low3, low4, low5,
    full0, full1, full2, full3, full4, full5,
    small_at, small_from, pad, grad_pad, tap_sums, ssem, rsem, lsem,
):
    p, d = lax.axis_index("path"), lax.axis_index("dev")
    up, across, height, side = p // 2, lax.rem(p, 2), d // 2, lax.rem(d, 2)
    masks = [(0, 1), (0, 2), (0, 4), (0, 6), (1, 0), (2, 0), (3, 0)]
    bar = pltpu.get_barrier_semaphore()
    for m in masks:
        pl.semaphore_signal(bar, inc=1, device_id=(p ^ m[0], d ^ m[1]), device_id_type=MESH)
    pl.semaphore_wait(bar, len(masks))

    copies = []

    def send(src, dst, m):
        n = len(copies)
        copy = pltpu.make_async_remote_copy(
            src, dst, ssem.at[n], rsem.at[n], device_id=(p ^ m[0], d ^ m[1]), device_id_type=MESH
        )
        copies.append(copy)
        copy.start()
        return copy

    local = []

    def fetch(src, dst):
        copy = pltpu.make_async_copy(src, dst, lsem.at[len(local)])
        local.append(copy)
        copy.start()
        return copy

    thin = [(t0, own0, two0, True), (t1, own1, two1, False), (t2, own2, two2, True), (t3, own3, two3, False)]
    wide = [
        (big0, (acc0a, acc0b), (land0a, land0b), (two0a, two0b), tmp0),
        (big1, (acc1a, acc1b), (land1a, land1b), (two1a, two1b), tmp1),
    ]
    outs = [o0, o1, o2, o3, o4, o5]
    zrs, lows, wholes = [zr0, zr1, zr2, zr3, zr4, zr5], [low0, low1, low2, low3, low4, low5], [full0, full1, full2, full3, full4, full5]

    def thin_two(i):
        src, own, two, upward = thin[i]
        index, mask = (up, (2, 0)) if upward else (across, (1, 0))
        loaded = fetch(src.at[:, :, index], own)
        return loaded, send(src.at[:, :, 1 - index], two, mask)

    def wide_one(w):
        src, acc, land, _, _ = wide[w]
        half = src.shape[5] // 2
        a, b = pl.ds(0, half), pl.ds(half, half)
        return (
            fetch(src.at[:, :, :, across, :, a], acc[0]),
            fetch(src.at[:, :, up, :, :, b], acc[1]),
            send(src.at[:, :, :, 1 - across, :, a], land[0], (1, 0)),
            send(src.at[:, :, 1 - up, :, :, b], land[1], (2, 0)),
        )

    def wide_two(w, started):
        src, acc, land, two, tmp = wide[w]
        started[0].wait()
        started[1].wait()
        sent = []
        for k in range(2):
            started[2 + k].wait_recv()
            loads = [fetch(land[k].at[0], tmp.at[0])]
            for z in range(4):
                if z < 3:
                    loads.append(fetch(land[k].at[z + 1], tmp.at[(z + 1) % 2]))
                loads[z].wait()
                for c in range(2):
                    for q in range(2):
                        acc[k][z, c, q] = add_block(acc[k][z, c, q], tmp[z % 2, c, q])
            index, mask = (up, (2, 0)) if k == 0 else (across, (1, 0))
            sent.append(send(acc[k].at[:, :, 1 - index], two[k], mask))
        return sent

    def heights(n, parts):
        zr = zrs[n]
        half = zr.shape[3] // len(parts)
        return [
            send(part.at[height ^ m], zr.at[m - 1, :, :, pl.ds(k * half, half)], (0, 2 * m))
            for m in (1, 2, 3)
            for k, part in enumerate(parts)
        ]

    def thin_three(i, started):
        _, own, two, _ = thin[i]
        started[0].wait()
        started[1].wait_recv()
        for z in range(4):
            for c in range(2):
                two[z, c] = add_block(two[z, c], own[z, c])
        return heights(i, [two])

    def wide_three(w, sent):
        _, acc, _, two, _ = wide[w]
        for k in range(2):
            index = up if k == 0 else across
            sent[k].wait_recv()
            for z in range(4):
                for c in range(2):
                    two[k][z, c] = add_block(two[k][z, c], acc[k][z, c, index])
        return heights(4 + w, two)

    def total(n, parts, sent):
        for copy in sent:
            copy.wait_recv()
        zr, low, whole = zrs[n], lows[n], wholes[n]
        half = zr.shape[3] // len(parts)
        for k, part in enumerate(parts):
            cols = slice(k * half, (k + 1) * half)
            for c in range(2):
                value = part[height, c].astype(jnp.float32)
                for m in range(3):
                    value = value + zr[m, c, :, cols].astype(jnp.float32)
                low[c, :, cols] = value.astype(jnp.bfloat16)
        whole[side] = low[side]
        return send(low.at[1 - side], whole.at[side], (0, 1))

    def spread(n, swapped):
        swapped.wait_recv()
        return [fetch(wholes[n], outs[n].at[p])] + [send(wholes[n], outs[n].at[p], (m, 0)) for m in (1, 2, 3)]

    side_cells, _, channels = maps.shape
    count = channels // LANES

    def norm_back():
        clear_edges(pad, side_cells)
        clear_edges(grad_pad, side_cells)
        small_at[0] = small_in[...]

        def norm(h, carry):
            v = mixed[h]
            centred = v - jnp.mean(v, axis=-1, keepdims=True)
            scale = lax.rsqrt(jnp.mean(centred * centred, axis=-1, keepdims=True) + 1e-06)
            unit = centred * scale
            grad = grad_normed[h]
            small_at[0, SIDE * SIDE : SIDE * SIDE + 1, :] += jnp.sum(grad * unit, axis=0, keepdims=True)
            grad = grad * gain[...]
            grad_maps[h] = scale * (
                grad - jnp.mean(grad, axis=-1, keepdims=True) - unit * jnp.mean(grad * unit, axis=-1, keepdims=True)
            )
            return carry

        lax.fori_loop(0, side_cells, norm, 0)

    def blocks(first, last):
        def one(block, carry):
            at = lane_block(block)
            inside = (slice(REACH, REACH + side_cells), slice(EDGE, EDGE + side_cells), slice(None))
            pad[inside] = maps[:, :, at].astype(jnp.float32)
            grad_pad[inside] = grad_maps[:, :, at]
            tap_sums[...] = jnp.zeros_like(tap_sums)

            def rows(group, inner):
                base = group * GROUP
                sums = conv_rows(grad_pad, lambda t: taps[pl.ds(t, 1), at], group, True, side_cells)
                for r in range(GROUP):
                    grad_maps[base + r, :, at] = sums[r]
                for dc in range(SIDE):
                    grads = [grad_pad[base + REACH + r, EDGE : EDGE + side_cells, :] for r in range(GROUP)]
                    acc = [None] * SIDE
                    for j in range(GROUP + SIDE - 1):
                        row = pad[base + j, EDGE - REACH + dc : EDGE - REACH + dc + side_cells, :]
                        for r in range(GROUP):
                            dr = j - r
                            if 0 <= dr < SIDE:
                                term = row * grads[r]
                                acc[dr] = term if acc[dr] is None else acc[dr] + term
                    for dr in range(SIDE):
                        tap_sums[dr * SIDE + dc] += jnp.sum(acc[dr].reshape(side_cells // 8, 8, LANES), axis=0)
                return inner

            lax.fori_loop(0, side_cells // GROUP, rows, 0)
            small_at[0, : SIDE * SIDE, at] = jnp.sum(tap_sums[...], axis=1)
            return carry

        lax.fori_loop(first, last, one, 0)

    small_masks = [(0, 1), (1, 0), (2, 0), (0, 2), (0, 4)]

    def small_send(s):
        return send(small_at.at[s], small_from.at[s], small_masks[s])

    def small_step(s, copy):
        copy.wait_recv()
        value = small_at[s] + small_from[s]
        if s + 1 < len(small_masks):
            small_at[s + 1] = value
            return small_send(s + 1)
        small_out[...] = value

    thin_sent = [thin_two(i) for i in range(4)]
    one_reduce = wide_one(0)
    norm_back()
    blocks(0, count // 2)
    thin_high = [thin_three(0, thin_sent[0]), thin_three(1, thin_sent[1])]
    one_expand = wide_one(1)
    blocks(count // 2, 3 * count // 4)
    thin_high += [thin_three(2, thin_sent[2]), thin_three(3, thin_sent[3])]
    blocks(3 * count // 4, count)
    small = small_send(0)
    two_reduce = wide_two(0, one_reduce)
    small = small_step(0, small)
    swaps = [total(i, [thin[i][2]], thin_high[i]) for i in range(2)]
    small = small_step(1, small)
    high_reduce = wide_three(0, two_reduce)
    two_expand = wide_two(1, one_expand)
    small = small_step(2, small)
    swaps += [total(i, [thin[i][2]], thin_high[i]) for i in (2, 3)]
    last = [spread(i, swaps[i]) for i in range(4)]
    high_expand = wide_three(1, two_expand)
    small = small_step(3, small)
    swap_reduce = total(4, wide[0][3], high_reduce)
    last.append(spread(4, swap_reduce))
    small = small_step(4, small)
    swap_expand = total(5, wide[1][3], high_expand)
    last.append(spread(5, swap_expand))
    for group in last:
        group[0].wait()
        for copy in group[1:]:
            copy.wait_recv()
    for copy in copies:
        copy.wait_send()


def scatter_gradients(part_reduce, part_expand, thins, small, grad_normed, mixed, maps, taps, gain):
    side, _, channels = maps.shape
    low, full = jnp.bfloat16, jnp.float32
    anyspec, whole = pl.BlockSpec(memory_space=pl.ANY), pl.BlockSpec(memory_space=VMEM)
    dma = pltpu.SemaphoreType.DMA
    finals = [(t.shape[3], t.shape[4]) for t in thins] + [w.shape[4:] for w in (part_reduce, part_expand)]
    landing = []
    scratch = []
    for w in (part_reduce, part_expand):
        shape = w.shape[:3] + (w.shape[4], w.shape[5] // 2)
        landing += [jax.ShapeDtypeStruct(shape, low)] * 2
        scratch += [VMEM(shape, low)] * 2
    scratch += [VMEM(w.shape[:2] + (w.shape[4], w.shape[5] // 2), low) for w in (part_reduce, part_expand) for _ in range(2)]
    scratch += [VMEM((2, 2, 2, w.shape[4], w.shape[5] // 2), low) for w in (part_reduce, part_expand)]
    scratch += [VMEM(t.shape[:2] + t.shape[3:], low) for t in thins] * 2
    scratch += [VMEM((3, 2) + f, low) for f in finals]
    scratch += [VMEM((2,) + f, low) for f in finals] * 2
    edge = (side + 2 * REACH, side + 2 * EDGE, LANES)
    scratch += [VMEM((5,) + small.shape, full)] * 2
    scratch += [VMEM(edge, full)] * 2 + [VMEM((SIDE * SIDE, 8, LANES), full)]
    scratch += [dma((80,)), dma((80,)), dma((40,))]
    results = pl.pallas_call(
        scatter_kernel,
        out_shape=[jax.ShapeDtypeStruct(maps.shape, full), jax.ShapeDtypeStruct(small.shape, full)]
        + [jax.ShapeDtypeStruct((4, 2) + f, low) for f in finals]
        + landing,
        in_specs=[anyspec] * 6 + [whole] * 6,
        out_specs=[whole] * 2 + [anyspec] * 10,
        scratch_shapes=scratch,
        compiler_params=pltpu.CompilerParams(
            collective_id=1, has_side_effects=True, vmem_limit_bytes=60 * 2**20
        ),
    )(part_reduce, part_expand, *thins, small, grad_normed, mixed, maps, taps, gain.reshape(1, channels))
    return results[0], results[1], results[2:8]


def layer_norm(values, gain_vec):
    centred = values - jnp.mean(values, axis=-1, keepdims=True)
    spread = jnp.mean(centred * centred, axis=-1, keepdims=True)
    return centred * lax.rsqrt(spread + 1e-06) * gain_vec


def depthwise(feature_map, taps_table, kernel_side):
    half_side = kernel_side // 2
    padded = jnp.pad(feature_map, ((0, 0), (half_side, half_side), (half_side, half_side), (0, 0)))
    map_side = feature_map.shape[1]
    accum_sum = jnp.zeros(feature_map.shape, feature_map.dtype)
    for offset_row in range(kernel_side):
        for offset_col in range(kernel_side):
            window = padded[
                :, offset_row : offset_row + map_side, offset_col : offset_col + map_side, :
            ]
            accum_sum = accum_sum + window * taps_table[offset_row * kernel_side + offset_col]
    return accum_sum


def section_depthwise(grid_field, grid_kernel):
    return depthwise(grid_field, grid_kernel, 7)


def adapter_depthwise(grid_field, grid_kernel):
    return depthwise(grid_field, grid_kernel, 3)


def swap(value, axis, mask):
    size = lax.axis_size(axis)
    return lax.ppermute(value, axis, [(i, i ^ mask) for i in range(size)])


def pick(value, index, axis):
    return lax.dynamic_index_in_dim(value, index, axis, keepdims=False)


def add_low(left, right):
    return (left.astype(jnp.float32) + right.astype(jnp.float32)).astype(jnp.bfloat16)


def place():
    path, dev = lax.axis_index("path"), lax.axis_index("dev")
    return path, path // 2, lax.rem(path, 2), dev // 2, lax.rem(dev, 2)


def both_images(rows):
    return jnp.concatenate([rows, swap(rows, "dev", 1)])


def pair_gradient(rows, grads):
    side = place()[4]
    half = grads.shape[1] // 2
    low, high = grads[:, :half], grads[:, half:]
    mine = jnp.where(side == 0, low, high)
    theirs = swap(jnp.where(side == 0, high, low), "dev", 1)
    product = lax.dot_general(
        rows, jnp.concatenate([mine, theirs]), (((0,), (0,)), ((), ())), preferred_element_type=jnp.float32
    )
    return product.astype(jnp.bfloat16).reshape(4, 2, 2, 2, rows.shape[1] // 32, half)


def across_sum(share, axis):
    across = place()[2]
    return add_low(pick(share, across, axis), swap(pick(share, 1 - across, axis), "path", 1))


def up_sum(share, axis):
    up = place()[1]
    return add_low(pick(share, up, axis), swap(pick(share, 1 - up, axis), "path", 2))


def tie(*values):
    return lax.optimization_barrier(values)


def finish(pieces):
    parts, _, rows, half = pieces.shape
    return jnp.moveaxis(pieces, 1, 2).reshape(parts * rows, 2 * half).astype(jnp.float32)


def plain_sum(rows, grads):
    product = lax.dot_general(
        rows, grads, (((0,), (0,)), ((), ())), preferred_element_type=jnp.float32
    ).astype(jnp.bfloat16)
    share = lax.psum_scatter(product, "dev", scatter_dimension=0, tiled=True)
    return lax.psum(share, "path").astype(jnp.float32)


def local(
    inputs,
    hires_maps,
    target_path,
    cotangent,
    attn_gain,
    w_qkv,
    w_out,
    mlp_gain,
    w_fc1,
    w_fc2,
    w_adapter,
    adapter_kernel,
    merge_gate,
    section_kernel,
    section_gain,
    w_expand,
    w_reduce,
    layer_scale,
):
    tuned = lax.axis_size("path") == 4 and lax.axis_size("dev") == 8
    weights = (w_expand, w_reduce, w_adapter, w_qkv, w_out, w_fc1, w_fc2)
    if tuned:
        fulls, section_mixed, section_normed = gather_weights(
            weights, hires_maps[0], section_kernel, section_gain
        )
    else:
        fulls = [lax.all_gather(shard, "dev", axis=0, tiled=True) for shard in weights]
    full_expand, full_reduce, full_adapter, full_qkv, full_out, full_fc1, full_fc2 = fulls
    path_count = lax.axis_size("path")
    maps_float = hires_maps.astype(jnp.float32)
    map_side = maps_float.shape[1]
    channels = maps_float.shape[3]
    grid_side = map_side // 2
    tokens = grid_side * grid_side
    quarter_rows = tokens // path_count
    model_width = inputs.shape[2]
    head_count = model_width // HEAD_DIM
    score_scale = HEAD_DIM ** (-0.5)
    if not tuned:
        section_mixed, section_back = jax.vjp(section_depthwise, maps_float, section_kernel)
        section_normed, section_norm_back = jax.vjp(layer_norm, section_mixed, section_gain)
    section_rows = section_normed.reshape(-1, channels).astype(jnp.bfloat16)
    expanded = jnp.dot(section_rows, full_expand, preferred_element_type=jnp.float32)
    activated, section_gelu_back = jax.vjp(jax.nn.gelu, expanded)
    activated_low = activated.astype(jnp.bfloat16)
    reduced = jnp.dot(activated_low, full_reduce, preferred_element_type=jnp.float32).reshape(
        maps_float.shape
    )
    section_out = maps_float + layer_scale * reduced
    pooled = jnp.mean(
        section_out.reshape(grid_side, 2, grid_side, 2, channels), axis=(1, 3)
    ).reshape(tokens, channels)
    pieces = pooled.astype(jnp.bfloat16).reshape(path_count, quarter_rows, channels)
    own_target = jnp.broadcast_to(target_path, (path_count, 1))
    spread_pieces, spread_targets = (
        lax.all_to_all(pieces, "path", split_axis=0, concat_axis=0, tiled=True),
        lax.all_to_all(own_target, "path", split_axis=0, concat_axis=0, tiled=True),
    )
    selector = (
        jnp.arange(path_count, dtype=jnp.int32)[:, None] == spread_targets.reshape(1, path_count)
    ).astype(jnp.float32)
    routed = jnp.einsum("pq,qtc->ptc", selector, spread_pieces.astype(jnp.float32)).astype(
        jnp.bfloat16
    )
    arrived = lax.all_to_all(routed, "path", split_axis=0, concat_axis=0, tiled=True)
    features = arrived.reshape(tokens, channels)
    adapted = jnp.dot(features, full_adapter, preferred_element_type=jnp.float32)
    spread_map, adapter_back = jax.vjp(
        adapter_depthwise, adapted.reshape(1, grid_side, grid_side, model_width), adapter_kernel
    )
    spread_rows = spread_map.reshape(tokens, model_width)
    gate_factor = jnp.tanh(merge_gate)
    hidden_in = inputs[0].astype(jnp.float32) + gate_factor * spread_rows
    normed_one, norm_one_back = jax.vjp(layer_norm, hidden_in, attn_gain)
    attn_rows = normed_one.astype(jnp.bfloat16)
    projected = jnp.dot(attn_rows, full_qkv, preferred_element_type=jnp.float32).astype(
        jnp.bfloat16
    )
    queries = projected[:, :model_width].reshape(tokens, head_count, HEAD_DIM)
    key_rows = projected[:, model_width : 2 * model_width].reshape(tokens, head_count, HEAD_DIM)
    values = projected[:, 2 * model_width :].reshape(tokens, head_count, HEAD_DIM)
    scores = (
        jnp.einsum("thd,shd->hts", queries, key_rows, preferred_element_type=jnp.float32)
        * score_scale
    )
    probs = jax.nn.softmax(scores, axis=-1)
    probs_low = probs.astype(jnp.bfloat16)
    attn_mixed = jnp.einsum("hts,shd->thd", probs_low, values, preferred_element_type=jnp.float32)
    attn_mixed = attn_mixed.astype(jnp.bfloat16).reshape(tokens, model_width)
    attended = jnp.dot(attn_mixed, full_out, preferred_element_type=jnp.float32)
    hidden_mid = hidden_in + attended
    normed_two, norm_two_back = jax.vjp(layer_norm, hidden_mid, mlp_gain)
    mlp_rows = normed_two.astype(jnp.bfloat16)
    raised = jnp.dot(mlp_rows, full_fc1, preferred_element_type=jnp.float32)
    lifted_value, gelu_back = jax.vjp(jax.nn.gelu, raised)
    lifted = lifted_value.astype(jnp.bfloat16)
    lowered = jnp.dot(lifted, full_fc2, preferred_element_type=jnp.float32)
    result = (hidden_mid + lowered)[None].astype(jnp.bfloat16)
    grad_out = cotangent[0].astype(jnp.float32)
    grad_out_low = grad_out.astype(jnp.bfloat16)
    if tuned:
        part_fc2 = pair_gradient(both_images(lifted), grad_out_low)
    else:
        grad_fc2_w = plain_sum(lifted, grad_out_low)
    grad_lifted = jnp.dot(grad_out_low, full_fc2.T, preferred_element_type=jnp.float32)
    grad_raised = gelu_back(grad_lifted)[0].astype(jnp.bfloat16)
    if tuned:
        part_fc1 = pair_gradient(both_images(mlp_rows), grad_raised)
    else:
        grad_fc1_w = plain_sum(mlp_rows, grad_raised)
    grad_normed_two = jnp.dot(grad_raised, full_fc1.T, preferred_element_type=jnp.float32)
    grad_mid_norm, grad_mlp_gain = norm_two_back(grad_normed_two)
    grad_mid = grad_out + grad_mid_norm
    grad_attended = grad_mid.astype(jnp.bfloat16)
    if tuned:
        part_out = pair_gradient(both_images(attn_mixed), grad_attended)
    else:
        grad_out_w = plain_sum(attn_mixed, grad_attended)
    grad_mixed = jnp.dot(grad_attended, full_out.T, preferred_element_type=jnp.float32)
    grad_mixed = grad_mixed.astype(jnp.bfloat16).reshape(tokens, head_count, HEAD_DIM)
    grad_probs = jnp.einsum("thd,shd->hts", grad_mixed, values, preferred_element_type=jnp.float32)
    grad_values = jnp.einsum(
        "hts,thd->shd", probs_low, grad_mixed, preferred_element_type=jnp.float32
    )
    grad_scores = probs * (grad_probs - jnp.sum(grad_probs * probs, axis=-1, keepdims=True))
    grad_scores = grad_scores.astype(jnp.bfloat16)
    grad_queries = (
        jnp.einsum("hts,shd->thd", grad_scores, key_rows, preferred_element_type=jnp.float32)
        * score_scale
    )
    grad_keys = (
        jnp.einsum("hts,thd->shd", grad_scores, queries, preferred_element_type=jnp.float32)
        * score_scale
    )
    grad_projected = jnp.concatenate(
        [
            grad_queries.reshape(tokens, model_width),
            grad_keys.reshape(tokens, model_width),
            grad_values.reshape(tokens, model_width),
        ],
        axis=1,
    ).astype(jnp.bfloat16)
    if tuned:
        part_qkv = pair_gradient(both_images(attn_rows), grad_projected)
    else:
        grad_qkv_w = plain_sum(attn_rows, grad_projected)
    grad_normed_one = jnp.dot(grad_projected, full_qkv.T, preferred_element_type=jnp.float32)
    grad_in_norm, grad_attn_gain = norm_one_back(grad_normed_one)
    grad_in = grad_mid + grad_in_norm
    grad_merge = jnp.sum(grad_in * spread_rows, axis=0) * (1.0 - gate_factor * gate_factor)
    grad_spread = (grad_in * gate_factor).reshape(1, grid_side, grid_side, model_width)
    grad_adapted, grad_adapter_taps = adapter_back(grad_spread)
    grad_adapted_low = grad_adapted.reshape(tokens, model_width).astype(jnp.bfloat16)
    if tuned:
        part_adapter = pair_gradient(both_images(features), grad_adapted_low)
    else:
        grad_adapter_w = plain_sum(features, grad_adapted_low)
    grad_features = jnp.dot(grad_adapted_low, full_adapter.T, preferred_element_type=jnp.float32)
    grad_pieces = grad_features.astype(jnp.bfloat16).reshape(path_count, quarter_rows, channels)
    grad_routed = lax.all_to_all(grad_pieces, "path", split_axis=0, concat_axis=0, tiled=True)
    grad_unrouted = jnp.einsum("pq,ptc->qtc", selector, grad_routed.astype(jnp.float32)).astype(
        jnp.bfloat16
    )
    grad_home = lax.all_to_all(grad_unrouted, "path", split_axis=0, concat_axis=0, tiled=True)
    if tuned:
        step_fc2, step_fc1 = across_sum(part_fc2, 3), up_sum(part_fc1, 2)
        step_qkv = across_sum(part_qkv, 3)
        step_rest = up_sum(jnp.concatenate([part_out, part_adapter], axis=4), 2)
    grad_pooled = grad_home.astype(jnp.float32).reshape(tokens, channels)
    quarter = (grad_pooled * 0.25).reshape(1, grid_side, 1, grid_side, 1, channels)
    grad_section_out = jnp.broadcast_to(quarter, (1, grid_side, 2, grid_side, 2, channels)).reshape(
        maps_float.shape
    )
    grad_scale = jnp.sum((grad_section_out * reduced).reshape(-1, channels), axis=0)
    grad_reduced = (grad_section_out * layer_scale).reshape(-1, channels).astype(jnp.bfloat16)
    if tuned:
        part_reduce = pair_gradient(both_images(activated_low), grad_reduced)
    else:
        grad_reduce_w = plain_sum(activated_low, grad_reduced)
    grad_activated = jnp.dot(grad_reduced, full_reduce.T, preferred_element_type=jnp.float32)
    grad_expanded = section_gelu_back(grad_activated)[0].astype(jnp.bfloat16)
    if tuned:
        grad_expanded, part_reduce, step_fc2, step_fc1 = tie(grad_expanded, part_reduce, step_fc2, step_fc1)
    if tuned:
        part_expand = pair_gradient(both_images(section_rows), grad_expanded)
    else:
        grad_expand_w = plain_sum(section_rows, grad_expanded)
    grad_section_normed = jnp.dot(
        grad_expanded, full_expand.T, preferred_element_type=jnp.float32
    ).reshape(maps_float.shape)
    if tuned:
        small_rows = jnp.concatenate(
            [
                jnp.zeros((section_kernel.shape[0] + 1, channels), jnp.float32),
                jnp.concatenate([grad_attn_gain, grad_mlp_gain, grad_merge, grad_adapter_taps.reshape(-1)]).reshape(-1, channels),
                grad_scale[None],
            ]
        )
        small_count = small_rows.shape[0]
        small_rows = jnp.pad(small_rows, ((0, -small_count % 8), (0, 0)))
        grad_maps, small_rows, pieces = scatter_gradients(
            part_reduce,
            part_expand,
            [step_fc2, step_fc1, step_qkv, step_rest],
            small_rows,
            grad_section_normed[0],
            section_mixed,
            hires_maps[0],
            section_kernel,
            section_gain,
        )
        grad_maps = grad_maps[None] + grad_section_out
        split = part_out.shape[4]
        grad_fc2_w, grad_fc1_w, grad_qkv_w = [finish(piece) for piece in pieces[:3]]
        grad_out_w, grad_adapter_w = finish(pieces[3][:, :, :split]), finish(pieces[3][:, :, split:])
        grad_reduce_w, grad_expand_w = finish(pieces[4]), finish(pieces[5])
    else:
        grad_section_mixed, grad_section_gain = section_norm_back(grad_section_normed)
        grad_maps_conv, grad_section_taps = section_back(grad_section_mixed)
        grad_maps = grad_section_out + grad_maps_conv
    summed = (
        grad_qkv_w,
        grad_out_w,
        grad_fc1_w,
        grad_fc2_w,
        grad_adapter_w,
        grad_expand_w,
        grad_reduce_w,
    )
    if tuned:
        tap_count = section_kernel.shape[0]
        flat = small_rows[tap_count + 1 : small_count - 1].reshape(-1)
        small_sums = (
            flat[:model_width],
            flat[model_width : 2 * model_width],
            flat[2 * model_width : 3 * model_width],
            flat[3 * model_width :].reshape(adapter_kernel.shape),
            small_rows[tap_count],
            small_rows[:tap_count],
            small_rows[small_count - 1],
        )
    else:
        small_sums = lax.psum(
            (
                grad_attn_gain,
                grad_mlp_gain,
                grad_merge,
                grad_adapter_taps,
                grad_section_gain,
                grad_section_taps,
                grad_scale,
            ),
            ("path", "dev"),
        )
    return (
        result,
        grad_in[None],
        grad_maps,
        small_sums[0],
        summed[0],
        summed[1],
        small_sums[1],
        summed[2],
        summed[3],
        summed[4],
        small_sums[3],
        small_sums[2],
        small_sums[5],
        small_sums[4],
        summed[5],
        summed[6],
        small_sums[6],
    )


def solution(mesh):
    return jax.shard_map(
        local,
        mesh=mesh,
        in_specs=(
            P(("path", "dev"), None, None),
            P(("path", "dev"), None, None, None),
            P("path", "dev"),
            P(("path", "dev"), None, None),
            P(),
            P("dev", None),
            P("dev", None),
            P(),
            P("dev", None),
            P("dev", None),
            P("dev", None),
            P(),
            P(),
            P(),
            P(),
            P("dev", None),
            P("dev", None),
            P(),
        ),
        out_specs=(
            P(("path", "dev"), None, None),
            P(("path", "dev"), None, None),
            P(("path", "dev"), None, None, None),
            P(),
            P("dev", None),
            P("dev", None),
            P(),
            P("dev", None),
            P("dev", None),
            P("dev", None),
            P(),
            P(),
            P(),
            P(),
            P("dev", None),
            P("dev", None),
            P(),
        ),
        check_vma=False,
    )
```

```python
import functools

import jax
import jax.numpy as jnp
from jax import lax
from jax.experimental import pallas as pl
from jax.experimental.pallas import tpu as pltpu
from jax.sharding import PartitionSpec as P

HEAD_DIM = 64
MESH = pl.DeviceIdType.MESH
VMEM = pltpu.VMEM
SIDE, REACH, EDGE, GROUP, LANES = 7, 3, 8, 8, 128


def conv_rows(src, taps, group, flip, side):
    base = group * GROUP
    sums = [None] * GROUP
    for dc in range(SIDE):
        col = [taps((SIDE - 1 - dr) * SIDE + SIDE - 1 - dc if flip else dr * SIDE + dc) for dr in range(SIDE)]
        for j in range(GROUP + SIDE - 1):
            row = src[base + j, EDGE - REACH + dc : EDGE - REACH + dc + side, :]
            for r in range(GROUP):
                if 0 <= j - r < SIDE:
                    term = row * col[j - r]
                    sums[r] = term if sums[r] is None else sums[r] + term
    return sums


def clear_edges(pad, side):
    rows, columns, lanes = pad.shape[-3:]
    pad[:, :EDGE, :] = jnp.zeros((rows, EDGE, lanes), jnp.float32)
    pad[:, EDGE + side :, :] = jnp.zeros((rows, columns - EDGE - side, lanes), jnp.float32)
    pad[:REACH] = jnp.zeros((REACH, columns, lanes), jnp.float32)
    pad[REACH + side :] = jnp.zeros((rows - REACH - side, columns, lanes), jnp.float32)


def lane_block(block):
    return pl.ds(pl.multiple_of(block * LANES, LANES), LANES)


def mix_block(block, maps, taps, mixed, pad):
    side = maps.shape[0]
    at = lane_block(block)
    pad[REACH : REACH + side, EDGE : EDGE + side, :] = maps[:, :, at].astype(jnp.float32)

    def rows(group, carry):
        sums = conv_rows(pad, lambda t: taps[pl.ds(t, 1), at], group, False, side)
        for r in range(GROUP):
            mixed[group * GROUP + r, :, at] = sums[r]
        return carry

    lax.fori_loop(0, side // GROUP, rows, 0)


def section_mix(maps, taps, gain, mixed, rows, pad):
    side, _, channels = maps.shape
    clear_edges(pad, side)

    def blocks(block, carry):
        mix_block(block, maps, taps, mixed, pad)
        return carry

    lax.fori_loop(0, channels // LANES, blocks, 0)

    def norm(pair, carry):
        v = mixed[pl.ds(2 * pair, 2)].reshape(2 * side, channels)
        centred = v - jnp.mean(v, axis=-1, keepdims=True)
        scale = lax.rsqrt(jnp.mean(centred * centred, axis=-1, keepdims=True) + 1e-06)
        at = pl.ds(pl.multiple_of(pair * 2 * side, 2 * side), 2 * side)
        rows[at, :] = (centred * scale * gain[...]).astype(jnp.bfloat16)
        return carry

    lax.fori_loop(0, side // 2, norm, 0)


STEP = 512


def product(left, right, total, left_at, right_at):
    total[...] = jnp.zeros_like(total)

    def step(k, carry):
        here = pl.multiple_of(k * STEP, STEP)
        total[...] += jnp.dot(
            left[:, pl.ds(left_at + here, STEP)],
            right[pl.ds(here, STEP), pl.ds(pl.multiple_of(right_at, STEP), STEP)],
            preferred_element_type=jnp.float32,
        )
        return carry

    lax.fori_loop(0, right.shape[0] // STEP, step, 0)


def gather_jobs(shapes):
    jobs = []
    for w, (r, n) in enumerate(shapes):
        parts = max(1, round(r // 4 * n / (16 * 6144)))
        while n % (parts * STEP):
            parts -= 1
        jobs += [(w, r // 4, k * (n // parts), n // parts) for k in range(parts)]
    return jobs


def gather_kernel(jobs, count, expand, reduce, *refs):
    shards = refs[:count]
    maps, taps, gain, scale, target = refs[count : count + 5]
    fulls = refs[count + 5 : 2 * count + 5]
    mixed, rows, targets, expanded, active, reduced, pooled = refs[2 * count + 5 : 2 * count + 12]
    pad, wide_w, deep_w, total, stage, pair_sum = refs[2 * count + 12 : 2 * count + 18]
    zs, zr, ps, pr, cs, cr, os, orr, ls, ts, tr, ws, es = refs[2 * count + 18 :]
    p, d = lax.axis_index("path"), lax.axis_index("dev")

    def at(m):
        return (p ^ m[0], d ^ m[1])

    masks = [(0, 1), (0, 2), (0, 4), (0, 6), (1, 0), (2, 0), (3, 0)]
    bar = pltpu.get_barrier_semaphore()
    for m in masks:
        pl.semaphore_signal(bar, inc=1, device_id=at(m), device_id_type=MESH)
    pl.semaphore_wait(bar, len(masks))

    def copy(src, dst, ss, rs, m):
        return pltpu.make_async_remote_copy(src, dst, ss, rs, device_id=at(m), device_id_type=MESH)

    def quarter(w, owner, q, nq, c0, nc):
        r = shards[w].shape[0]
        return fulls[w].at[pl.ds(pl.multiple_of(owner * r + q * nq, 16), nq), pl.ds(c0, nc)]

    J = len(jobs)

    def Z(i, k):
        w, nq, c0, nc = jobs[i]
        src = shards[w].at[pl.ds(pl.multiple_of(p * nq, 16), nq), pl.ds(c0, nc)]
        return copy(src, quarter(w, d, p, nq, c0, nc), zs.at[i, k], zr.at[i, k], (0, 2 * (k + 1)))

    def XY(i, k, axis):
        w, nq, c0, nc = jobs[i]
        ref = quarter(w, d ^ (2 * (k + 1)), p, nq, c0, nc)
        return copy(ref, ref, ps.at[i, k, axis], pr.at[i, k, axis], (1 + axis, 0))

    def DG(i, k, axis):
        w, nq, c0, nc = jobs[i]
        h = nc // 2
        ref = quarter(w, d ^ (2 * (k + 1)), p ^ (2 - axis), nq, c0 + axis * h, h)
        return copy(ref, ref, ps.at[i, k, 2 + axis], pr.at[i, k, 2 + axis], (1 + axis, 0))

    def S(i, k):
        w, nq, c0, nc = jobs[i]
        r = shards[w].shape[0]
        ref = fulls[w].at[pl.ds(pl.multiple_of((d ^ (2 * (k + 1))) * r, 16), r), pl.ds(c0, nc)]
        return copy(ref, ref, cs.at[i, k], cr.at[i, k], (0, 1))

    for i in range(min(AHEAD, J)):
        for k in range(3):
            Z(i, k).start()
    own = []
    for w in range(count):
        r = shards[w].shape[0]
        place = fulls[w].at[pl.ds(pl.multiple_of(d * r, 16), r)]
        pair = pltpu.make_async_copy(shards[w], place, ls.at[w]), copy(shards[w], place, os.at[w], orr.at[w], (0, 1))
        for c in pair:
            c.start()
        own.append(pair)
    targets[p] = target[...]
    named = [copy(target, targets.at[p], ts.at[m - 1], tr.at[m - 1], (m, 0)) for m in (1, 2, 3)]
    for c in named:
        c.start()
    section_mix(maps, taps, gain, mixed, rows, pad)

    ready = set()

    def ensure(w):
        if w not in ready:
            ready.add(w)
            own[w][0].wait()
            own[w][1].wait_recv()

    def expand_block(c0, nc):
        load = pltpu.make_async_copy(fulls[expand].at[:, pl.ds(c0, nc)], wide_w, ws.at[0])
        load.start()
        load.wait()

        def chunk(j, carry):
            here = pl.multiple_of(j * STEP, STEP)
            product(rows, wide_w, total, 0, here)
            stage[...] = total[...]
            active[:, pl.ds(c0 + here, STEP)] = jax.nn.gelu(total[...]).astype(jnp.bfloat16)
            out = pltpu.make_async_copy(stage, expanded.at[:, pl.ds(c0 + here, STEP)], es.at[0])
            out.start()
            out.wait()
            return carry

        lax.fori_loop(0, nc // STEP, chunk, 0)

    def reduce_block(c0, nc):
        load = pltpu.make_async_copy(fulls[reduce].at[:, pl.ds(c0, nc)], deep_w, ws.at[1])
        load.start()
        load.wait()
        cols = pl.ds(c0, nc)
        product(active, deep_w, total, 0, 0)
        reduced[:, cols] = total[...]
        side = maps.shape[0]

        def pool(h, carry):
            both = jnp.zeros((side, nc), jnp.float32)
            for r in range(2):
                row = 2 * h + r
                part = total[pl.ds(pl.multiple_of(row * side, 8), side), :]
                both += maps[row, :, cols].astype(jnp.float32) + scale[:, cols] * part
            half = side // 2
            for k in range(nc // LANES):
                pair_sum[k] = both[:, k * LANES : (k + 1) * LANES]
            for k in range(nc // LANES):
                even = pair_sum[k, pl.ds(0, half, stride=2), :]
                odd = pair_sum[k, pl.ds(1, half, stride=2), :]
                pooled[h, :, c0 + k * LANES : c0 + (k + 1) * LANES] = (even + odd) * 0.25
            return carry

        lax.fori_loop(0, side // 2, pool, 0)

    for i in range(J + 3):
        if i < J:
            for k in range(3):
                Z(i, k).wait_recv()
                XY(i, k, 0).start()
                XY(i, k, 1).start()
            if i + AHEAD < J:
                for k in range(3):
                    Z(i + AHEAD, k).start()
        if 0 <= i - 1 < J:
            for k in range(3):
                XY(i - 1, k, 0).wait_recv()
                DG(i - 1, k, 1).start()
                XY(i - 1, k, 1).wait_recv()
                DG(i - 1, k, 0).start()
        if 0 <= i - 2 < J:
            for k in range(3):
                DG(i - 2, k, 0).wait_recv()
                DG(i - 2, k, 1).wait_recv()
                S(i - 2, k).start()
        if 0 <= i - 3 < J:
            for k in range(3):
                S(i - 3, k).wait_recv()
            w, _, c0, nc = jobs[i - 3]
            ensure(w)
            if w == expand:
                expand_block(c0, nc)
            if w == reduce:
                reduce_block(c0, nc)
    for c in named:
        c.wait()
    for w in range(count):
        ensure(w)
        own[w][1].wait_send()
    for i in range(J):
        for k in range(3):
            Z(i, k).wait_send()
            S(i, k).wait_send()
            for a in range(2):
                XY(i, k, a).wait_send()
                DG(i, k, a).wait_send()


AHEAD = 3
GATHER_ORDER = (4, 0, 1, 5, 6, 3, 2)


def gather_weights(shards, maps, taps, gain, scale, target, expand, reduce):
    shapes = [s.shape for s in shards]
    jobs = gather_jobs(shapes)
    n, J = len(shards), len(jobs)
    side, _, channels = maps.shape
    cells, hidden = side * side, shapes[expand][1]
    wide = max(nc for w, _, _, nc in jobs if w == expand)
    low, full = jnp.bfloat16, jnp.float32
    anyspec, whole = pl.BlockSpec(memory_space=pl.ANY), pl.BlockSpec(memory_space=VMEM)
    dma = pltpu.SemaphoreType.DMA
    shape = jax.ShapeDtypeStruct
    results = pl.pallas_call(
        functools.partial(gather_kernel, jobs, n, expand, reduce),
        out_shape=[shape((8 * r, c), low) for r, c in shapes]
        + [
            shape(maps.shape, full),
            shape((cells, channels), low),
            shape((4, 8, LANES), jnp.int32),
            shape((cells, hidden), full),
            shape((cells, hidden), low),
            shape((cells, channels), full),
            shape((side // 2, side // 2, channels), full),
        ],
        in_specs=[anyspec] * n + [whole] * 5,
        out_specs=[anyspec] * n + [whole] * 3 + [anyspec] + [whole] * 3,
        scratch_shapes=[
            VMEM((side + 2 * REACH, side + 2 * EDGE, LANES), full),
            VMEM((channels, wide), low),
            VMEM((hidden, STEP), low),
            VMEM((cells, STEP), full),
            VMEM((cells, STEP), full),
            VMEM((STEP // LANES, side, LANES), full),
        ]
        + [dma((J, 3)), dma((J, 3)), dma((J, 3, 4)), dma((J, 3, 4)), dma((J, 3)), dma((J, 3))]
        + [dma((n,)), dma((n,)), dma((n,)), dma((3,)), dma((3,)), dma((2,)), dma((1,))],
        compiler_params=pltpu.CompilerParams(
            collective_id=0, has_side_effects=True, vmem_limit_bytes=60 * 2**20
        ),
    )(
        *shards, maps, taps, gain.reshape(1, channels), scale.reshape(1, channels),
        jnp.broadcast_to(target, (8, LANES)),
    )
    rest = results[n:]
    return results[:n], rest[0], rest[1], rest[2][:, 0, 0], rest[3], rest[4], rest[5], rest[6]


def add_block(total, term):
    return (total.astype(jnp.float32) + term.astype(jnp.float32)).astype(jnp.bfloat16)


def scatter_kernel(
    big0, big1, land0a, land0b, t0, t1, t2, t3, small_in, grad_normed, mixed, maps, taps, gain,
    grad_maps, small_out, o0, o1, o2, o3, o4, o5, land1a, land1b,
    acc0a, acc0b, acc1a, acc1b, two0a, two0b, two1a, two1b, tmp0, tmp1,
    own0, own1, own2, own3, two0, two1, two2, two3,
    zr0, zr1, zr2, zr3, zr4, zr5, low0, low1, low2, low3, low4, low5,
    full0, full1, full2, full3, full4, full5,
    small_at, small_from, pad, grad_pad, tap_sums, ssem, rsem, lsem,
):
    p, d = lax.axis_index("path"), lax.axis_index("dev")
    up, across, height, side = p // 2, lax.rem(p, 2), d // 2, lax.rem(d, 2)
    masks = [(0, 1), (0, 2), (0, 4), (0, 6), (1, 0), (2, 0), (3, 0)]
    bar = pltpu.get_barrier_semaphore()
    for m in masks:
        pl.semaphore_signal(bar, inc=1, device_id=(p ^ m[0], d ^ m[1]), device_id_type=MESH)
    pl.semaphore_wait(bar, len(masks))

    copies = []

    def send(src, dst, m):
        n = len(copies)
        copy = pltpu.make_async_remote_copy(
            src, dst, ssem.at[n], rsem.at[n], device_id=(p ^ m[0], d ^ m[1]), device_id_type=MESH
        )
        copies.append(copy)
        copy.start()
        return copy

    local = []

    def fetch(src, dst):
        copy = pltpu.make_async_copy(src, dst, lsem.at[len(local)])
        local.append(copy)
        copy.start()
        return copy

    thin = [(t0, own0, two0, True), (t1, own1, two1, False), (t2, own2, two2, True), (t3, own3, two3, False)]
    wide = [
        (big0, (acc0a, acc0b), (land0a, land0b), (two0a, two0b), tmp0),
        (big1, (acc1a, acc1b), (land1a, land1b), (two1a, two1b), tmp1),
    ]
    outs = [o0, o1, o2, o3, o4, o5]
    zrs, lows, wholes = [zr0, zr1, zr2, zr3, zr4, zr5], [low0, low1, low2, low3, low4, low5], [full0, full1, full2, full3, full4, full5]

    def thin_two(i):
        src, own, two, upward = thin[i]
        index, mask = (up, (2, 0)) if upward else (across, (1, 0))
        loaded = fetch(src.at[:, :, index], own)
        return loaded, send(src.at[:, :, 1 - index], two, mask)

    def wide_one(w, ours):
        src, acc, land, _, _ = wide[w]
        half = src.shape[5] // 2
        a, b = pl.ds(0, half), pl.ds(half, half)
        loaded = [fetch(src.at[:, :, :, across, :, a], acc[0]), fetch(src.at[:, :, up, :, :, b], acc[1])]
        if not ours:
            return loaded
        return loaded + [
            send(src.at[:, :, :, 1 - across, :, a], land[0], (1, 0)),
            send(src.at[:, :, 1 - up, :, :, b], land[1], (2, 0)),
        ]

    def wide_two(w, started):
        src, acc, land, two, tmp = wide[w]
        started[0].wait()
        started[1].wait()
        sent = []
        for copy in started[2:]:
            copy.wait_recv()
        for k in range(2):
            loads = [fetch(land[k].at[0], tmp.at[0])]
            for z in range(4):
                if z < 3:
                    loads.append(fetch(land[k].at[z + 1], tmp.at[(z + 1) % 2]))
                loads[z].wait()
                for c in range(2):
                    for q in range(2):
                        acc[k][z, c, q] = add_block(acc[k][z, c, q], tmp[z % 2, c, q])
            index, mask = (up, (2, 0)) if k == 0 else (across, (1, 0))
            sent.append(send(acc[k].at[:, :, 1 - index], two[k], mask))
        return sent

    def heights(n, parts, k):
        zr = zrs[n]
        half = zr.shape[3] // len(parts)
        return [
            send(parts[k].at[height ^ m], zr.at[m - 1, :, :, pl.ds(k * half, half)], (0, 2 * m)) for m in (1, 2, 3)
        ]

    def thin_three(i, started):
        _, own, two, _ = thin[i]
        started[0].wait()
        started[1].wait_recv()
        for z in range(4):
            for c in range(2):
                two[z, c] = add_block(two[z, c], own[z, c])
        return heights(i, [two], 0)

    def wide_three(w, sent):
        _, acc, _, two, _ = wide[w]
        for k in range(2):
            index = up if k == 0 else across
            sent[k].wait_recv()
            for z in range(4):
                for c in range(2):
                    two[k][z, c] = add_block(two[k][z, c], acc[k][z, c, index])
        return heights(4 + w, two, 0)

    def total(n, parts, k, sent):
        for copy in sent:
            copy.wait_recv()
        zr, low, whole = zrs[n], lows[n], wholes[n]
        size = zr.shape[3]
        half = size // len(parts)
        cols = slice(k * half, (k + 1) * half)
        for c in range(2):
            value = parts[k][height, c].astype(jnp.float32)
            for m in range(3):
                value = value + zr[m, c, :, cols].astype(jnp.float32)
            low[c, :, cols] = value.astype(jnp.bfloat16)
        place = (slice(None), pl.ds(pl.multiple_of(side * size + k * half, LANES), half))
        whole[place] = low[side, :, cols]
        return send(low.at[1 - side, :, cols], whole.at[place], (0, 1))

    def spread(n, swapped):
        swapped.wait_recv()
        return [fetch(wholes[n], outs[n].at[p])] + [send(wholes[n], outs[n].at[p], (m, 0)) for m in (1, 2, 3)]

    def spread_part(n, k, swapped):
        swapped.wait_recv()
        size = zrs[n].shape[3]
        copies = []
        for c in range(2):
            cols = pl.ds(c * size + k * (size // 2), size // 2)
            src, dst = wholes[n].at[:, cols], outs[n].at[p, :, cols]
            copies += [fetch(src, dst)] + [send(src, dst, (m, 0)) for m in (1, 2, 3)]
        return copies

    side_cells, _, channels = maps.shape
    count = channels // LANES

    def norm_back():
        clear_edges(pad, side_cells)
        clear_edges(grad_pad, side_cells)
        small_at[0] = small_in[...]

        def norm(h, carry):
            v = mixed[h]
            centred = v - jnp.mean(v, axis=-1, keepdims=True)
            scale = lax.rsqrt(jnp.mean(centred * centred, axis=-1, keepdims=True) + 1e-06)
            unit = centred * scale
            grad = grad_normed[h]
            small_at[0, SIDE * SIDE : SIDE * SIDE + 1, :] += jnp.sum(grad * unit, axis=0, keepdims=True)
            grad = grad * gain[...]
            grad_maps[h] = scale * (
                grad - jnp.mean(grad, axis=-1, keepdims=True) - unit * jnp.mean(grad * unit, axis=-1, keepdims=True)
            )
            return carry

        lax.fori_loop(0, side_cells, norm, 0)

    def blocks(first, last):
        def one(block, carry):
            at = lane_block(block)
            inside = (slice(REACH, REACH + side_cells), slice(EDGE, EDGE + side_cells), slice(None))
            pad[inside] = maps[:, :, at].astype(jnp.float32)
            grad_pad[inside] = grad_maps[:, :, at]
            tap_sums[...] = jnp.zeros_like(tap_sums)

            def rows(group, inner):
                base = group * GROUP
                sums = conv_rows(grad_pad, lambda t: taps[pl.ds(t, 1), at], group, True, side_cells)
                for r in range(GROUP):
                    grad_maps[base + r, :, at] = sums[r]
                for dc in range(SIDE):
                    grads = [grad_pad[base + REACH + r, EDGE : EDGE + side_cells, :] for r in range(GROUP)]
                    acc = [None] * SIDE
                    for j in range(GROUP + SIDE - 1):
                        row = pad[base + j, EDGE - REACH + dc : EDGE - REACH + dc + side_cells, :]
                        for r in range(GROUP):
                            dr = j - r
                            if 0 <= dr < SIDE:
                                term = row * grads[r]
                                acc[dr] = term if acc[dr] is None else acc[dr] + term
                    for dr in range(SIDE):
                        tap_sums[dr * SIDE + dc] += jnp.sum(acc[dr].reshape(side_cells // 8, 8, LANES), axis=0)
                return inner

            lax.fori_loop(0, side_cells // GROUP, rows, 0)
            small_at[0, : SIDE * SIDE, at] = jnp.sum(tap_sums[...], axis=1)
            return carry

        lax.fori_loop(first, last, one, 0)

    small_masks = [(0, 1), (1, 0), (2, 0), (0, 2), (0, 4)]

    def small_send(s):
        return send(small_at.at[s], small_from.at[s], small_masks[s])

    def small_step(s, copy):
        copy.wait_recv()
        value = small_at[s] + small_from[s]
        if s + 1 < len(small_masks):
            small_at[s + 1] = value
            return small_send(s + 1)
        small_out[...] = value

    thin_sent = [thin_two(i) for i in range(4)]
    one_reduce = wide_one(0, False)
    norm_back()
    blocks(0, count // 6)
    two_reduce = wide_two(0, one_reduce)
    blocks(count // 6, count // 3)
    thin_high = [thin_three(i, thin_sent[i]) for i in range(4)]
    one_expand = wide_one(1, True)
    blocks(count // 3, count // 2)
    high_reduce = wide_three(0, two_reduce)
    high_reduce += heights(4, wide[0][3], 1)
    blocks(count // 2, count)
    small = small_send(0)
    two_expand = wide_two(1, one_expand)
    small = small_step(0, small)
    swaps = [total(i, [thin[i][2]], 0, thin_high[i]) for i in range(4)]
    small = small_step(1, small)
    high_expand = wide_three(1, two_expand)
    last = [spread(i, swaps[i]) for i in range(4)]
    small = small_step(2, small)
    for copy in high_reduce:
        copy.wait_recv()
    swap_reduce = [total(4, wide[0][3], k, []) for k in range(2)]
    swap_reduce[0].wait_recv()
    last.append(spread(4, swap_reduce[1]))
    small = small_step(3, small)
    swap_low = total(5, wide[1][3], 0, high_expand)
    high_expand = heights(5, wide[1][3], 1)
    last.append(spread_part(5, 0, swap_low))
    small = small_step(4, small)
    swap_high = total(5, wide[1][3], 1, high_expand)
    last.append(spread_part(5, 1, swap_high))
    for group in last:
        for k, copy in enumerate(group):
            if k % 4:
                copy.wait_recv()
            else:
                copy.wait()
    for copy in copies:
        copy.wait_send()


def scatter_gradients(part_reduce, part_expand, landed, thins, small, grad_normed, mixed, maps, taps, gain):
    side, _, channels = maps.shape
    low, full = jnp.bfloat16, jnp.float32
    anyspec, whole = pl.BlockSpec(memory_space=pl.ANY), pl.BlockSpec(memory_space=VMEM)
    dma = pltpu.SemaphoreType.DMA
    finals = [(t.shape[3], t.shape[4]) for t in thins] + [w.shape[4:] for w in (part_reduce, part_expand)]
    scratch = []
    for w in (part_reduce, part_expand):
        shape = w.shape[:3] + (w.shape[4], w.shape[5] // 2)
        landing = [jax.ShapeDtypeStruct(shape, low)] * 2
        scratch += [VMEM(shape, low)] * 2
    scratch += [VMEM(w.shape[:2] + (w.shape[4], w.shape[5] // 2), low) for w in (part_reduce, part_expand) for _ in range(2)]
    scratch += [VMEM((2, 2, 2, w.shape[4], w.shape[5] // 2), low) for w in (part_reduce, part_expand)]
    scratch += [VMEM(t.shape[:2] + t.shape[3:], low) for t in thins] * 2
    scratch += [VMEM((3, 2) + f, low) for f in finals]
    scratch += [VMEM((2,) + f, low) for f in finals]
    scratch += [VMEM((f[0], 2 * f[1]), low) for f in finals]
    edge = (side + 2 * REACH, side + 2 * EDGE, LANES)
    scratch += [VMEM((5,) + small.shape, full)] * 2
    scratch += [VMEM(edge, full)] * 2 + [VMEM((SIDE * SIDE, 8, LANES), full)]
    scratch += [dma((80,)), dma((80,)), dma((40,))]
    results = pl.pallas_call(
        scatter_kernel,
        out_shape=[jax.ShapeDtypeStruct(maps.shape, full), jax.ShapeDtypeStruct(small.shape, full)]
        + [jax.ShapeDtypeStruct((4, f[0], 2 * f[1]), low) for f in finals]
        + landing,
        in_specs=[anyspec] * 8 + [whole] * 6,
        out_specs=[whole] * 2 + [anyspec] * 8,
        scratch_shapes=scratch,
        compiler_params=pltpu.CompilerParams(
            collective_id=1, has_side_effects=True, vmem_limit_bytes=60 * 2**20
        ),
    )(part_reduce, part_expand, *landed, *thins, small, grad_normed, mixed, maps, taps, gain.reshape(1, channels))
    return results[0], results[1], results[2:8]


def layer_norm(values, gain_vec):
    centred = values - jnp.mean(values, axis=-1, keepdims=True)
    spread = jnp.mean(centred * centred, axis=-1, keepdims=True)
    return centred * lax.rsqrt(spread + 1e-06) * gain_vec


def depthwise(feature_map, taps_table, kernel_side):
    half_side = kernel_side // 2
    padded = jnp.pad(feature_map, ((0, 0), (half_side, half_side), (half_side, half_side), (0, 0)))
    map_side = feature_map.shape[1]
    accum_sum = jnp.zeros(feature_map.shape, feature_map.dtype)
    for offset_row in range(kernel_side):
        for offset_col in range(kernel_side):
            window = padded[
                :, offset_row : offset_row + map_side, offset_col : offset_col + map_side, :
            ]
            accum_sum = accum_sum + window * taps_table[offset_row * kernel_side + offset_col]
    return accum_sum


def section_depthwise(grid_field, grid_kernel):
    return depthwise(grid_field, grid_kernel, 7)


def adapter_depthwise(grid_field, grid_kernel):
    return depthwise(grid_field, grid_kernel, 3)


def swap(value, axis, mask):
    size = lax.axis_size(axis)
    return lax.ppermute(value, axis, [(i, i ^ mask) for i in range(size)])


def pick(value, index, axis):
    return lax.dynamic_index_in_dim(value, index, axis, keepdims=False)


def add_low(left, right):
    return (left.astype(jnp.float32) + right.astype(jnp.float32)).astype(jnp.bfloat16)


def place():
    path, dev = lax.axis_index("path"), lax.axis_index("dev")
    return path, path // 2, lax.rem(path, 2), dev // 2, lax.rem(dev, 2)


def both_images(rows):
    return jnp.concatenate([rows, swap(rows, "dev", 1)])


def pair_gradient(rows, grads):
    side = place()[4]
    half = grads.shape[1] // 2
    low, high = grads[:, :half], grads[:, half:]
    mine = jnp.where(side == 0, low, high)
    theirs = swap(jnp.where(side == 0, high, low), "dev", 1)
    product = lax.dot_general(
        rows, jnp.concatenate([mine, theirs]), (((0,), (0,)), ((), ())), preferred_element_type=jnp.float32
    )
    return product.astype(jnp.bfloat16).reshape(4, 2, 2, 2, rows.shape[1] // 32, half)


def across_half(share, axis):
    return swap(pick(share, 1 - place()[2], axis), "path", 1)


def up_half(share, axis):
    return swap(pick(share, 1 - place()[1], axis), "path", 2)


def across_sum(share, axis, other):
    return add_low(pick(share, place()[2], axis), other)


def up_sum(share, axis, other):
    return add_low(pick(share, place()[1], axis), other)


def tie(*values):
    return lax.optimization_barrier(values)


def finish(pieces):
    return pieces.reshape(-1, pieces.shape[2]).astype(jnp.float32)


def plain_sum(rows, grads):
    product = lax.dot_general(
        rows, grads, (((0,), (0,)), ((), ())), preferred_element_type=jnp.float32
    ).astype(jnp.bfloat16)
    share = lax.psum_scatter(product, "dev", scatter_dimension=0, tiled=True)
    return lax.psum(share, "path").astype(jnp.float32)


def local(
    inputs,
    hires_maps,
    target_path,
    cotangent,
    attn_gain,
    w_qkv,
    w_out,
    mlp_gain,
    w_fc1,
    w_fc2,
    w_adapter,
    adapter_kernel,
    merge_gate,
    section_kernel,
    section_gain,
    w_expand,
    w_reduce,
    layer_scale,
):
    tuned = lax.axis_size("path") == 4 and lax.axis_size("dev") == 8
    weights = (w_expand, w_reduce, w_adapter, w_qkv, w_out, w_fc1, w_fc2)
    if tuned:
        ordered, section_mixed, section_rows, spread_targets, expanded, activated_low, reduced, pooled = gather_weights(
            [weights[i] for i in GATHER_ORDER],
            hires_maps[0],
            section_kernel,
            section_gain,
            layer_scale,
            target_path,
            GATHER_ORDER.index(0),
            GATHER_ORDER.index(1),
        )
        fulls = [ordered[GATHER_ORDER.index(i)] for i in range(len(weights))]
    else:
        fulls = [lax.all_gather(shard, "dev", axis=0, tiled=True) for shard in weights]
    full_expand, full_reduce, full_adapter, full_qkv, full_out, full_fc1, full_fc2 = fulls
    path_count = lax.axis_size("path")
    maps_float = hires_maps.astype(jnp.float32)
    map_side = maps_float.shape[1]
    channels = maps_float.shape[3]
    grid_side = map_side // 2
    tokens = grid_side * grid_side
    quarter_rows = tokens // path_count
    model_width = inputs.shape[2]
    head_count = model_width // HEAD_DIM
    score_scale = HEAD_DIM ** (-0.5)
    if not tuned:
        section_mixed, section_back = jax.vjp(section_depthwise, maps_float, section_kernel)
        section_normed, section_norm_back = jax.vjp(layer_norm, section_mixed, section_gain)
    if tuned:
        _, section_gelu_back = jax.vjp(jax.nn.gelu, expanded)
        reduced = reduced.reshape(maps_float.shape)
    else:
        section_rows = section_normed.reshape(-1, channels).astype(jnp.bfloat16)
        expanded = jnp.dot(section_rows, full_expand, preferred_element_type=jnp.float32)
        activated, section_gelu_back = jax.vjp(jax.nn.gelu, expanded)
        activated_low = activated.astype(jnp.bfloat16)
        reduced = jnp.dot(activated_low, full_reduce, preferred_element_type=jnp.float32).reshape(
            maps_float.shape
        )
        section_out = maps_float + layer_scale * reduced
        pooled = jnp.mean(
            section_out.reshape(grid_side, 2, grid_side, 2, channels), axis=(1, 3)
        ).reshape(tokens, channels)
    pieces = pooled.astype(jnp.bfloat16).reshape(path_count, quarter_rows, channels)
    spread_pieces = lax.all_to_all(pieces, "path", split_axis=0, concat_axis=0, tiled=True)
    if not tuned:
        own_target = jnp.broadcast_to(target_path, (path_count, 1))
        spread_targets = lax.all_to_all(own_target, "path", split_axis=0, concat_axis=0, tiled=True)
    selector = (
        jnp.arange(path_count, dtype=jnp.int32)[:, None] == spread_targets.reshape(1, path_count)
    ).astype(jnp.float32)
    routed = jnp.einsum("pq,qtc->ptc", selector, spread_pieces.astype(jnp.float32)).astype(
        jnp.bfloat16
    )
    arrived = lax.all_to_all(routed, "path", split_axis=0, concat_axis=0, tiled=True)
    features = arrived.reshape(tokens, channels)
    adapted = jnp.dot(features, full_adapter, preferred_element_type=jnp.float32)
    spread_map, adapter_back = jax.vjp(
        adapter_depthwise, adapted.reshape(1, grid_side, grid_side, model_width), adapter_kernel
    )
    spread_rows = spread_map.reshape(tokens, model_width)
    gate_factor = jnp.tanh(merge_gate)
    hidden_in = inputs[0].astype(jnp.float32) + gate_factor * spread_rows
    normed_one, norm_one_back = jax.vjp(layer_norm, hidden_in, attn_gain)
    attn_rows = normed_one.astype(jnp.bfloat16)
    projected = jnp.dot(attn_rows, full_qkv, preferred_element_type=jnp.float32).astype(
        jnp.bfloat16
    )
    queries = projected[:, :model_width].reshape(tokens, head_count, HEAD_DIM)
    key_rows = projected[:, model_width : 2 * model_width].reshape(tokens, head_count, HEAD_DIM)
    values = projected[:, 2 * model_width :].reshape(tokens, head_count, HEAD_DIM)
    scores = (
        jnp.einsum("thd,shd->hts", queries, key_rows, preferred_element_type=jnp.float32)
        * score_scale
    )
    probs = jax.nn.softmax(scores, axis=-1)
    probs_low = probs.astype(jnp.bfloat16)
    attn_mixed = jnp.einsum("hts,shd->thd", probs_low, values, preferred_element_type=jnp.float32)
    attn_mixed = attn_mixed.astype(jnp.bfloat16).reshape(tokens, model_width)
    attended = jnp.dot(attn_mixed, full_out, preferred_element_type=jnp.float32)
    hidden_mid = hidden_in + attended
    normed_two, norm_two_back = jax.vjp(layer_norm, hidden_mid, mlp_gain)
    mlp_rows = normed_two.astype(jnp.bfloat16)
    raised = jnp.dot(mlp_rows, full_fc1, preferred_element_type=jnp.float32)
    lifted_value, gelu_back = jax.vjp(jax.nn.gelu, raised)
    lifted = lifted_value.astype(jnp.bfloat16)
    lowered = jnp.dot(lifted, full_fc2, preferred_element_type=jnp.float32)
    result = (hidden_mid + lowered)[None].astype(jnp.bfloat16)
    grad_out = cotangent[0].astype(jnp.float32)
    grad_out_low = grad_out.astype(jnp.bfloat16)
    if tuned:
        part_fc2 = pair_gradient(both_images(lifted), grad_out_low)
    else:
        grad_fc2_w = plain_sum(lifted, grad_out_low)
    grad_lifted = jnp.dot(grad_out_low, full_fc2.T, preferred_element_type=jnp.float32)
    grad_raised = gelu_back(grad_lifted)[0].astype(jnp.bfloat16)
    if tuned:
        part_fc1 = pair_gradient(both_images(mlp_rows), grad_raised)
    else:
        grad_fc1_w = plain_sum(mlp_rows, grad_raised)
    grad_normed_two = jnp.dot(grad_raised, full_fc1.T, preferred_element_type=jnp.float32)
    grad_mid_norm, grad_mlp_gain = norm_two_back(grad_normed_two)
    grad_mid = grad_out + grad_mid_norm
    grad_attended = grad_mid.astype(jnp.bfloat16)
    if tuned:
        part_out = pair_gradient(both_images(attn_mixed), grad_attended)
    else:
        grad_out_w = plain_sum(attn_mixed, grad_attended)
    grad_mixed = jnp.dot(grad_attended, full_out.T, preferred_element_type=jnp.float32)
    grad_mixed = grad_mixed.astype(jnp.bfloat16).reshape(tokens, head_count, HEAD_DIM)
    grad_probs = jnp.einsum("thd,shd->hts", grad_mixed, values, preferred_element_type=jnp.float32)
    grad_values = jnp.einsum(
        "hts,thd->shd", probs_low, grad_mixed, preferred_element_type=jnp.float32
    )
    grad_scores = probs * (grad_probs - jnp.sum(grad_probs * probs, axis=-1, keepdims=True))
    grad_scores = grad_scores.astype(jnp.bfloat16)
    grad_queries = (
        jnp.einsum("hts,shd->thd", grad_scores, key_rows, preferred_element_type=jnp.float32)
        * score_scale
    )
    grad_keys = (
        jnp.einsum("hts,thd->shd", grad_scores, queries, preferred_element_type=jnp.float32)
        * score_scale
    )
    grad_projected = jnp.concatenate(
        [
            grad_queries.reshape(tokens, model_width),
            grad_keys.reshape(tokens, model_width),
            grad_values.reshape(tokens, model_width),
        ],
        axis=1,
    ).astype(jnp.bfloat16)
    if tuned:
        part_qkv = pair_gradient(both_images(attn_rows), grad_projected)
    else:
        grad_qkv_w = plain_sum(attn_rows, grad_projected)
    grad_normed_one = jnp.dot(grad_projected, full_qkv.T, preferred_element_type=jnp.float32)
    grad_in_norm, grad_attn_gain = norm_one_back(grad_normed_one)
    grad_in = grad_mid + grad_in_norm
    grad_merge = jnp.sum(grad_in * spread_rows, axis=0) * (1.0 - gate_factor * gate_factor)
    grad_spread = (grad_in * gate_factor).reshape(1, grid_side, grid_side, model_width)
    grad_adapted, grad_adapter_taps = adapter_back(grad_spread)
    grad_adapted_low = grad_adapted.reshape(tokens, model_width).astype(jnp.bfloat16)
    if tuned:
        part_adapter = pair_gradient(both_images(features), grad_adapted_low)
    else:
        grad_adapter_w = plain_sum(features, grad_adapted_low)
    grad_features = jnp.dot(grad_adapted_low, full_adapter.T, preferred_element_type=jnp.float32)
    if tuned:
        grad_features, part_fc2, part_fc1 = tie(grad_features, part_fc2, part_fc1)
    grad_pieces = grad_features.astype(jnp.bfloat16).reshape(path_count, quarter_rows, channels)
    grad_routed = lax.all_to_all(grad_pieces, "path", split_axis=0, concat_axis=0, tiled=True)
    grad_unrouted = jnp.einsum("pq,ptc->qtc", selector, grad_routed.astype(jnp.float32)).astype(
        jnp.bfloat16
    )
    grad_home = lax.all_to_all(grad_unrouted, "path", split_axis=0, concat_axis=0, tiled=True)
    if tuned:
        part_rest = jnp.concatenate([part_out, part_adapter], axis=4)
        grad_home, part_fc2, part_fc1, part_qkv, part_rest = tie(grad_home, part_fc2, part_fc1, part_qkv, part_rest)
        half_fc2, half_fc1 = across_half(part_fc2, 3), up_half(part_fc1, 2)
    grad_pooled = grad_home.astype(jnp.float32).reshape(tokens, channels)
    quarter = (grad_pooled * 0.25).reshape(1, grid_side, 1, grid_side, 1, channels)
    grad_section_out = jnp.broadcast_to(quarter, (1, grid_side, 2, grid_side, 2, channels)).reshape(
        maps_float.shape
    )
    grad_scale = jnp.sum((grad_section_out * reduced).reshape(-1, channels), axis=0)
    grad_reduced = (grad_section_out * layer_scale).reshape(-1, channels).astype(jnp.bfloat16)
    if tuned:
        part_reduce = pair_gradient(both_images(activated_low), grad_reduced)
        grad_reduced, part_reduce, half_fc2, half_fc1 = tie(grad_reduced, part_reduce, half_fc2, half_fc1)
        half_qkv, half_rest = across_half(part_qkv, 3), up_half(part_rest, 2)
        columns = part_reduce.shape[5] // 2
        landed = [across_half(part_reduce[..., :columns], 3), up_half(part_reduce[..., columns:], 2)]
    else:
        grad_reduce_w = plain_sum(activated_low, grad_reduced)
    grad_activated = jnp.dot(grad_reduced, full_reduce.T, preferred_element_type=jnp.float32)
    grad_expanded = section_gelu_back(grad_activated)[0].astype(jnp.bfloat16)
    if tuned:
        part_expand = pair_gradient(both_images(section_rows), grad_expanded)
    else:
        grad_expand_w = plain_sum(section_rows, grad_expanded)
    grad_section_normed = jnp.dot(
        grad_expanded, full_expand.T, preferred_element_type=jnp.float32
    ).reshape(maps_float.shape)
    if tuned:
        part_expand, half_qkv, half_rest = tie(part_expand, half_qkv, half_rest)
        step_fc2, step_fc1 = across_sum(part_fc2, 3, half_fc2), up_sum(part_fc1, 2, half_fc1)
        step_qkv, step_rest = across_sum(part_qkv, 3, half_qkv), up_sum(part_rest, 2, half_rest)
        small_rows = jnp.concatenate(
            [
                jnp.zeros((section_kernel.shape[0] + 1, channels), jnp.float32),
                jnp.concatenate([grad_attn_gain, grad_mlp_gain, grad_merge, grad_adapter_taps.reshape(-1)]).reshape(-1, channels),
                grad_scale[None],
            ]
        )
        small_count = small_rows.shape[0]
        small_rows = jnp.pad(small_rows, ((0, -small_count % 8), (0, 0)))
        grad_maps, small_rows, pieces = scatter_gradients(
            part_reduce,
            part_expand,
            landed,
            [step_fc2, step_fc1, step_qkv, step_rest],
            small_rows,
            grad_section_normed[0],
            section_mixed,
            hires_maps[0],
            section_kernel,
            section_gain,
        )
        grad_maps = grad_maps[None] + grad_section_out
        split = part_out.shape[4]
        grad_fc2_w, grad_fc1_w, grad_qkv_w = [finish(piece) for piece in pieces[:3]]
        grad_out_w, grad_adapter_w = finish(pieces[3][:, :split]), finish(pieces[3][:, split:])
        grad_reduce_w, grad_expand_w = finish(pieces[4]), finish(pieces[5])
    else:
        grad_section_mixed, grad_section_gain = section_norm_back(grad_section_normed)
        grad_maps_conv, grad_section_taps = section_back(grad_section_mixed)
        grad_maps = grad_section_out + grad_maps_conv
    summed = (
        grad_qkv_w,
        grad_out_w,
        grad_fc1_w,
        grad_fc2_w,
        grad_adapter_w,
        grad_expand_w,
        grad_reduce_w,
    )
    if tuned:
        tap_count = section_kernel.shape[0]
        flat = small_rows[tap_count + 1 : small_count - 1].reshape(-1)
        small_sums = (
            flat[:model_width],
            flat[model_width : 2 * model_width],
            flat[2 * model_width : 3 * model_width],
            flat[3 * model_width :].reshape(adapter_kernel.shape),
            small_rows[tap_count],
            small_rows[:tap_count],
            small_rows[small_count - 1],
        )
    else:
        small_sums = lax.psum(
            (
                grad_attn_gain,
                grad_mlp_gain,
                grad_merge,
                grad_adapter_taps,
                grad_section_gain,
                grad_section_taps,
                grad_scale,
            ),
            ("path", "dev"),
        )
    return (
        result,
        grad_in[None],
        grad_maps,
        small_sums[0],
        summed[0],
        summed[1],
        small_sums[1],
        summed[2],
        summed[3],
        summed[4],
        small_sums[3],
        small_sums[2],
        small_sums[5],
        small_sums[4],
        summed[5],
        summed[6],
        small_sums[6],
    )


def solution(mesh):
    return jax.shard_map(
        local,
        mesh=mesh,
        in_specs=(
            P(("path", "dev"), None, None),
            P(("path", "dev"), None, None, None),
            P("path", "dev"),
            P(("path", "dev"), None, None),
            P(),
            P("dev", None),
            P("dev", None),
            P(),
            P("dev", None),
            P("dev", None),
            P("dev", None),
            P(),
            P(),
            P(),
            P(),
            P("dev", None),
            P("dev", None),
            P(),
        ),
        out_specs=(
            P(("path", "dev"), None, None),
            P(("path", "dev"), None, None),
            P(("path", "dev"), None, None, None),
            P(),
            P("dev", None),
            P("dev", None),
            P(),
            P("dev", None),
            P("dev", None),
            P("dev", None),
            P(),
            P(),
            P(),
            P(),
            P("dev", None),
            P("dev", None),
            P(),
        ),
        check_vma=False,
    )
```

```python
import functools

import jax
import jax.numpy as jnp
from jax import lax
from jax.experimental import pallas as pl
from jax.experimental.pallas import tpu as pltpu
from jax.sharding import PartitionSpec as P

HEAD_DIM = 64
MESH = pl.DeviceIdType.MESH
VMEM = pltpu.VMEM
SIDE, REACH, EDGE, GROUP, LANES = 7, 3, 8, 8, 128


def conv_rows(src, taps, group, flip, side):
    base = group * GROUP
    sums = [None] * GROUP
    for dc in range(SIDE):
        col = [taps((SIDE - 1 - dr) * SIDE + SIDE - 1 - dc if flip else dr * SIDE + dc) for dr in range(SIDE)]
        for j in range(GROUP + SIDE - 1):
            row = src[base + j, EDGE - REACH + dc : EDGE - REACH + dc + side, :]
            for r in range(GROUP):
                if 0 <= j - r < SIDE:
                    term = row * col[j - r]
                    sums[r] = term if sums[r] is None else sums[r] + term
    return sums


def clear_edges(pad, side):
    rows, columns, lanes = pad.shape[-3:]
    pad[:, :EDGE, :] = jnp.zeros((rows, EDGE, lanes), jnp.float32)
    pad[:, EDGE + side :, :] = jnp.zeros((rows, columns - EDGE - side, lanes), jnp.float32)
    pad[:REACH] = jnp.zeros((REACH, columns, lanes), jnp.float32)
    pad[REACH + side :] = jnp.zeros((rows - REACH - side, columns, lanes), jnp.float32)


def lane_block(block):
    return pl.ds(pl.multiple_of(block * LANES, LANES), LANES)


def mix_block(block, maps, taps, mixed, pad):
    side = maps.shape[0]
    at = lane_block(block)
    pad[REACH : REACH + side, EDGE : EDGE + side, :] = maps[:, :, at].astype(jnp.float32)

    def rows(group, carry):
        sums = conv_rows(pad, lambda t: taps[pl.ds(t, 1), at], group, False, side)
        for r in range(GROUP):
            mixed[group * GROUP + r, :, at] = sums[r]
        return carry

    lax.fori_loop(0, side // GROUP, rows, 0)


def section_mix(maps, taps, gain, mixed, rows, pad):
    side, _, channels = maps.shape
    clear_edges(pad, side)

    def blocks(block, carry):
        mix_block(block, maps, taps, mixed, pad)
        return carry

    lax.fori_loop(0, channels // LANES, blocks, 0)

    def norm(pair, carry):
        v = mixed[pl.ds(2 * pair, 2)].reshape(2 * side, channels)
        centred = v - jnp.mean(v, axis=-1, keepdims=True)
        scale = lax.rsqrt(jnp.mean(centred * centred, axis=-1, keepdims=True) + 1e-06)
        at = pl.ds(pl.multiple_of(pair * 2 * side, 2 * side), 2 * side)
        rows[at, :] = (centred * scale * gain[...]).astype(jnp.bfloat16)
        return carry

    lax.fori_loop(0, side // 2, norm, 0)


STEP = 512


def product(left, right, total, left_at, right_at):
    total[...] = jnp.zeros_like(total)

    def step(k, carry):
        here = pl.multiple_of(k * STEP, STEP)
        total[...] += jnp.dot(
            left[:, pl.ds(left_at + here, STEP)],
            right[pl.ds(here, STEP), pl.ds(pl.multiple_of(right_at, STEP), STEP)],
            preferred_element_type=jnp.float32,
        )
        return carry

    lax.fori_loop(0, right.shape[0] // STEP, step, 0)


def gather_jobs(shapes):
    jobs = []
    for w, (r, n) in enumerate(shapes):
        parts = max(1, round(r // 4 * n / (16 * 6144)))
        while n % (parts * STEP):
            parts -= 1
        jobs += [(w, r // 4, k * (n // parts), n // parts) for k in range(parts)]
    return jobs


def gather_kernel(jobs, count, expand, reduce, *refs):
    shards = refs[:count]
    maps, taps, gain, scale, target = refs[count : count + 5]
    fulls = refs[count + 5 : 2 * count + 5]
    mixed, rows, targets, expanded, active, reduced, features = refs[2 * count + 5 : 2 * count + 12]
    pad, wide_w, deep_w, total, stage, pair_sum, pooled, leaving, met, sorted_maps, landing = refs[2 * count + 12 : 2 * count + 23]
    zs, zr, ps, pr, cs, cr, os, orr, ls, ts, tr, ws, es, fs, fr, gs, gr = refs[2 * count + 23 :]
    p, d = lax.axis_index("path"), lax.axis_index("dev")

    def at(m):
        return (p ^ m[0], d ^ m[1])

    masks = [(0, 1), (0, 2), (0, 4), (0, 6), (1, 0), (2, 0), (3, 0)]
    bar = pltpu.get_barrier_semaphore()
    for m in masks:
        pl.semaphore_signal(bar, inc=1, device_id=at(m), device_id_type=MESH)
    pl.semaphore_wait(bar, len(masks))

    def copy(src, dst, ss, rs, m):
        return pltpu.make_async_remote_copy(src, dst, ss, rs, device_id=at(m), device_id_type=MESH)

    def quarter(w, owner, q, nq, c0, nc):
        r = shards[w].shape[0]
        return fulls[w].at[pl.ds(pl.multiple_of(owner * r + q * nq, 16), nq), pl.ds(c0, nc)]

    J = len(jobs)

    def Z(i, k):
        w, nq, c0, nc = jobs[i]
        src = shards[w].at[pl.ds(pl.multiple_of(p * nq, 16), nq), pl.ds(c0, nc)]
        return copy(src, quarter(w, d, p, nq, c0, nc), zs.at[i, k], zr.at[i, k], (0, 2 * (k + 1)))

    def XY(i, k, axis):
        w, nq, c0, nc = jobs[i]
        ref = quarter(w, d ^ (2 * (k + 1)), p, nq, c0, nc)
        return copy(ref, ref, ps.at[i, k, axis], pr.at[i, k, axis], (1 + axis, 0))

    def DG(i, k, axis):
        w, nq, c0, nc = jobs[i]
        h = nc // 2
        ref = quarter(w, d ^ (2 * (k + 1)), p ^ (2 - axis), nq, c0 + axis * h, h)
        return copy(ref, ref, ps.at[i, k, 2 + axis], pr.at[i, k, 2 + axis], (1 + axis, 0))

    def S(i, k):
        w, nq, c0, nc = jobs[i]
        r = shards[w].shape[0]
        ref = fulls[w].at[pl.ds(pl.multiple_of((d ^ (2 * (k + 1))) * r, 16), r), pl.ds(c0, nc)]
        return copy(ref, ref, cs.at[i, k], cr.at[i, k], (0, 1))

    for i in range(min(AHEAD, J)):
        for k in range(3):
            Z(i, k).start()
    own = []
    for w in range(count):
        r = shards[w].shape[0]
        place = fulls[w].at[pl.ds(pl.multiple_of(d * r, 16), r)]
        pair = pltpu.make_async_copy(shards[w], place, ls.at[w]), copy(shards[w], place, os.at[w], orr.at[w], (0, 1))
        for c in pair:
            c.start()
        own.append(pair)
    targets[p] = target[...]
    named = [copy(target, targets.at[p], ts.at[m - 1], tr.at[m - 1], (m, 0)) for m in (1, 2, 3)]
    for c in named:
        c.start()
    section_mix(maps, taps, gain, mixed, rows, pad)

    ready = set()

    def ensure(w):
        if w not in ready:
            ready.add(w)
            own[w][0].wait()
            own[w][1].wait_recv()

    def expand_block(c0, nc):
        load = pltpu.make_async_copy(fulls[expand].at[:, pl.ds(c0, nc)], wide_w, ws.at[0])
        load.start()
        load.wait()

        def chunk(j, carry):
            here = pl.multiple_of(j * STEP, STEP)
            product(rows, wide_w, total, 0, here)
            stage[...] = total[...]
            active[:, pl.ds(c0 + here, STEP)] = jax.nn.gelu(total[...]).astype(jnp.bfloat16)
            out = pltpu.make_async_copy(stage, expanded.at[:, pl.ds(c0 + here, STEP)], es.at[0])
            out.start()
            out.wait()
            return carry

        lax.fori_loop(0, nc // STEP, chunk, 0)

    def reduce_block(c0, nc):
        load = pltpu.make_async_copy(fulls[reduce].at[:, pl.ds(c0, nc)], deep_w, ws.at[1])
        load.start()
        load.wait()
        cols = pl.ds(c0, nc)
        product(active, deep_w, total, 0, 0)
        reduced[:, cols] = total[...]
        side = maps.shape[0]

        def pool(h, carry):
            both = jnp.zeros((side, nc), jnp.float32)
            for r in range(2):
                row = 2 * h + r
                part = total[pl.ds(pl.multiple_of(row * side, 8), side), :]
                both += maps[row, :, cols].astype(jnp.float32) + scale[:, cols] * part
            half = side // 2
            for k in range(nc // LANES):
                pair_sum[k] = both[:, k * LANES : (k + 1) * LANES]
            for k in range(nc // LANES):
                even = pair_sum[k, pl.ds(0, half, stride=2), :]
                odd = pair_sum[k, pl.ds(1, half, stride=2), :]
                pooled[h, :, c0 + k * LANES : c0 + (k + 1) * LANES] = (even + odd) * 0.25
            return carry

        lax.fori_loop(0, side // 2, pool, 0)

    parts = maps.shape[2] // 4

    def hop(src, dst, ss, rs):
        return [copy(src.at[p ^ m], dst.at[p], ss.at[m - 1], rs.at[m - 1], (m, 0)) for m in (1, 2, 3)]

    def route_one():
        for k in range(4):
            leaving[k] = pooled[..., k * parts : (k + 1) * parts].reshape(leaving.shape[1:]).astype(jnp.bfloat16)
        met[p] = leaving[p]
        sent = hop(leaving, met, fs, fr)
        for c in sent:
            c.start()
        return sent

    def route_two(sent):
        for c in sent + named:
            c.wait()
        for k in range(4):
            chosen = jnp.zeros(met.shape[1:], jnp.float32)
            for q in range(4):
                here = targets[q, :1, :1] == k
                chosen += jnp.where(here, met[q].astype(jnp.float32), 0.0)
            sorted_maps[k] = chosen.astype(jnp.bfloat16)
        landing[p] = sorted_maps[p]
        sent = hop(sorted_maps, landing, gs, gr)
        for c in sent:
            c.start()
        return sent

    def route_three(sent):
        for c in sent:
            c.wait()
        for k in range(4):
            features[:, k * parts : (k + 1) * parts] = landing[k]

    last_reduce = max(i for i in range(J) if jobs[i][0] == reduce)
    routed = None
    for i in range(J + 3):
        if i < J:
            for k in range(3):
                Z(i, k).wait_recv()
                XY(i, k, 0).start()
                XY(i, k, 1).start()
            if i + AHEAD < J:
                for k in range(3):
                    Z(i + AHEAD, k).start()
        if 0 <= i - 1 < J:
            for k in range(3):
                XY(i - 1, k, 0).wait_recv()
                DG(i - 1, k, 1).start()
                XY(i - 1, k, 1).wait_recv()
                DG(i - 1, k, 0).start()
        if 0 <= i - 2 < J:
            for k in range(3):
                DG(i - 2, k, 0).wait_recv()
                DG(i - 2, k, 1).wait_recv()
                S(i - 2, k).start()
        if 0 <= i - 3 < J:
            for k in range(3):
                S(i - 3, k).wait_recv()
            w, _, c0, nc = jobs[i - 3]
            ensure(w)
            if w == expand:
                expand_block(c0, nc)
            if w == reduce:
                reduce_block(c0, nc)
            if i - 3 == last_reduce:
                routed = route_one()
            if i - 3 == last_reduce + 1:
                routed = route_two(routed)
            if i - 3 == last_reduce + 2:
                route_three(routed)
    for w in range(count):
        ensure(w)
        own[w][1].wait_send()
    for i in range(J):
        for k in range(3):
            Z(i, k).wait_send()
            S(i, k).wait_send()
            for a in range(2):
                XY(i, k, a).wait_send()
                DG(i, k, a).wait_send()


AHEAD = 3
GATHER_ORDER = (4, 0, 1, 5, 6, 3, 2)


def gather_weights(shards, maps, taps, gain, scale, target, expand, reduce):
    shapes = [s.shape for s in shards]
    jobs = gather_jobs(shapes)
    n, J = len(shards), len(jobs)
    side, _, channels = maps.shape
    cells, hidden = side * side, shapes[expand][1]
    wide = max(nc for w, _, _, nc in jobs if w == expand)
    low, full = jnp.bfloat16, jnp.float32
    anyspec, whole = pl.BlockSpec(memory_space=pl.ANY), pl.BlockSpec(memory_space=VMEM)
    dma = pltpu.SemaphoreType.DMA
    shape = jax.ShapeDtypeStruct
    results = pl.pallas_call(
        functools.partial(gather_kernel, jobs, n, expand, reduce),
        out_shape=[shape((8 * r, c), low) for r, c in shapes]
        + [
            shape(maps.shape, full),
            shape((cells, channels), low),
            shape((4, 8, LANES), jnp.int32),
            shape((cells, hidden), full),
            shape((cells, hidden), low),
            shape((cells, channels), full),
            shape((cells // 4, channels), low),
        ],
        in_specs=[anyspec] * n + [whole] * 5,
        out_specs=[anyspec] * n + [whole] * 3 + [anyspec] + [whole] * 3,
        scratch_shapes=[
            VMEM((side + 2 * REACH, side + 2 * EDGE, LANES), full),
            VMEM((channels, wide), low),
            VMEM((hidden, STEP), low),
            VMEM((cells, STEP), full),
            VMEM((cells, STEP), full),
            VMEM((STEP // LANES, side, LANES), full),
            VMEM((side // 2, side // 2, channels), full),
            VMEM((4, cells // 4, channels // 4), low),
            VMEM((4, cells // 4, channels // 4), low),
            VMEM((4, cells // 4, channels // 4), low),
            VMEM((4, cells // 4, channels // 4), low),
        ]
        + [dma((J, 3)), dma((J, 3)), dma((J, 3, 4)), dma((J, 3, 4)), dma((J, 3)), dma((J, 3))]
        + [dma((n,)), dma((n,)), dma((n,)), dma((3,)), dma((3,)), dma((2,)), dma((1,))] + [dma((3,))] * 4,
        compiler_params=pltpu.CompilerParams(
            collective_id=0, has_side_effects=True, vmem_limit_bytes=60 * 2**20
        ),
    )(
        *shards, maps, taps, gain.reshape(1, channels), scale.reshape(1, channels),
        jnp.broadcast_to(target, (8, LANES)),
    )
    rest = results[n:]
    return results[:n], rest[0], rest[1], rest[2][:, 0, 0], rest[3], rest[4], rest[5], rest[6]


def add_block(total, term):
    return (total.astype(jnp.float32) + term.astype(jnp.float32)).astype(jnp.bfloat16)


def scatter_kernel(
    big0, big1, land0a, land0b, land0c, land0d, t0, t1, t2, t3, small_in, grad_normed, mixed, maps, taps, gain,
    grad_maps, small_out, o0, o1, o2, o3, o4, o5, land1a, land1b,
    acc0a, acc0b, acc1a, acc1b, two0a, two0b, two1a, two1b, tmp0, tmp1,
    own0, own1, own2, own3, two0, two1, two2, two3,
    zr0, zr1, zr2, zr3, zr4, zr5, low0, low1, low2, low3, low4, low5,
    full0, full1, full2, full3, full4, full5,
    small_at, small_from, pad, grad_pad, tap_sums, ssem, rsem, lsem,
):
    p, d = lax.axis_index("path"), lax.axis_index("dev")
    up, across, height, side = p // 2, lax.rem(p, 2), d // 2, lax.rem(d, 2)
    masks = [(0, 1), (0, 2), (0, 4), (0, 6), (1, 0), (2, 0), (3, 0)]
    bar = pltpu.get_barrier_semaphore()
    for m in masks:
        pl.semaphore_signal(bar, inc=1, device_id=(p ^ m[0], d ^ m[1]), device_id_type=MESH)
    pl.semaphore_wait(bar, len(masks))

    copies = []

    def send(src, dst, m):
        n = len(copies)
        copy = pltpu.make_async_remote_copy(
            src, dst, ssem.at[n], rsem.at[n], device_id=(p ^ m[0], d ^ m[1]), device_id_type=MESH
        )
        copies.append(copy)
        copy.start()
        return copy

    local = []

    def fetch(src, dst):
        copy = pltpu.make_async_copy(src, dst, lsem.at[len(local)])
        local.append(copy)
        copy.start()
        return copy

    thin = [(t0, own0, two0, True), (t1, own1, two1, False), (t2, own2, two2, True), (t3, own3, two3, False)]
    wide = [
        (big0, (acc0a, acc0b), ((land0a, land0b), (land0c, land0d)), (two0a, two0b), tmp0),
        (big1, (acc1a, acc1b), ((land1a,), (land1b,)), (two1a, two1b), tmp1),
    ]
    outs = [o0, o1, o2, o3, o4, o5]
    zrs, lows, wholes = [zr0, zr1, zr2, zr3, zr4, zr5], [low0, low1, low2, low3, low4, low5], [full0, full1, full2, full3, full4, full5]

    def thin_two(i):
        src, own, two, upward = thin[i]
        index, mask = (up, (2, 0)) if upward else (across, (1, 0))
        loaded = fetch(src.at[:, :, index], own)
        return loaded, send(src.at[:, :, 1 - index], two, mask)

    def wide_one(w, ours):
        src, acc, land, _, _ = wide[w]
        half = src.shape[5] // 2
        a, b = pl.ds(0, half), pl.ds(half, half)
        loaded = [fetch(src.at[:, :, :, across, :, a], acc[0]), fetch(src.at[:, :, up, :, :, b], acc[1])]
        if not ours:
            return loaded
        return loaded + [
            send(src.at[:, :, :, 1 - across, :, a], land[0][0], (1, 0)),
            send(src.at[:, :, 1 - up, :, :, b], land[1][0], (2, 0)),
        ]

    def wide_two(w, started):
        src, acc, land, two, tmp = wide[w]
        started[0].wait()
        started[1].wait()
        sent = []
        for copy in started[2:]:
            copy.wait_recv()
        for k in range(2):
            each = 4 // len(land[k])
            loads = [fetch(land[k][0].at[0], tmp.at[0])]
            for z in range(4):
                if z < 3:
                    loads.append(fetch(land[k][(z + 1) // each].at[(z + 1) % each], tmp.at[(z + 1) % 2]))
                loads[z].wait()
                for c in range(2):
                    for q in range(2):
                        acc[k][z, c, q] = add_block(acc[k][z, c, q], tmp[z % 2, c, q])
            index, mask = (up, (2, 0)) if k == 0 else (across, (1, 0))
            sent.append(send(acc[k].at[:, :, 1 - index], two[k], mask))
        return sent

    def heights(n, parts, k):
        zr = zrs[n]
        half = zr.shape[3] // len(parts)
        return [
            send(parts[k].at[height ^ m], zr.at[m - 1, :, :, pl.ds(k * half, half)], (0, 2 * m)) for m in (1, 2, 3)
        ]

    def thin_three(i, started):
        _, own, two, _ = thin[i]
        started[0].wait()
        started[1].wait_recv()
        for z in range(4):
            for c in range(2):
                two[z, c] = add_block(two[z, c], own[z, c])
        return heights(i, [two], 0)

    def wide_three(w, sent):
        _, acc, _, two, _ = wide[w]
        for k in range(2):
            index = up if k == 0 else across
            sent[k].wait_recv()
            for z in range(4):
                for c in range(2):
                    two[k][z, c] = add_block(two[k][z, c], acc[k][z, c, index])
        return heights(4 + w, two, 0)

    def total(n, parts, k, sent):
        for copy in sent:
            copy.wait_recv()
        zr, low, whole = zrs[n], lows[n], wholes[n]
        size = zr.shape[3]
        half = size // len(parts)
        cols = slice(k * half, (k + 1) * half)
        for c in range(2):
            value = parts[k][height, c].astype(jnp.float32)
            for m in range(3):
                value = value + zr[m, c, :, cols].astype(jnp.float32)
            low[c, :, cols] = value.astype(jnp.bfloat16)
        place = (slice(None), pl.ds(pl.multiple_of(side * size + k * half, LANES), half))
        whole[place] = low[side, :, cols]
        return send(low.at[1 - side, :, cols], whole.at[place], (0, 1))

    def spread(n, swapped):
        swapped.wait_recv()
        return [fetch(wholes[n], outs[n].at[p])] + [send(wholes[n], outs[n].at[p], (m, 0)) for m in (1, 2, 3)]

    def spread_part(n, k, swapped):
        swapped.wait_recv()
        size = zrs[n].shape[3]
        copies = []
        for c in range(2):
            cols = pl.ds(c * size + k * (size // 2), size // 2)
            src, dst = wholes[n].at[:, cols], outs[n].at[p, :, cols]
            copies += [fetch(src, dst)] + [send(src, dst, (m, 0)) for m in (1, 2, 3)]
        return copies

    side_cells, _, channels = maps.shape
    count = channels // LANES

    def norm_back():
        clear_edges(pad, side_cells)
        clear_edges(grad_pad, side_cells)
        small_at[0] = small_in[...]

        def norm(h, carry):
            v = mixed[h]
            centred = v - jnp.mean(v, axis=-1, keepdims=True)
            scale = lax.rsqrt(jnp.mean(centred * centred, axis=-1, keepdims=True) + 1e-06)
            unit = centred * scale
            grad = grad_normed[h]
            small_at[0, SIDE * SIDE : SIDE * SIDE + 1, :] += jnp.sum(grad * unit, axis=0, keepdims=True)
            grad = grad * gain[...]
            grad_maps[h] = scale * (
                grad - jnp.mean(grad, axis=-1, keepdims=True) - unit * jnp.mean(grad * unit, axis=-1, keepdims=True)
            )
            return carry

        lax.fori_loop(0, side_cells, norm, 0)

    def blocks(first, last):
        def one(block, carry):
            at = lane_block(block)
            inside = (slice(REACH, REACH + side_cells), slice(EDGE, EDGE + side_cells), slice(None))
            pad[inside] = maps[:, :, at].astype(jnp.float32)
            grad_pad[inside] = grad_maps[:, :, at]
            tap_sums[...] = jnp.zeros_like(tap_sums)

            def rows(group, inner):
                base = group * GROUP
                sums = conv_rows(grad_pad, lambda t: taps[pl.ds(t, 1), at], group, True, side_cells)
                for r in range(GROUP):
                    grad_maps[base + r, :, at] = sums[r]
                for dc in range(SIDE):
                    grads = [grad_pad[base + REACH + r, EDGE : EDGE + side_cells, :] for r in range(GROUP)]
                    acc = [None] * SIDE
                    for j in range(GROUP + SIDE - 1):
                        row = pad[base + j, EDGE - REACH + dc : EDGE - REACH + dc + side_cells, :]
                        for r in range(GROUP):
                            dr = j - r
                            if 0 <= dr < SIDE:
                                term = row * grads[r]
                                acc[dr] = term if acc[dr] is None else acc[dr] + term
                    for dr in range(SIDE):
                        tap_sums[dr * SIDE + dc] += jnp.sum(acc[dr].reshape(side_cells // 8, 8, LANES), axis=0)
                return inner

            lax.fori_loop(0, side_cells // GROUP, rows, 0)
            small_at[0, : SIDE * SIDE, at] = jnp.sum(tap_sums[...], axis=1)
            return carry

        lax.fori_loop(first, last, one, 0)

    small_masks = [(0, 1), (1, 0), (2, 0), (0, 2), (0, 4)]

    def small_send(s):
        return send(small_at.at[s], small_from.at[s], small_masks[s])

    def small_step(s, copy):
        copy.wait_recv()
        value = small_at[s] + small_from[s]
        if s + 1 < len(small_masks):
            small_at[s + 1] = value
            return small_send(s + 1)
        small_out[...] = value

    thin_sent = [thin_two(i) for i in range(4)]
    one_reduce = wide_one(0, False)
    norm_back()
    blocks(0, count // 6)
    two_reduce = wide_two(0, one_reduce)
    blocks(count // 6, count // 3)
    thin_high = [thin_three(i, thin_sent[i]) for i in range(4)]
    one_expand = wide_one(1, True)
    blocks(count // 3, count // 2)
    high_reduce = wide_three(0, two_reduce)
    high_reduce += heights(4, wide[0][3], 1)
    blocks(count // 2, count)
    small = small_send(0)
    two_expand = wide_two(1, one_expand)
    small = small_step(0, small)
    swaps = [total(i, [thin[i][2]], 0, thin_high[i]) for i in range(4)]
    small = small_step(1, small)
    high_expand = wide_three(1, two_expand)
    last = [spread(i, swaps[i]) for i in range(4)]
    small = small_step(2, small)
    for copy in high_reduce:
        copy.wait_recv()
    swap_reduce = [total(4, wide[0][3], k, []) for k in range(2)]
    swap_reduce[0].wait_recv()
    last.append(spread(4, swap_reduce[1]))
    small = small_step(3, small)
    swap_low = total(5, wide[1][3], 0, high_expand)
    high_expand = heights(5, wide[1][3], 1)
    last.append(spread_part(5, 0, swap_low))
    small = small_step(4, small)
    swap_high = total(5, wide[1][3], 1, high_expand)
    last.append(spread_part(5, 1, swap_high))
    for group in last:
        for k, copy in enumerate(group):
            if k % 4:
                copy.wait_recv()
            else:
                copy.wait()
    for copy in copies:
        copy.wait_send()


def scatter_gradients(part_reduce, part_expand, landed, thins, small, grad_normed, mixed, maps, taps, gain):
    side, _, channels = maps.shape
    low, full = jnp.bfloat16, jnp.float32
    anyspec, whole = pl.BlockSpec(memory_space=pl.ANY), pl.BlockSpec(memory_space=VMEM)
    dma = pltpu.SemaphoreType.DMA
    finals = [(t.shape[3], t.shape[4]) for t in thins] + [w.shape[4:] for w in (part_reduce, part_expand)]
    scratch = []
    for w in (part_reduce, part_expand):
        shape = w.shape[:3] + (w.shape[4], w.shape[5] // 2)
        landing = [jax.ShapeDtypeStruct(shape, low)] * 2
        scratch += [VMEM(shape, low)] * 2
    scratch += [VMEM(w.shape[:2] + (w.shape[4], w.shape[5] // 2), low) for w in (part_reduce, part_expand) for _ in range(2)]
    scratch += [VMEM((2, 2, 2, w.shape[4], w.shape[5] // 2), low) for w in (part_reduce, part_expand)]
    scratch += [VMEM(t.shape[:2] + t.shape[3:], low) for t in thins] * 2
    scratch += [VMEM((3, 2) + f, low) for f in finals]
    scratch += [VMEM((2,) + f, low) for f in finals]
    scratch += [VMEM((f[0], 2 * f[1]), low) for f in finals]
    edge = (side + 2 * REACH, side + 2 * EDGE, LANES)
    scratch += [VMEM((5,) + small.shape, full)] * 2
    scratch += [VMEM(edge, full)] * 2 + [VMEM((SIDE * SIDE, 8, LANES), full)]
    scratch += [dma((80,)), dma((80,)), dma((40,))]
    results = pl.pallas_call(
        scatter_kernel,
        out_shape=[jax.ShapeDtypeStruct(maps.shape, full), jax.ShapeDtypeStruct(small.shape, full)]
        + [jax.ShapeDtypeStruct((4, f[0], 2 * f[1]), low) for f in finals]
        + landing,
        in_specs=[anyspec] * 10 + [whole] * 6,
        out_specs=[whole] * 2 + [anyspec] * 8,
        scratch_shapes=scratch,
        compiler_params=pltpu.CompilerParams(
            collective_id=1, has_side_effects=True, vmem_limit_bytes=60 * 2**20
        ),
    )(part_reduce, part_expand, *landed, *thins, small, grad_normed, mixed, maps, taps, gain.reshape(1, channels))
    return results[0], results[1], results[2:8]


def layer_norm(values, gain_vec):
    centred = values - jnp.mean(values, axis=-1, keepdims=True)
    spread = jnp.mean(centred * centred, axis=-1, keepdims=True)
    return centred * lax.rsqrt(spread + 1e-06) * gain_vec


def depthwise(feature_map, taps_table, kernel_side):
    half_side = kernel_side // 2
    padded = jnp.pad(feature_map, ((0, 0), (half_side, half_side), (half_side, half_side), (0, 0)))
    map_side = feature_map.shape[1]
    accum_sum = jnp.zeros(feature_map.shape, feature_map.dtype)
    for offset_row in range(kernel_side):
        for offset_col in range(kernel_side):
            window = padded[
                :, offset_row : offset_row + map_side, offset_col : offset_col + map_side, :
            ]
            accum_sum = accum_sum + window * taps_table[offset_row * kernel_side + offset_col]
    return accum_sum


def section_depthwise(grid_field, grid_kernel):
    return depthwise(grid_field, grid_kernel, 7)


def adapter_depthwise(grid_field, grid_kernel):
    return depthwise(grid_field, grid_kernel, 3)


def swap(value, axis, mask):
    size = lax.axis_size(axis)
    return lax.ppermute(value, axis, [(i, i ^ mask) for i in range(size)])


def pick(value, index, axis):
    return lax.dynamic_index_in_dim(value, index, axis, keepdims=False)


def add_low(left, right):
    return (left.astype(jnp.float32) + right.astype(jnp.float32)).astype(jnp.bfloat16)


def place():
    path, dev = lax.axis_index("path"), lax.axis_index("dev")
    return path, path // 2, lax.rem(path, 2), dev // 2, lax.rem(dev, 2)


def both_images(rows):
    return jnp.concatenate([rows, swap(rows, "dev", 1)])


def pair_halves(grads):
    side = place()[4]
    half = grads.shape[1] // 2
    low, high = grads[:, :half], grads[:, half:]
    theirs = swap(jnp.where(side == 0, high, low), "dev", 1)
    return jnp.concatenate([jnp.where(side == 0, low, high), theirs])


def pair_product(rows, grads):
    result = lax.dot_general(rows, grads, (((0,), (0,)), ((), ())), preferred_element_type=jnp.float32)
    return result.astype(jnp.bfloat16).reshape(4, 2, 2, 2, rows.shape[1] // 32, grads.shape[1])


def pair_gradient(rows, grads):
    return pair_product(rows, pair_halves(grads))


def across_half(share, axis):
    return swap(pick(share, 1 - place()[2], axis), "path", 1)


def up_half(share, axis):
    return swap(pick(share, 1 - place()[1], axis), "path", 2)


def across_sum(share, axis, other):
    return add_low(pick(share, place()[2], axis), other)


def up_sum(share, axis, other):
    return add_low(pick(share, place()[1], axis), other)


def tie(*values):
    return lax.optimization_barrier(values)


def finish(pieces):
    return pieces.reshape(-1, pieces.shape[2]).astype(jnp.float32)


def plain_sum(rows, grads):
    product = lax.dot_general(
        rows, grads, (((0,), (0,)), ((), ())), preferred_element_type=jnp.float32
    ).astype(jnp.bfloat16)
    share = lax.psum_scatter(product, "dev", scatter_dimension=0, tiled=True)
    return lax.psum(share, "path").astype(jnp.float32)


def local(
    inputs,
    hires_maps,
    target_path,
    cotangent,
    attn_gain,
    w_qkv,
    w_out,
    mlp_gain,
    w_fc1,
    w_fc2,
    w_adapter,
    adapter_kernel,
    merge_gate,
    section_kernel,
    section_gain,
    w_expand,
    w_reduce,
    layer_scale,
):
    tuned = lax.axis_size("path") == 4 and lax.axis_size("dev") == 8
    weights = (w_expand, w_reduce, w_adapter, w_qkv, w_out, w_fc1, w_fc2)
    if tuned:
        ordered, section_mixed, section_rows, spread_targets, expanded, activated_low, reduced, features = gather_weights(
            [weights[i] for i in GATHER_ORDER],
            hires_maps[0],
            section_kernel,
            section_gain,
            layer_scale,
            target_path,
            GATHER_ORDER.index(0),
            GATHER_ORDER.index(1),
        )
        fulls = [ordered[GATHER_ORDER.index(i)] for i in range(len(weights))]
    else:
        fulls = [lax.all_gather(shard, "dev", axis=0, tiled=True) for shard in weights]
    full_expand, full_reduce, full_adapter, full_qkv, full_out, full_fc1, full_fc2 = fulls
    path_count = lax.axis_size("path")
    maps_float = hires_maps.astype(jnp.float32)
    map_side = maps_float.shape[1]
    channels = maps_float.shape[3]
    grid_side = map_side // 2
    tokens = grid_side * grid_side
    quarter_rows = tokens // path_count
    model_width = inputs.shape[2]
    head_count = model_width // HEAD_DIM
    score_scale = HEAD_DIM ** (-0.5)
    if not tuned:
        section_mixed, section_back = jax.vjp(section_depthwise, maps_float, section_kernel)
        section_normed, section_norm_back = jax.vjp(layer_norm, section_mixed, section_gain)
    if tuned:
        _, section_gelu_back = jax.vjp(jax.nn.gelu, expanded)
        reduced = reduced.reshape(maps_float.shape)
    else:
        section_rows = section_normed.reshape(-1, channels).astype(jnp.bfloat16)
        expanded = jnp.dot(section_rows, full_expand, preferred_element_type=jnp.float32)
        activated, section_gelu_back = jax.vjp(jax.nn.gelu, expanded)
        activated_low = activated.astype(jnp.bfloat16)
        reduced = jnp.dot(activated_low, full_reduce, preferred_element_type=jnp.float32).reshape(
            maps_float.shape
        )
        section_out = maps_float + layer_scale * reduced
        pooled = jnp.mean(
            section_out.reshape(grid_side, 2, grid_side, 2, channels), axis=(1, 3)
        ).reshape(tokens, channels)
    if not tuned:
        pieces = pooled.astype(jnp.bfloat16).reshape(path_count, quarter_rows, channels)
        own_target = jnp.broadcast_to(target_path, (path_count, 1))
        spread_pieces = lax.all_to_all(pieces, "path", split_axis=0, concat_axis=0, tiled=True)
        spread_targets = lax.all_to_all(own_target, "path", split_axis=0, concat_axis=0, tiled=True)
    selector = (
        jnp.arange(path_count, dtype=jnp.int32)[:, None] == spread_targets.reshape(1, path_count)
    ).astype(jnp.float32)
    if not tuned:
        routed = jnp.einsum("pq,qtc->ptc", selector, spread_pieces.astype(jnp.float32)).astype(jnp.bfloat16)
        arrived = lax.all_to_all(routed, "path", split_axis=0, concat_axis=0, tiled=True)
        features = arrived.reshape(tokens, channels)
    adapted = jnp.dot(features, full_adapter, preferred_element_type=jnp.float32)
    spread_map, adapter_back = jax.vjp(
        adapter_depthwise, adapted.reshape(1, grid_side, grid_side, model_width), adapter_kernel
    )
    spread_rows = spread_map.reshape(tokens, model_width)
    gate_factor = jnp.tanh(merge_gate)
    hidden_in = inputs[0].astype(jnp.float32) + gate_factor * spread_rows
    normed_one, norm_one_back = jax.vjp(layer_norm, hidden_in, attn_gain)
    attn_rows = normed_one.astype(jnp.bfloat16)
    projected = jnp.dot(attn_rows, full_qkv, preferred_element_type=jnp.float32).astype(
        jnp.bfloat16
    )
    queries = projected[:, :model_width].reshape(tokens, head_count, HEAD_DIM)
    key_rows = projected[:, model_width : 2 * model_width].reshape(tokens, head_count, HEAD_DIM)
    values = projected[:, 2 * model_width :].reshape(tokens, head_count, HEAD_DIM)
    scores = (
        jnp.einsum("thd,shd->hts", queries, key_rows, preferred_element_type=jnp.float32)
        * score_scale
    )
    probs = jax.nn.softmax(scores, axis=-1)
    probs_low = probs.astype(jnp.bfloat16)
    attn_mixed = jnp.einsum("hts,shd->thd", probs_low, values, preferred_element_type=jnp.float32)
    attn_mixed = attn_mixed.astype(jnp.bfloat16).reshape(tokens, model_width)
    attended = jnp.dot(attn_mixed, full_out, preferred_element_type=jnp.float32)
    hidden_mid = hidden_in + attended
    normed_two, norm_two_back = jax.vjp(layer_norm, hidden_mid, mlp_gain)
    mlp_rows = normed_two.astype(jnp.bfloat16)
    raised = jnp.dot(mlp_rows, full_fc1, preferred_element_type=jnp.float32)
    lifted_value, gelu_back = jax.vjp(jax.nn.gelu, raised)
    lifted = lifted_value.astype(jnp.bfloat16)
    lowered = jnp.dot(lifted, full_fc2, preferred_element_type=jnp.float32)
    result = (hidden_mid + lowered)[None].astype(jnp.bfloat16)
    grad_out = cotangent[0].astype(jnp.float32)
    grad_out_low = grad_out.astype(jnp.bfloat16)
    if tuned:
        part_fc2 = pair_gradient(both_images(lifted), grad_out_low)
    else:
        grad_fc2_w = plain_sum(lifted, grad_out_low)
    grad_lifted = jnp.dot(grad_out_low, full_fc2.T, preferred_element_type=jnp.float32)
    grad_raised = gelu_back(grad_lifted)[0].astype(jnp.bfloat16)
    if tuned:
        part_fc1 = pair_gradient(both_images(mlp_rows), grad_raised)
    else:
        grad_fc1_w = plain_sum(mlp_rows, grad_raised)
    grad_normed_two = jnp.dot(grad_raised, full_fc1.T, preferred_element_type=jnp.float32)
    grad_mid_norm, grad_mlp_gain = norm_two_back(grad_normed_two)
    grad_mid = grad_out + grad_mid_norm
    grad_attended = grad_mid.astype(jnp.bfloat16)
    if tuned:
        part_out = pair_gradient(both_images(attn_mixed), grad_attended)
    else:
        grad_out_w = plain_sum(attn_mixed, grad_attended)
    grad_mixed = jnp.dot(grad_attended, full_out.T, preferred_element_type=jnp.float32)
    grad_mixed = grad_mixed.astype(jnp.bfloat16).reshape(tokens, head_count, HEAD_DIM)
    grad_probs = jnp.einsum("thd,shd->hts", grad_mixed, values, preferred_element_type=jnp.float32)
    grad_values = jnp.einsum(
        "hts,thd->shd", probs_low, grad_mixed, preferred_element_type=jnp.float32
    )
    grad_scores = probs * (grad_probs - jnp.sum(grad_probs * probs, axis=-1, keepdims=True))
    grad_scores = grad_scores.astype(jnp.bfloat16)
    grad_queries = (
        jnp.einsum("hts,shd->thd", grad_scores, key_rows, preferred_element_type=jnp.float32)
        * score_scale
    )
    grad_keys = (
        jnp.einsum("hts,thd->shd", grad_scores, queries, preferred_element_type=jnp.float32)
        * score_scale
    )
    grad_projected = jnp.concatenate(
        [
            grad_queries.reshape(tokens, model_width),
            grad_keys.reshape(tokens, model_width),
            grad_values.reshape(tokens, model_width),
        ],
        axis=1,
    ).astype(jnp.bfloat16)
    if tuned:
        part_qkv = pair_gradient(both_images(attn_rows), grad_projected)
    else:
        grad_qkv_w = plain_sum(attn_rows, grad_projected)
    grad_normed_one = jnp.dot(grad_projected, full_qkv.T, preferred_element_type=jnp.float32)
    grad_in_norm, grad_attn_gain = norm_one_back(grad_normed_one)
    grad_in = grad_mid + grad_in_norm
    grad_merge = jnp.sum(grad_in * spread_rows, axis=0) * (1.0 - gate_factor * gate_factor)
    grad_spread = (grad_in * gate_factor).reshape(1, grid_side, grid_side, model_width)
    grad_adapted, grad_adapter_taps = adapter_back(grad_spread)
    grad_adapted_low = grad_adapted.reshape(tokens, model_width).astype(jnp.bfloat16)
    if tuned:
        part_adapter = pair_gradient(both_images(features), grad_adapted_low)
    else:
        grad_adapter_w = plain_sum(features, grad_adapted_low)
    grad_features = jnp.dot(grad_adapted_low, full_adapter.T, preferred_element_type=jnp.float32)
    if tuned:
        grad_features, part_fc2, part_fc1 = tie(grad_features, part_fc2, part_fc1)
    grad_pieces = grad_features.astype(jnp.bfloat16).reshape(path_count, quarter_rows, channels)
    grad_routed = lax.all_to_all(grad_pieces, "path", split_axis=0, concat_axis=0, tiled=True)
    grad_unrouted = jnp.einsum("pq,ptc->qtc", selector, grad_routed.astype(jnp.float32)).astype(
        jnp.bfloat16
    )
    grad_home = lax.all_to_all(grad_unrouted, "path", split_axis=0, concat_axis=0, tiled=True)
    if tuned:
        part_rest = jnp.concatenate([part_out, part_adapter], axis=4)
        grad_home, part_fc2, part_fc1, part_qkv, part_rest = tie(grad_home, part_fc2, part_fc1, part_qkv, part_rest)
        half_fc2, half_fc1 = across_half(part_fc2, 3), up_half(part_fc1, 2)
    grad_pooled = grad_home.astype(jnp.float32).reshape(tokens, channels)
    quarter = (grad_pooled * 0.25).reshape(1, grid_side, 1, grid_side, 1, channels)
    grad_section_out = jnp.broadcast_to(quarter, (1, grid_side, 2, grid_side, 2, channels)).reshape(
        maps_float.shape
    )
    grad_scale = jnp.sum((grad_section_out * reduced).reshape(-1, channels), axis=0)
    grad_reduced = (grad_section_out * layer_scale).reshape(-1, channels).astype(jnp.bfloat16)
    if tuned:
        part_reduce = pair_gradient(both_images(activated_low), grad_reduced)
        half_qkv, half_rest = across_half(part_qkv, 3), up_half(part_rest, 2)
        columns = part_reduce.shape[5] // 2
        leaving = [
            pick(part_reduce[first : first + 2, ..., :columns], 1 - place()[2], 3) for first in (0, 2)
        ] + [pick(part_reduce[first : first + 2, ..., columns:], 1 - place()[1], 2) for first in (0, 2)]
        grad_reduced, part_reduce, *leaving = tie(grad_reduced, part_reduce, *leaving)
        landed = [swap(piece, "path", 1 + k // 2) for k, piece in enumerate(leaving)]
    else:
        grad_reduce_w = plain_sum(activated_low, grad_reduced)
    grad_activated = jnp.dot(grad_reduced, full_reduce.T, preferred_element_type=jnp.float32)
    grad_expanded = section_gelu_back(grad_activated)[0].astype(jnp.bfloat16)
    if tuned:
        grad_expanded, half_fc2, half_fc1 = tie(grad_expanded, half_fc2, half_fc1)
    else:
        grad_expand_w = plain_sum(section_rows, grad_expanded)
    grad_section_normed = jnp.dot(
        grad_expanded, full_expand.T, preferred_element_type=jnp.float32
    ).reshape(maps_float.shape)
    if tuned:
        halves_expand = pair_halves(grad_expanded)
        grad_section_normed, halves_expand, half_qkv, half_rest, landed[0], landed[2] = tie(
            grad_section_normed, halves_expand, half_qkv, half_rest, landed[0], landed[2]
        )
        part_expand = pair_product(both_images(section_rows), halves_expand)
        step_fc2, step_fc1 = across_sum(part_fc2, 3, half_fc2), up_sum(part_fc1, 2, half_fc1)
        step_qkv, step_rest = across_sum(part_qkv, 3, half_qkv), up_sum(part_rest, 2, half_rest)
        small_rows = jnp.concatenate(
            [
                jnp.zeros((section_kernel.shape[0] + 1, channels), jnp.float32),
                jnp.concatenate([grad_attn_gain, grad_mlp_gain, grad_merge, grad_adapter_taps.reshape(-1)]).reshape(-1, channels),
                grad_scale[None],
            ]
        )
        small_count = small_rows.shape[0]
        small_rows = jnp.pad(small_rows, ((0, -small_count % 8), (0, 0)))
        grad_maps, small_rows, pieces = scatter_gradients(
            part_reduce,
            part_expand,
            landed,
            [step_fc2, step_fc1, step_qkv, step_rest],
            small_rows,
            grad_section_normed[0],
            section_mixed,
            hires_maps[0],
            section_kernel,
            section_gain,
        )
        grad_maps = grad_maps[None] + grad_section_out
        split = part_out.shape[4]
        grad_fc2_w, grad_fc1_w, grad_qkv_w = [finish(piece) for piece in pieces[:3]]
        grad_out_w, grad_adapter_w = finish(pieces[3][:, :split]), finish(pieces[3][:, split:])
        grad_reduce_w, grad_expand_w = finish(pieces[4]), finish(pieces[5])
    else:
        grad_section_mixed, grad_section_gain = section_norm_back(grad_section_normed)
        grad_maps_conv, grad_section_taps = section_back(grad_section_mixed)
        grad_maps = grad_section_out + grad_maps_conv
    summed = (
        grad_qkv_w,
        grad_out_w,
        grad_fc1_w,
        grad_fc2_w,
        grad_adapter_w,
        grad_expand_w,
        grad_reduce_w,
    )
    if tuned:
        tap_count = section_kernel.shape[0]
        flat = small_rows[tap_count + 1 : small_count - 1].reshape(-1)
        small_sums = (
            flat[:model_width],
            flat[model_width : 2 * model_width],
            flat[2 * model_width : 3 * model_width],
            flat[3 * model_width :].reshape(adapter_kernel.shape),
            small_rows[tap_count],
            small_rows[:tap_count],
            small_rows[small_count - 1],
        )
    else:
        small_sums = lax.psum(
            (
                grad_attn_gain,
                grad_mlp_gain,
                grad_merge,
                grad_adapter_taps,
                grad_section_gain,
                grad_section_taps,
                grad_scale,
            ),
            ("path", "dev"),
        )
    return (
        result,
        grad_in[None],
        grad_maps,
        small_sums[0],
        summed[0],
        summed[1],
        small_sums[1],
        summed[2],
        summed[3],
        summed[4],
        small_sums[3],
        small_sums[2],
        small_sums[5],
        small_sums[4],
        summed[5],
        summed[6],
        small_sums[6],
    )


def solution(mesh):
    return jax.shard_map(
        local,
        mesh=mesh,
        in_specs=(
            P(("path", "dev"), None, None),
            P(("path", "dev"), None, None, None),
            P("path", "dev"),
            P(("path", "dev"), None, None),
            P(),
            P("dev", None),
            P("dev", None),
            P(),
            P("dev", None),
            P("dev", None),
            P("dev", None),
            P(),
            P(),
            P(),
            P(),
            P("dev", None),
            P("dev", None),
            P(),
        ),
        out_specs=(
            P(("path", "dev"), None, None),
            P(("path", "dev"), None, None),
            P(("path", "dev"), None, None, None),
            P(),
            P("dev", None),
            P("dev", None),
            P(),
            P("dev", None),
            P("dev", None),
            P("dev", None),
            P(),
            P(),
            P(),
            P(),
            P("dev", None),
            P("dev", None),
            P(),
        ),
        check_vma=False,
    )
```

```python
import functools

import jax
import jax.numpy as jnp
from jax import lax
from jax.experimental import pallas as pl
from jax.experimental.pallas import tpu as pltpu
from jax.sharding import PartitionSpec as P

HEAD_DIM = 64
MESH = pl.DeviceIdType.MESH
VMEM = pltpu.VMEM
SIDE, REACH, EDGE, GROUP, LANES = 7, 3, 8, 8, 128


def conv_rows(src, taps, group, flip, side):
    base = group * GROUP
    sums = [None] * GROUP
    for dc in range(SIDE):
        col = [taps((SIDE - 1 - dr) * SIDE + SIDE - 1 - dc if flip else dr * SIDE + dc) for dr in range(SIDE)]
        for j in range(GROUP + SIDE - 1):
            row = src[base + j, EDGE - REACH + dc : EDGE - REACH + dc + side, :]
            for r in range(GROUP):
                if 0 <= j - r < SIDE:
                    term = row * col[j - r]
                    sums[r] = term if sums[r] is None else sums[r] + term
    return sums


def clear_edges(pad, side):
    rows, columns, lanes = pad.shape[-3:]
    pad[:, :EDGE, :] = jnp.zeros((rows, EDGE, lanes), jnp.float32)
    pad[:, EDGE + side :, :] = jnp.zeros((rows, columns - EDGE - side, lanes), jnp.float32)
    pad[:REACH] = jnp.zeros((REACH, columns, lanes), jnp.float32)
    pad[REACH + side :] = jnp.zeros((rows - REACH - side, columns, lanes), jnp.float32)


def lane_block(block):
    return pl.ds(pl.multiple_of(block * LANES, LANES), LANES)


def mix_block(block, maps, taps, mixed, pad):
    side = maps.shape[0]
    at = lane_block(block)
    pad[REACH : REACH + side, EDGE : EDGE + side, :] = maps[:, :, at].astype(jnp.float32)

    def rows(group, carry):
        sums = conv_rows(pad, lambda t: taps[pl.ds(t, 1), at], group, False, side)
        for r in range(GROUP):
            mixed[group * GROUP + r, :, at] = sums[r]
        return carry

    lax.fori_loop(0, side // GROUP, rows, 0)


def section_mix(maps, taps, gain, mixed, rows, pad):
    side, _, channels = maps.shape
    clear_edges(pad, side)

    def blocks(block, carry):
        mix_block(block, maps, taps, mixed, pad)
        return carry

    lax.fori_loop(0, channels // LANES, blocks, 0)

    def norm(pair, carry):
        v = mixed[pl.ds(2 * pair, 2)].reshape(2 * side, channels)
        centred = v - jnp.mean(v, axis=-1, keepdims=True)
        scale = lax.rsqrt(jnp.mean(centred * centred, axis=-1, keepdims=True) + 1e-06)
        at = pl.ds(pl.multiple_of(pair * 2 * side, 2 * side), 2 * side)
        rows[at, :] = (centred * scale * gain[...]).astype(jnp.bfloat16)
        return carry

    lax.fori_loop(0, side // 2, norm, 0)


STEP = 512


def product(left, right, total, left_at, right_at):
    total[...] = jnp.zeros_like(total)

    def step(k, carry):
        here = pl.multiple_of(k * STEP, STEP)
        total[...] += jnp.dot(
            left[:, pl.ds(left_at + here, STEP)],
            right[pl.ds(here, STEP), pl.ds(pl.multiple_of(right_at, STEP), STEP)],
            preferred_element_type=jnp.float32,
        )
        return carry

    lax.fori_loop(0, right.shape[0] // STEP, step, 0)


def gather_jobs(shapes):
    jobs = []
    for w, (r, n) in enumerate(shapes):
        parts = max(1, round(r // 4 * n / (16 * 6144)))
        while n % (parts * STEP):
            parts -= 1
        jobs += [(w, r // 4, k * (n // parts), n // parts) for k in range(parts)]
    return jobs


def gather_kernel(jobs, count, expand, reduce, *refs):
    shards = refs[:count]
    maps, taps, gain, scale, target = refs[count : count + 5]
    fulls = refs[count + 5 : 2 * count + 5]
    mixed, rows, targets, expanded, active, reduced, features = refs[2 * count + 5 : 2 * count + 12]
    pad, wide_w, deep_w, total, stage, pair_sum, pooled, leaving, met, sorted_maps, landing = refs[2 * count + 12 : 2 * count + 23]
    zs, zr, ps, pr, cs, cr, os, orr, ls, ts, tr, ws, es, fs, fr, gs, gr = refs[2 * count + 23 :]
    p, d = lax.axis_index("path"), lax.axis_index("dev")

    def at(m):
        return (p ^ m[0], d ^ m[1])

    masks = [(0, 1), (0, 2), (0, 4), (0, 6), (1, 0), (2, 0), (3, 0)]
    bar = pltpu.get_barrier_semaphore()
    for m in masks:
        pl.semaphore_signal(bar, inc=1, device_id=at(m), device_id_type=MESH)
    pl.semaphore_wait(bar, len(masks))

    def copy(src, dst, ss, rs, m):
        return pltpu.make_async_remote_copy(src, dst, ss, rs, device_id=at(m), device_id_type=MESH)

    def quarter(w, owner, q, nq, c0, nc):
        r = shards[w].shape[0]
        return fulls[w].at[pl.ds(pl.multiple_of(owner * r + q * nq, 16), nq), pl.ds(c0, nc)]

    J = len(jobs)

    def Z(i, k):
        w, nq, c0, nc = jobs[i]
        src = shards[w].at[pl.ds(pl.multiple_of(p * nq, 16), nq), pl.ds(c0, nc)]
        return copy(src, quarter(w, d, p, nq, c0, nc), zs.at[i, k], zr.at[i, k], (0, 2 * (k + 1)))

    def XY(i, k, axis):
        w, nq, c0, nc = jobs[i]
        ref = quarter(w, d ^ (2 * (k + 1)), p, nq, c0, nc)
        return copy(ref, ref, ps.at[i, k, axis], pr.at[i, k, axis], (1 + axis, 0))

    def DG(i, k, axis):
        w, nq, c0, nc = jobs[i]
        h = nc // 2
        ref = quarter(w, d ^ (2 * (k + 1)), p ^ (2 - axis), nq, c0 + axis * h, h)
        return copy(ref, ref, ps.at[i, k, 2 + axis], pr.at[i, k, 2 + axis], (1 + axis, 0))

    def S(i, k):
        w, nq, c0, nc = jobs[i]
        r = shards[w].shape[0]
        ref = fulls[w].at[pl.ds(pl.multiple_of((d ^ (2 * (k + 1))) * r, 16), r), pl.ds(c0, nc)]
        return copy(ref, ref, cs.at[i, k], cr.at[i, k], (0, 1))

    for i in range(min(AHEAD, J)):
        for k in range(3):
            Z(i, k).start()
    own = []
    for w in range(count):
        r = shards[w].shape[0]
        place = fulls[w].at[pl.ds(pl.multiple_of(d * r, 16), r)]
        pair = pltpu.make_async_copy(shards[w], place, ls.at[w]), copy(shards[w], place, os.at[w], orr.at[w], (0, 1))
        for c in pair:
            c.start()
        own.append(pair)
    targets[p] = target[...]
    named = [copy(target, targets.at[p], ts.at[m - 1], tr.at[m - 1], (m, 0)) for m in (1, 2, 3)]
    for c in named:
        c.start()
    section_mix(maps, taps, gain, mixed, rows, pad)

    ready = set()

    def ensure(w):
        if w not in ready:
            ready.add(w)
            own[w][0].wait()
            own[w][1].wait_recv()

    def expand_block(c0, nc):
        load = pltpu.make_async_copy(fulls[expand].at[:, pl.ds(c0, nc)], wide_w, ws.at[0])
        load.start()
        load.wait()

        def chunk(j, carry):
            here = pl.multiple_of(j * STEP, STEP)
            product(rows, wide_w, total, 0, here)
            stage[...] = total[...]
            active[:, pl.ds(c0 + here, STEP)] = jax.nn.gelu(total[...]).astype(jnp.bfloat16)
            out = pltpu.make_async_copy(stage, expanded.at[:, pl.ds(c0 + here, STEP)], es.at[0])
            out.start()
            out.wait()
            return carry

        lax.fori_loop(0, nc // STEP, chunk, 0)

    def reduce_block(c0, nc):
        load = pltpu.make_async_copy(fulls[reduce].at[:, pl.ds(c0, nc)], deep_w, ws.at[1])
        load.start()
        load.wait()
        cols = pl.ds(c0, nc)
        product(active, deep_w, total, 0, 0)
        reduced[:, cols] = total[...]
        side = maps.shape[0]

        def pool(h, carry):
            both = jnp.zeros((side, nc), jnp.float32)
            for r in range(2):
                row = 2 * h + r
                part = total[pl.ds(pl.multiple_of(row * side, 8), side), :]
                both += maps[row, :, cols].astype(jnp.float32) + scale[:, cols] * part
            half = side // 2
            for k in range(nc // LANES):
                pair_sum[k] = both[:, k * LANES : (k + 1) * LANES]
            for k in range(nc // LANES):
                even = pair_sum[k, pl.ds(0, half, stride=2), :]
                odd = pair_sum[k, pl.ds(1, half, stride=2), :]
                pooled[h, :, c0 + k * LANES : c0 + (k + 1) * LANES] = (even + odd) * 0.25
            return carry

        lax.fori_loop(0, side // 2, pool, 0)

    parts = maps.shape[2] // 4

    def hop(src, dst, ss, rs):
        return [copy(src.at[p ^ m], dst.at[p], ss.at[m - 1], rs.at[m - 1], (m, 0)) for m in (1, 2, 3)]

    def route_one():
        for k in range(4):
            leaving[k] = pooled[..., k * parts : (k + 1) * parts].reshape(leaving.shape[1:]).astype(jnp.bfloat16)
        met[p] = leaving[p]
        sent = hop(leaving, met, fs, fr)
        for c in sent:
            c.start()
        return sent

    def route_two(sent):
        for c in sent + named:
            c.wait()
        for k in range(4):
            chosen = jnp.zeros(met.shape[1:], jnp.float32)
            for q in range(4):
                here = targets[q, :1, :1] == k
                chosen += jnp.where(here, met[q].astype(jnp.float32), 0.0)
            sorted_maps[k] = chosen.astype(jnp.bfloat16)
        landing[p] = sorted_maps[p]
        sent = hop(sorted_maps, landing, gs, gr)
        for c in sent:
            c.start()
        return sent

    def route_three(sent):
        for c in sent:
            c.wait()
        for k in range(4):
            features[:, k * parts : (k + 1) * parts] = landing[k]

    last_reduce = max(i for i in range(J) if jobs[i][0] == reduce)
    routed = None
    for i in range(J + 3):
        if i < J:
            for k in range(3):
                Z(i, k).wait_recv()
                XY(i, k, 0).start()
                XY(i, k, 1).start()
            if i + AHEAD < J:
                for k in range(3):
                    Z(i + AHEAD, k).start()
        if 0 <= i - 1 < J:
            for k in range(3):
                XY(i - 1, k, 0).wait_recv()
                DG(i - 1, k, 1).start()
                XY(i - 1, k, 1).wait_recv()
                DG(i - 1, k, 0).start()
        if 0 <= i - 2 < J:
            for k in range(3):
                DG(i - 2, k, 0).wait_recv()
                DG(i - 2, k, 1).wait_recv()
                S(i - 2, k).start()
        if 0 <= i - 3 < J:
            for k in range(3):
                S(i - 3, k).wait_recv()
            w, _, c0, nc = jobs[i - 3]
            ensure(w)
            if w == expand:
                expand_block(c0, nc)
            if w == reduce:
                reduce_block(c0, nc)
            if i - 3 == last_reduce:
                routed = route_one()
            if i - 3 == last_reduce + 1:
                routed = route_two(routed)
            if i - 3 == last_reduce + 2:
                route_three(routed)
    for w in range(count):
        ensure(w)
        own[w][1].wait_send()
    for i in range(J):
        for k in range(3):
            Z(i, k).wait_send()
            S(i, k).wait_send()
            for a in range(2):
                XY(i, k, a).wait_send()
                DG(i, k, a).wait_send()


AHEAD = 3
GATHER_ORDER = (4, 0, 1, 5, 6, 3, 2)


def gather_weights(shards, maps, taps, gain, scale, target, expand, reduce):
    shapes = [s.shape for s in shards]
    jobs = gather_jobs(shapes)
    n, J = len(shards), len(jobs)
    side, _, channels = maps.shape
    cells, hidden = side * side, shapes[expand][1]
    wide = max(nc for w, _, _, nc in jobs if w == expand)
    low, full = jnp.bfloat16, jnp.float32
    anyspec, whole = pl.BlockSpec(memory_space=pl.ANY), pl.BlockSpec(memory_space=VMEM)
    dma = pltpu.SemaphoreType.DMA
    shape = jax.ShapeDtypeStruct
    results = pl.pallas_call(
        functools.partial(gather_kernel, jobs, n, expand, reduce),
        out_shape=[shape((8 * r, c), low) for r, c in shapes]
        + [
            shape(maps.shape, full),
            shape((cells, channels), low),
            shape((4, 8, LANES), jnp.int32),
            shape((cells, hidden), full),
            shape((cells, hidden), low),
            shape((cells, channels), full),
            shape((cells // 4, channels), low),
        ],
        in_specs=[anyspec] * n + [whole] * 5,
        out_specs=[anyspec] * n + [whole] * 3 + [anyspec] + [whole] * 3,
        scratch_shapes=[
            VMEM((side + 2 * REACH, side + 2 * EDGE, LANES), full),
            VMEM((channels, wide), low),
            VMEM((hidden, STEP), low),
            VMEM((cells, STEP), full),
            VMEM((cells, STEP), full),
            VMEM((STEP // LANES, side, LANES), full),
            VMEM((side // 2, side // 2, channels), full),
            VMEM((4, cells // 4, channels // 4), low),
            VMEM((4, cells // 4, channels // 4), low),
            VMEM((4, cells // 4, channels // 4), low),
            VMEM((4, cells // 4, channels // 4), low),
        ]
        + [dma((J, 3)), dma((J, 3)), dma((J, 3, 4)), dma((J, 3, 4)), dma((J, 3)), dma((J, 3))]
        + [dma((n,)), dma((n,)), dma((n,)), dma((3,)), dma((3,)), dma((2,)), dma((1,))] + [dma((3,))] * 4,
        compiler_params=pltpu.CompilerParams(
            collective_id=0, has_side_effects=True, vmem_limit_bytes=60 * 2**20
        ),
    )(
        *shards, maps, taps, gain.reshape(1, channels), scale.reshape(1, channels),
        jnp.broadcast_to(target, (8, LANES)),
    )
    rest = results[n:]
    return results[:n], rest[0], rest[1], rest[2][:, 0, 0], rest[3], rest[4], rest[5], rest[6]


def add_block(total, term):
    return (total.astype(jnp.float32) + term.astype(jnp.float32)).astype(jnp.bfloat16)


def scatter_kernel(
    big0, big1, land0a, land0b, land0c, land0d, t0, t1, t2, t3, small_in, grad_normed, mixed, maps, taps, gain,
    grad_maps, small_out, o0, o1, o2, o3, o4, o5, land1a, land1b,
    acc0a, acc0b, acc1a, acc1b, two0a, two0b, two1a, two1b, tmp0, tmp1,
    own0, own1, own2, own3, two0, two1, two2, two3,
    zr0, zr1, zr2, zr3, zr4, zr5, low0, low1, low2, low3, low4, low5,
    full0, full1, full2, full3, full4, full5,
    small_at, small_from, pad, grad_pad, tap_sums, ssem, rsem, lsem,
):
    p, d = lax.axis_index("path"), lax.axis_index("dev")
    up, across, height, side = p // 2, lax.rem(p, 2), d // 2, lax.rem(d, 2)
    masks = [(0, 1), (0, 2), (0, 4), (0, 6), (1, 0), (2, 0), (3, 0)]
    bar = pltpu.get_barrier_semaphore()
    for m in masks:
        pl.semaphore_signal(bar, inc=1, device_id=(p ^ m[0], d ^ m[1]), device_id_type=MESH)
    pl.semaphore_wait(bar, len(masks))

    copies = []

    def send(src, dst, m):
        n = len(copies)
        copy = pltpu.make_async_remote_copy(
            src, dst, ssem.at[n], rsem.at[n], device_id=(p ^ m[0], d ^ m[1]), device_id_type=MESH
        )
        copies.append(copy)
        copy.start()
        return copy

    local = []

    def fetch(src, dst):
        copy = pltpu.make_async_copy(src, dst, lsem.at[len(local)])
        local.append(copy)
        copy.start()
        return copy

    thin = [(t0, own0, two0, True), (t1, own1, two1, False), (t2, own2, two2, True), (t3, own3, two3, False)]
    wide = [
        (big0, (acc0a, acc0b), ((land0a, land0b), (land0c, land0d)), (two0a, two0b), tmp0),
        (big1, (acc1a, acc1b), ((land1a,), (land1b,)), (two1a, two1b), tmp1),
    ]
    outs = [o0, o1, o2, o3, o4, o5]
    zrs, lows, wholes = [zr0, zr1, zr2, zr3, zr4, zr5], [low0, low1, low2, low3, low4, low5], [full0, full1, full2, full3, full4, full5]

    def thin_two(i):
        src, own, two, upward = thin[i]
        index, mask = (up, (2, 0)) if upward else (across, (1, 0))
        loaded = fetch(src.at[:, :, index], own)
        return loaded, send(src.at[:, :, 1 - index], two, mask)

    def wide_one(w, ours):
        src, acc, land, _, _ = wide[w]
        half = src.shape[5] // 2
        a, b = pl.ds(0, half), pl.ds(half, half)
        loaded = [fetch(src.at[:, :, :, across, :, a], acc[0]), fetch(src.at[:, :, up, :, :, b], acc[1])]
        if not ours:
            return loaded
        return loaded + [
            send(src.at[:, :, :, 1 - across, :, a], land[0][0], (1, 0)),
            send(src.at[:, :, 1 - up, :, :, b], land[1][0], (2, 0)),
        ]

    def wide_two(w, started):
        src, acc, land, two, tmp = wide[w]
        started[0].wait()
        started[1].wait()
        sent = []
        for copy in started[2:]:
            copy.wait_recv()
        for k in range(2):
            each = 4 // len(land[k])
            loads = [fetch(land[k][0].at[0], tmp.at[0])]
            for z in range(4):
                if z < 3:
                    loads.append(fetch(land[k][(z + 1) // each].at[(z + 1) % each], tmp.at[(z + 1) % 2]))
                loads[z].wait()
                for c in range(2):
                    for q in range(2):
                        acc[k][z, c, q] = add_block(acc[k][z, c, q], tmp[z % 2, c, q])
            index, mask = (up, (2, 0)) if k == 0 else (across, (1, 0))
            sent.append(send(acc[k].at[:, :, 1 - index], two[k], mask))
        return sent

    def columns_of(n, parts, k):
        half = zrs[n].shape[3] // len(parts)
        return pl.ds(k * half, half)

    def heights(n, parts, k):
        cols = columns_of(n, parts, k)
        return [send(parts[k].at[height ^ m], zrs[n].at[m // 2, :, :, cols], (0, 2)) for m in (1, 3)]

    def further(n, parts, k, sent):
        for copy in sent:
            copy.wait_recv()
        cols = columns_of(n, parts, k)
        for c in range(2):
            zrs[n][1, c, :, cols] = add_block(zrs[n][1, c, :, cols], parts[k][height ^ 2, c])
        return send(zrs[n].at[1, :, :, cols], zrs[n].at[2, :, :, cols], (0, 4))

    def thin_three(i, started):
        _, own, two, _ = thin[i]
        started[0].wait()
        started[1].wait_recv()
        for z in range(4):
            for c in range(2):
                two[z, c] = add_block(two[z, c], own[z, c])
        return heights(i, [two], 0)

    def wide_three(w, sent):
        _, acc, _, two, _ = wide[w]
        for k in range(2):
            index = up if k == 0 else across
            sent[k].wait_recv()
            for z in range(4):
                for c in range(2):
                    two[k][z, c] = add_block(two[k][z, c], acc[k][z, c, index])
        return heights(4 + w, two, 0)

    def total(n, parts, k, sent):
        sent.wait_recv()
        zr, low, whole = zrs[n], lows[n], wholes[n]
        size = zr.shape[3]
        half = size // len(parts)
        cols = slice(k * half, (k + 1) * half)
        for c in range(2):
            value = parts[k][height, c].astype(jnp.float32)
            for m in (0, 2):
                value = value + zr[m, c, :, cols].astype(jnp.float32)
            low[c, :, cols] = value.astype(jnp.bfloat16)
        place = (slice(None), pl.ds(pl.multiple_of(side * size + k * half, LANES), half))
        whole[place] = low[side, :, cols]
        return send(low.at[1 - side, :, cols], whole.at[place], (0, 1))

    def spread(n, swapped, first=0, parts=1):
        swapped.wait_recv()
        size = zrs[n].shape[3]
        group = []
        for c in range(2):
            cols = pl.ds(c * size + first * (size // parts), size // parts)
            src, dst = wholes[n].at[:, cols], outs[n].at[p, :, cols]
            group.append((n, cols, fetch(src, dst), send(src, dst, (1, 0)), send(src, dst, (2, 0))))
        return group

    def relay(group):
        sent = []
        for n, cols, _, along_x, along_y in group:
            half = cols.size // 2
            for k, (copy, other, mask) in enumerate(((along_x, 1, (2, 0)), (along_y, 2, (1, 0)))):
                copy.wait_recv()
                ref = outs[n].at[p ^ other, :, pl.ds(cols.start + k * half, half)]
                sent.append(send(ref, ref, mask))
        return sent

    side_cells, _, channels = maps.shape
    count = channels // LANES

    def norm_back():
        clear_edges(pad, side_cells)
        clear_edges(grad_pad, side_cells)
        small_at[0] = small_in[...]

        def norm(h, carry):
            v = mixed[h]
            centred = v - jnp.mean(v, axis=-1, keepdims=True)
            scale = lax.rsqrt(jnp.mean(centred * centred, axis=-1, keepdims=True) + 1e-06)
            unit = centred * scale
            grad = grad_normed[h]
            small_at[0, SIDE * SIDE : SIDE * SIDE + 1, :] += jnp.sum(grad * unit, axis=0, keepdims=True)
            grad = grad * gain[...]
            grad_maps[h] = scale * (
                grad - jnp.mean(grad, axis=-1, keepdims=True) - unit * jnp.mean(grad * unit, axis=-1, keepdims=True)
            )
            return carry

        lax.fori_loop(0, side_cells, norm, 0)

    def blocks(first, last):
        def one(block, carry):
            at = lane_block(block)
            inside = (slice(REACH, REACH + side_cells), slice(EDGE, EDGE + side_cells), slice(None))
            pad[inside] = maps[:, :, at].astype(jnp.float32)
            grad_pad[inside] = grad_maps[:, :, at]
            tap_sums[...] = jnp.zeros_like(tap_sums)

            def rows(group, inner):
                base = group * GROUP
                sums = conv_rows(grad_pad, lambda t: taps[pl.ds(t, 1), at], group, True, side_cells)
                for r in range(GROUP):
                    grad_maps[base + r, :, at] = sums[r]
                for dc in range(SIDE):
                    grads = [grad_pad[base + REACH + r, EDGE : EDGE + side_cells, :] for r in range(GROUP)]
                    acc = [None] * SIDE
                    for j in range(GROUP + SIDE - 1):
                        row = pad[base + j, EDGE - REACH + dc : EDGE - REACH + dc + side_cells, :]
                        for r in range(GROUP):
                            dr = j - r
                            if 0 <= dr < SIDE:
                                term = row * grads[r]
                                acc[dr] = term if acc[dr] is None else acc[dr] + term
                    for dr in range(SIDE):
                        tap_sums[dr * SIDE + dc] += jnp.sum(acc[dr].reshape(side_cells // 8, 8, LANES), axis=0)
                return inner

            lax.fori_loop(0, side_cells // GROUP, rows, 0)
            small_at[0, : SIDE * SIDE, at] = jnp.sum(tap_sums[...], axis=1)
            return carry

        lax.fori_loop(first, last, one, 0)

    small_masks = [(0, 1), (1, 0), (2, 0), (0, 2), (0, 4), (0, 1)]
    small_half = small_in.shape[0] // 2
    small_rows = pl.ds(pl.multiple_of(side * small_half, 8), small_half)
    small_rest = pl.ds(pl.multiple_of((1 - side) * small_half, 8), small_half)

    def small_send(s, rows):
        return send(small_at.at[s, rows], small_from.at[s, rows], small_masks[s])

    def small_step(s, copy):
        copy.wait_recv()
        small_at[s + 1, small_rows] = small_at[s, small_rows] + small_from[s, small_rows]
        return small_send(s + 1, small_rows)

    def small_end(copy):
        copy.wait_recv()
        small_out[small_rows] = small_at[5, small_rows]
        small_out[small_rest] = small_from[5, small_rest]

    thin_parts = [[group[2]] for group in thin]
    parts_reduce, parts_expand = wide[0][3], wide[1][3]
    thin_sent = [thin_two(i) for i in range(4)]
    one_reduce = wide_one(0, False)
    norm_back()
    blocks(0, count // 6)
    two_reduce = wide_two(0, one_reduce)
    blocks(count // 6, count // 3)
    thin_high = [thin_three(i, thin_sent[i]) for i in range(4)]
    one_expand = wide_one(1, True)
    blocks(count // 3, count // 2)
    high_reduce = [wide_three(0, two_reduce), heights(4, parts_reduce, 1)]
    thin_high = [further(i, thin_parts[i], 0, thin_high[i]) for i in range(4)]
    blocks(count // 2, count)
    small = small_send(0, small_rest)
    small = small_step(0, small)
    high_reduce = [further(4, parts_reduce, k, high_reduce[k]) for k in range(2)]
    small = small_step(1, small)
    two_expand = wide_two(1, one_expand)
    swaps = [total(i, thin_parts[i], 0, thin_high[i]) for i in range(4)]
    small = small_step(2, small)
    small = small_step(3, small)
    high_low = wide_three(1, two_expand)
    thin_out = [spread(i, swaps[i]) for i in range(4)]
    small = small_step(4, small)
    swap_reduce = [total(4, parts_reduce, k, high_reduce[k]) for k in range(2)]
    high_low = further(5, parts_expand, 0, high_low)
    high_high = heights(5, parts_expand, 1)
    small_end(small)
    swap_reduce[0].wait_recv()
    reduce_out = spread(4, swap_reduce[1])
    last = [relay(group) for group in thin_out]
    swap_low = total(5, parts_expand, 0, high_low)
    high_high = further(5, parts_expand, 1, high_high)
    low_out = spread(5, swap_low, 0, 2)
    last.append(relay(reduce_out))
    swap_high = total(5, parts_expand, 1, high_high)
    high_out = spread(5, swap_high, 1, 2)
    last.append(relay(low_out))
    last.append(relay(high_out))
    for group in thin_out + [reduce_out, low_out, high_out]:
        for entry in group:
            entry[2].wait()
    for group in last:
        for copy in group:
            copy.wait_recv()
    for copy in copies:
        copy.wait_send()


def scatter_gradients(part_reduce, part_expand, landed, thins, small, grad_normed, mixed, maps, taps, gain):
    side, _, channels = maps.shape
    low, full = jnp.bfloat16, jnp.float32
    anyspec, whole = pl.BlockSpec(memory_space=pl.ANY), pl.BlockSpec(memory_space=VMEM)
    dma = pltpu.SemaphoreType.DMA
    finals = [(t.shape[3], t.shape[4]) for t in thins] + [w.shape[4:] for w in (part_reduce, part_expand)]
    scratch = []
    for w in (part_reduce, part_expand):
        shape = w.shape[:3] + (w.shape[4], w.shape[5] // 2)
        landing = [jax.ShapeDtypeStruct(shape, low)] * 2
        scratch += [VMEM(shape, low)] * 2
    scratch += [VMEM(w.shape[:2] + (w.shape[4], w.shape[5] // 2), low) for w in (part_reduce, part_expand) for _ in range(2)]
    scratch += [VMEM((2, 2, 2, w.shape[4], w.shape[5] // 2), low) for w in (part_reduce, part_expand)]
    scratch += [VMEM(t.shape[:2] + t.shape[3:], low) for t in thins] * 2
    scratch += [VMEM((3, 2) + f, low) for f in finals]
    scratch += [VMEM((2,) + f, low) for f in finals]
    scratch += [VMEM((f[0], 2 * f[1]), low) for f in finals]
    edge = (side + 2 * REACH, side + 2 * EDGE, LANES)
    scratch += [VMEM((6,) + small.shape, full)] * 2
    scratch += [VMEM(edge, full)] * 2 + [VMEM((SIDE * SIDE, 8, LANES), full)]
    scratch += [dma((120,)), dma((120,)), dma((48,))]
    results = pl.pallas_call(
        scatter_kernel,
        out_shape=[jax.ShapeDtypeStruct(maps.shape, full), jax.ShapeDtypeStruct(small.shape, full)]
        + [jax.ShapeDtypeStruct((4, f[0], 2 * f[1]), low) for f in finals]
        + landing,
        in_specs=[anyspec] * 10 + [whole] * 6,
        out_specs=[whole] * 2 + [anyspec] * 8,
        scratch_shapes=scratch,
        compiler_params=pltpu.CompilerParams(
            collective_id=1, has_side_effects=True, vmem_limit_bytes=60 * 2**20
        ),
    )(part_reduce, part_expand, *landed, *thins, small, grad_normed, mixed, maps, taps, gain.reshape(1, channels))
    return results[0], results[1], results[2:8]


def layer_norm(values, gain_vec):
    centred = values - jnp.mean(values, axis=-1, keepdims=True)
    spread = jnp.mean(centred * centred, axis=-1, keepdims=True)
    return centred * lax.rsqrt(spread + 1e-06) * gain_vec


def depthwise(feature_map, taps_table, kernel_side):
    half_side = kernel_side // 2
    padded = jnp.pad(feature_map, ((0, 0), (half_side, half_side), (half_side, half_side), (0, 0)))
    map_side = feature_map.shape[1]
    accum_sum = jnp.zeros(feature_map.shape, feature_map.dtype)
    for offset_row in range(kernel_side):
        for offset_col in range(kernel_side):
            window = padded[
                :, offset_row : offset_row + map_side, offset_col : offset_col + map_side, :
            ]
            accum_sum = accum_sum + window * taps_table[offset_row * kernel_side + offset_col]
    return accum_sum


def section_depthwise(grid_field, grid_kernel):
    return depthwise(grid_field, grid_kernel, 7)


def adapter_depthwise(grid_field, grid_kernel):
    return depthwise(grid_field, grid_kernel, 3)


def swap(value, axis, mask):
    size = lax.axis_size(axis)
    return lax.ppermute(value, axis, [(i, i ^ mask) for i in range(size)])


def pick(value, index, axis):
    return lax.dynamic_index_in_dim(value, index, axis, keepdims=False)


def add_low(left, right):
    return (left.astype(jnp.float32) + right.astype(jnp.float32)).astype(jnp.bfloat16)


def place():
    path, dev = lax.axis_index("path"), lax.axis_index("dev")
    return path, path // 2, lax.rem(path, 2), dev // 2, lax.rem(dev, 2)


def both_images(rows):
    return jnp.concatenate([rows, swap(rows, "dev", 1)])


def pair_halves(grads):
    side = place()[4]
    half = grads.shape[1] // 2
    low, high = grads[:, :half], grads[:, half:]
    theirs = swap(jnp.where(side == 0, high, low), "dev", 1)
    return jnp.concatenate([jnp.where(side == 0, low, high), theirs])


def pair_product(rows, grads):
    result = lax.dot_general(rows, grads, (((0,), (0,)), ((), ())), preferred_element_type=jnp.float32)
    return result.astype(jnp.bfloat16).reshape(4, 2, 2, 2, rows.shape[1] // 32, grads.shape[1])


def pair_gradient(rows, grads):
    return pair_product(rows, pair_halves(grads))


def across_half(share, axis):
    return swap(pick(share, 1 - place()[2], axis), "path", 1)


def up_half(share, axis):
    return swap(pick(share, 1 - place()[1], axis), "path", 2)


def across_sum(share, axis, other):
    return add_low(pick(share, place()[2], axis), other)


def up_sum(share, axis, other):
    return add_low(pick(share, place()[1], axis), other)


def tie(*values):
    return lax.optimization_barrier(values)


def finish(pieces):
    return pieces.reshape(-1, pieces.shape[2]).astype(jnp.float32)


def plain_sum(rows, grads):
    product = lax.dot_general(
        rows, grads, (((0,), (0,)), ((), ())), preferred_element_type=jnp.float32
    ).astype(jnp.bfloat16)
    share = lax.psum_scatter(product, "dev", scatter_dimension=0, tiled=True)
    return lax.psum(share, "path").astype(jnp.float32)


def local(
    inputs,
    hires_maps,
    target_path,
    cotangent,
    attn_gain,
    w_qkv,
    w_out,
    mlp_gain,
    w_fc1,
    w_fc2,
    w_adapter,
    adapter_kernel,
    merge_gate,
    section_kernel,
    section_gain,
    w_expand,
    w_reduce,
    layer_scale,
):
    tuned = lax.axis_size("path") == 4 and lax.axis_size("dev") == 8
    weights = (w_expand, w_reduce, w_adapter, w_qkv, w_out, w_fc1, w_fc2)
    if tuned:
        ordered, section_mixed, section_rows, spread_targets, expanded, activated_low, reduced, features = gather_weights(
            [weights[i] for i in GATHER_ORDER],
            hires_maps[0],
            section_kernel,
            section_gain,
            layer_scale,
            target_path,
            GATHER_ORDER.index(0),
            GATHER_ORDER.index(1),
        )
        fulls = [ordered[GATHER_ORDER.index(i)] for i in range(len(weights))]
    else:
        fulls = [lax.all_gather(shard, "dev", axis=0, tiled=True) for shard in weights]
    full_expand, full_reduce, full_adapter, full_qkv, full_out, full_fc1, full_fc2 = fulls
    path_count = lax.axis_size("path")
    maps_float = hires_maps.astype(jnp.float32)
    map_side = maps_float.shape[1]
    channels = maps_float.shape[3]
    grid_side = map_side // 2
    tokens = grid_side * grid_side
    quarter_rows = tokens // path_count
    model_width = inputs.shape[2]
    head_count = model_width // HEAD_DIM
    score_scale = HEAD_DIM ** (-0.5)
    if not tuned:
        section_mixed, section_back = jax.vjp(section_depthwise, maps_float, section_kernel)
        section_normed, section_norm_back = jax.vjp(layer_norm, section_mixed, section_gain)
    if tuned:
        _, section_gelu_back = jax.vjp(jax.nn.gelu, expanded)
        reduced = reduced.reshape(maps_float.shape)
    else:
        section_rows = section_normed.reshape(-1, channels).astype(jnp.bfloat16)
        expanded = jnp.dot(section_rows, full_expand, preferred_element_type=jnp.float32)
        activated, section_gelu_back = jax.vjp(jax.nn.gelu, expanded)
        activated_low = activated.astype(jnp.bfloat16)
        reduced = jnp.dot(activated_low, full_reduce, preferred_element_type=jnp.float32).reshape(
            maps_float.shape
        )
        section_out = maps_float + layer_scale * reduced
        pooled = jnp.mean(
            section_out.reshape(grid_side, 2, grid_side, 2, channels), axis=(1, 3)
        ).reshape(tokens, channels)
    if not tuned:
        pieces = pooled.astype(jnp.bfloat16).reshape(path_count, quarter_rows, channels)
        own_target = jnp.broadcast_to(target_path, (path_count, 1))
        spread_pieces = lax.all_to_all(pieces, "path", split_axis=0, concat_axis=0, tiled=True)
        spread_targets = lax.all_to_all(own_target, "path", split_axis=0, concat_axis=0, tiled=True)
    selector = (
        jnp.arange(path_count, dtype=jnp.int32)[:, None] == spread_targets.reshape(1, path_count)
    ).astype(jnp.float32)
    if not tuned:
        routed = jnp.einsum("pq,qtc->ptc", selector, spread_pieces.astype(jnp.float32)).astype(jnp.bfloat16)
        arrived = lax.all_to_all(routed, "path", split_axis=0, concat_axis=0, tiled=True)
        features = arrived.reshape(tokens, channels)
    adapted = jnp.dot(features, full_adapter, preferred_element_type=jnp.float32)
    spread_map, adapter_back = jax.vjp(
        adapter_depthwise, adapted.reshape(1, grid_side, grid_side, model_width), adapter_kernel
    )
    spread_rows = spread_map.reshape(tokens, model_width)
    gate_factor = jnp.tanh(merge_gate)
    hidden_in = inputs[0].astype(jnp.float32) + gate_factor * spread_rows
    normed_one, norm_one_back = jax.vjp(layer_norm, hidden_in, attn_gain)
    attn_rows = normed_one.astype(jnp.bfloat16)
    projected = jnp.dot(attn_rows, full_qkv, preferred_element_type=jnp.float32).astype(
        jnp.bfloat16
    )
    queries = projected[:, :model_width].reshape(tokens, head_count, HEAD_DIM)
    key_rows = projected[:, model_width : 2 * model_width].reshape(tokens, head_count, HEAD_DIM)
    values = projected[:, 2 * model_width :].reshape(tokens, head_count, HEAD_DIM)
    scores = (
        jnp.einsum("thd,shd->hts", queries, key_rows, preferred_element_type=jnp.float32)
        * score_scale
    )
    probs = jax.nn.softmax(scores, axis=-1)
    probs_low = probs.astype(jnp.bfloat16)
    attn_mixed = jnp.einsum("hts,shd->thd", probs_low, values, preferred_element_type=jnp.float32)
    attn_mixed = attn_mixed.astype(jnp.bfloat16).reshape(tokens, model_width)
    attended = jnp.dot(attn_mixed, full_out, preferred_element_type=jnp.float32)
    hidden_mid = hidden_in + attended
    normed_two, norm_two_back = jax.vjp(layer_norm, hidden_mid, mlp_gain)
    mlp_rows = normed_two.astype(jnp.bfloat16)
    raised = jnp.dot(mlp_rows, full_fc1, preferred_element_type=jnp.float32)
    lifted_value, gelu_back = jax.vjp(jax.nn.gelu, raised)
    lifted = lifted_value.astype(jnp.bfloat16)
    lowered = jnp.dot(lifted, full_fc2, preferred_element_type=jnp.float32)
    result = (hidden_mid + lowered)[None].astype(jnp.bfloat16)
    grad_out = cotangent[0].astype(jnp.float32)
    grad_out_low = grad_out.astype(jnp.bfloat16)
    if tuned:
        part_fc2 = pair_gradient(both_images(lifted), grad_out_low)
    else:
        grad_fc2_w = plain_sum(lifted, grad_out_low)
    grad_lifted = jnp.dot(grad_out_low, full_fc2.T, preferred_element_type=jnp.float32)
    grad_raised = gelu_back(grad_lifted)[0].astype(jnp.bfloat16)
    if tuned:
        part_fc1 = pair_gradient(both_images(mlp_rows), grad_raised)
    else:
        grad_fc1_w = plain_sum(mlp_rows, grad_raised)
    grad_normed_two = jnp.dot(grad_raised, full_fc1.T, preferred_element_type=jnp.float32)
    grad_mid_norm, grad_mlp_gain = norm_two_back(grad_normed_two)
    grad_mid = grad_out + grad_mid_norm
    grad_attended = grad_mid.astype(jnp.bfloat16)
    if tuned:
        part_out = pair_gradient(both_images(attn_mixed), grad_attended)
    else:
        grad_out_w = plain_sum(attn_mixed, grad_attended)
    grad_mixed = jnp.dot(grad_attended, full_out.T, preferred_element_type=jnp.float32)
    grad_mixed = grad_mixed.astype(jnp.bfloat16).reshape(tokens, head_count, HEAD_DIM)
    grad_probs = jnp.einsum("thd,shd->hts", grad_mixed, values, preferred_element_type=jnp.float32)
    grad_values = jnp.einsum(
        "hts,thd->shd", probs_low, grad_mixed, preferred_element_type=jnp.float32
    )
    grad_scores = probs * (grad_probs - jnp.sum(grad_probs * probs, axis=-1, keepdims=True))
    grad_scores = grad_scores.astype(jnp.bfloat16)
    grad_queries = (
        jnp.einsum("hts,shd->thd", grad_scores, key_rows, preferred_element_type=jnp.float32)
        * score_scale
    )
    grad_keys = (
        jnp.einsum("hts,thd->shd", grad_scores, queries, preferred_element_type=jnp.float32)
        * score_scale
    )
    grad_projected = jnp.concatenate(
        [
            grad_queries.reshape(tokens, model_width),
            grad_keys.reshape(tokens, model_width),
            grad_values.reshape(tokens, model_width),
        ],
        axis=1,
    ).astype(jnp.bfloat16)
    if tuned:
        part_qkv = pair_gradient(both_images(attn_rows), grad_projected)
    else:
        grad_qkv_w = plain_sum(attn_rows, grad_projected)
    grad_normed_one = jnp.dot(grad_projected, full_qkv.T, preferred_element_type=jnp.float32)
    grad_in_norm, grad_attn_gain = norm_one_back(grad_normed_one)
    grad_in = grad_mid + grad_in_norm
    grad_merge = jnp.sum(grad_in * spread_rows, axis=0) * (1.0 - gate_factor * gate_factor)
    grad_spread = (grad_in * gate_factor).reshape(1, grid_side, grid_side, model_width)
    grad_adapted, grad_adapter_taps = adapter_back(grad_spread)
    grad_adapted_low = grad_adapted.reshape(tokens, model_width).astype(jnp.bfloat16)
    if tuned:
        part_adapter = pair_gradient(both_images(features), grad_adapted_low)
    else:
        grad_adapter_w = plain_sum(features, grad_adapted_low)
    grad_features = jnp.dot(grad_adapted_low, full_adapter.T, preferred_element_type=jnp.float32)
    grad_pieces = grad_features.astype(jnp.bfloat16).reshape(path_count, quarter_rows, channels)
    grad_routed = lax.all_to_all(grad_pieces, "path", split_axis=0, concat_axis=0, tiled=True)
    grad_unrouted = jnp.einsum("pq,ptc->qtc", selector, grad_routed.astype(jnp.float32)).astype(
        jnp.bfloat16
    )
    grad_home = lax.all_to_all(grad_unrouted, "path", split_axis=0, concat_axis=0, tiled=True)
    if tuned:
        part_rest = jnp.concatenate([part_out, part_adapter], axis=4)
        _, up, across, _, _ = place()
        going = [pick(part_fc2, 1 - across, 3), pick(part_fc1, 1 - up, 2), pick(part_qkv, 1 - across, 3), pick(part_rest, 1 - up, 2)]
        grad_home, part_fc2, part_fc1, part_qkv, part_rest, *going = tie(
            grad_home, part_fc2, part_fc1, part_qkv, part_rest, *going
        )
        half_fc2, half_fc1, half_qkv, half_rest = [swap(piece, "path", 1 + k % 2) for k, piece in enumerate(going)]
    grad_pooled = grad_home.astype(jnp.float32).reshape(tokens, channels)
    quarter = (grad_pooled * 0.25).reshape(1, grid_side, 1, grid_side, 1, channels)
    grad_section_out = jnp.broadcast_to(quarter, (1, grid_side, 2, grid_side, 2, channels)).reshape(
        maps_float.shape
    )
    grad_scale = jnp.sum((grad_section_out * reduced).reshape(-1, channels), axis=0)
    grad_reduced = (grad_section_out * layer_scale).reshape(-1, channels).astype(jnp.bfloat16)
    if tuned:
        part_reduce = pair_gradient(both_images(activated_low), grad_reduced)
        columns = part_reduce.shape[5] // 2
        leaving = [
            pick(part_reduce[first : first + 2, ..., :columns], 1 - place()[2], 3) for first in (0, 2)
        ] + [pick(part_reduce[first : first + 2, ..., columns:], 1 - place()[1], 2) for first in (0, 2)]
        grad_reduced, part_reduce, *leaving = tie(grad_reduced, part_reduce, *leaving)
        landed = [swap(piece, "path", 1 + k // 2) for k, piece in enumerate(leaving)]
    else:
        grad_reduce_w = plain_sum(activated_low, grad_reduced)
    grad_activated = jnp.dot(grad_reduced, full_reduce.T, preferred_element_type=jnp.float32)
    grad_expanded = section_gelu_back(grad_activated)[0].astype(jnp.bfloat16)
    if tuned:
        grad_expanded, half_fc2, half_fc1 = tie(grad_expanded, half_fc2, half_fc1)
    else:
        grad_expand_w = plain_sum(section_rows, grad_expanded)
    grad_section_normed = jnp.dot(
        grad_expanded, full_expand.T, preferred_element_type=jnp.float32
    ).reshape(maps_float.shape)
    if tuned:
        halves_expand = pair_halves(grad_expanded)
        grad_section_normed, halves_expand, half_qkv, half_rest, landed[0], landed[2] = tie(
            grad_section_normed, halves_expand, half_qkv, half_rest, landed[0], landed[2]
        )
        part_expand = pair_product(both_images(section_rows), halves_expand)
        step_fc2, step_fc1 = across_sum(part_fc2, 3, half_fc2), up_sum(part_fc1, 2, half_fc1)
        step_qkv, step_rest = across_sum(part_qkv, 3, half_qkv), up_sum(part_rest, 2, half_rest)
        small_rows = jnp.concatenate(
            [
                jnp.zeros((section_kernel.shape[0] + 1, channels), jnp.float32),
                jnp.concatenate([grad_attn_gain, grad_mlp_gain, grad_merge, grad_adapter_taps.reshape(-1)]).reshape(-1, channels),
                grad_scale[None],
            ]
        )
        small_count = small_rows.shape[0]
        small_rows = jnp.pad(small_rows, ((0, -small_count % 16), (0, 0)))
        grad_maps, small_rows, pieces = scatter_gradients(
            part_reduce,
            part_expand,
            landed,
            [step_fc2, step_fc1, step_qkv, step_rest],
            small_rows,
            grad_section_normed[0],
            section_mixed,
            hires_maps[0],
            section_kernel,
            section_gain,
        )
        grad_maps = grad_maps[None] + grad_section_out
        split = part_out.shape[4]
        grad_fc2_w, grad_fc1_w, grad_qkv_w = [finish(piece) for piece in pieces[:3]]
        grad_out_w, grad_adapter_w = finish(pieces[3][:, :split]), finish(pieces[3][:, split:])
        grad_reduce_w, grad_expand_w = finish(pieces[4]), finish(pieces[5])
    else:
        grad_section_mixed, grad_section_gain = section_norm_back(grad_section_normed)
        grad_maps_conv, grad_section_taps = section_back(grad_section_mixed)
        grad_maps = grad_section_out + grad_maps_conv
    summed = (
        grad_qkv_w,
        grad_out_w,
        grad_fc1_w,
        grad_fc2_w,
        grad_adapter_w,
        grad_expand_w,
        grad_reduce_w,
    )
    if tuned:
        tap_count = section_kernel.shape[0]
        flat = small_rows[tap_count + 1 : small_count - 1].reshape(-1)
        small_sums = (
            flat[:model_width],
            flat[model_width : 2 * model_width],
            flat[2 * model_width : 3 * model_width],
            flat[3 * model_width :].reshape(adapter_kernel.shape),
            small_rows[tap_count],
            small_rows[:tap_count],
            small_rows[small_count - 1],
        )
    else:
        small_sums = lax.psum(
            (
                grad_attn_gain,
                grad_mlp_gain,
                grad_merge,
                grad_adapter_taps,
                grad_section_gain,
                grad_section_taps,
                grad_scale,
            ),
            ("path", "dev"),
        )
    return (
        result,
        grad_in[None],
        grad_maps,
        small_sums[0],
        summed[0],
        summed[1],
        small_sums[1],
        summed[2],
        summed[3],
        summed[4],
        small_sums[3],
        small_sums[2],
        small_sums[5],
        small_sums[4],
        summed[5],
        summed[6],
        small_sums[6],
    )


def solution(mesh):
    return jax.shard_map(
        local,
        mesh=mesh,
        in_specs=(
            P(("path", "dev"), None, None),
            P(("path", "dev"), None, None, None),
            P("path", "dev"),
            P(("path", "dev"), None, None),
            P(),
            P("dev", None),
            P("dev", None),
            P(),
            P("dev", None),
            P("dev", None),
            P("dev", None),
            P(),
            P(),
            P(),
            P(),
            P("dev", None),
            P("dev", None),
            P(),
        ),
        out_specs=(
            P(("path", "dev"), None, None),
            P(("path", "dev"), None, None),
            P(("path", "dev"), None, None, None),
            P(),
            P("dev", None),
            P("dev", None),
            P(),
            P("dev", None),
            P("dev", None),
            P("dev", None),
            P(),
            P(),
            P(),
            P(),
            P("dev", None),
            P("dev", None),
            P(),
        ),
        check_vma=False,
    )
```

```python
import functools

import jax
import jax.numpy as jnp
from jax import lax
from jax.experimental import pallas as pl
from jax.experimental.pallas import tpu as pltpu
from jax.sharding import PartitionSpec as P

HEAD_DIM = 64
MESH = pl.DeviceIdType.MESH
VMEM = pltpu.VMEM
SIDE, REACH, EDGE, GROUP, LANES = 7, 3, 8, 8, 128


def conv_rows(src, taps, group, flip, side):
    base = group * GROUP
    sums = [None] * GROUP
    for dc in range(SIDE):
        col = [taps((SIDE - 1 - dr) * SIDE + SIDE - 1 - dc if flip else dr * SIDE + dc) for dr in range(SIDE)]
        for j in range(GROUP + SIDE - 1):
            row = src[base + j, EDGE - REACH + dc : EDGE - REACH + dc + side, :]
            for r in range(GROUP):
                if 0 <= j - r < SIDE:
                    term = row * col[j - r]
                    sums[r] = term if sums[r] is None else sums[r] + term
    return sums


def clear_edges(pad, side):
    rows, columns, lanes = pad.shape[-3:]
    pad[:, :EDGE, :] = jnp.zeros((rows, EDGE, lanes), jnp.float32)
    pad[:, EDGE + side :, :] = jnp.zeros((rows, columns - EDGE - side, lanes), jnp.float32)
    pad[:REACH] = jnp.zeros((REACH, columns, lanes), jnp.float32)
    pad[REACH + side :] = jnp.zeros((rows - REACH - side, columns, lanes), jnp.float32)


def lane_block(block):
    return pl.ds(pl.multiple_of(block * LANES, LANES), LANES)


def mix_block(block, maps, taps, mixed, pad):
    side = maps.shape[0]
    at = lane_block(block)
    pad[REACH : REACH + side, EDGE : EDGE + side, :] = maps[:, :, at].astype(jnp.float32)

    def rows(group, carry):
        sums = conv_rows(pad, lambda t: taps[pl.ds(t, 1), at], group, False, side)
        for r in range(GROUP):
            mixed[group * GROUP + r, :, at] = sums[r]
        return carry

    lax.fori_loop(0, side // GROUP, rows, 0)


def mix_blocks(first, last, maps, taps, mixed, pad):
    def blocks(block, carry):
        mix_block(block, maps, taps, mixed, pad)
        return carry

    lax.fori_loop(first, last, blocks, 0)


def norm_all(gain, mixed, rows):
    side, _, channels = mixed.shape

    def norm(pair, carry):
        v = mixed[pl.ds(2 * pair, 2)].reshape(2 * side, channels)
        centred = v - jnp.mean(v, axis=-1, keepdims=True)
        scale = lax.rsqrt(jnp.mean(centred * centred, axis=-1, keepdims=True) + 1e-06)
        at = pl.ds(pl.multiple_of(pair * 2 * side, 2 * side), 2 * side)
        rows[at, :] = (centred * scale * gain[...]).astype(jnp.bfloat16)
        return carry

    lax.fori_loop(0, side // 2, norm, 0)


STEP = 512


def product(left, right, total, left_at, right_at):
    total[...] = jnp.zeros_like(total)

    def step(k, carry):
        here = pl.multiple_of(k * STEP, STEP)
        total[...] += jnp.dot(
            left[:, pl.ds(left_at + here, STEP)],
            right[pl.ds(here, STEP), pl.ds(pl.multiple_of(right_at, STEP), STEP)],
            preferred_element_type=jnp.float32,
        )
        return carry

    lax.fori_loop(0, right.shape[0] // STEP, step, 0)


def gather_jobs(shapes):
    jobs = []
    for w, (r, n) in enumerate(shapes):
        parts = max(1, round(r // 4 * n / (16 * 6144)))
        while n % (parts * STEP):
            parts -= 1
        jobs += [(w, r // 4, k * (n // parts), n // parts) for k in range(parts)]
    return jobs


def gather_kernel(jobs, count, expand, reduce, *refs):
    shards = refs[:count]
    maps, taps, gain, scale, target = refs[count : count + 5]
    fulls = refs[count + 5 : 2 * count + 5]
    mixed_out, rows_out, targets, expanded, block_active, block_reduced, features = refs[2 * count + 5 : 2 * count + 12]
    pad, wide_w, deep_w, total, stage, pair_sum, pooled, leaving, met, sorted_maps, landing = refs[2 * count + 12 : 2 * count + 23]
    mixed, rows, active = refs[2 * count + 23 : 2 * count + 26]
    zs, zr, ps, pr, cs, cr, os, orr, ls, ts, tr, ws, es, fs, fr, gs, gr, xs = refs[2 * count + 26 :]
    p, d = lax.axis_index("path"), lax.axis_index("dev")

    def at(m):
        return (p ^ m[0], d ^ m[1])

    masks = [(0, 1), (0, 2), (0, 4), (0, 6), (1, 0), (2, 0), (3, 0)]
    bar = pltpu.get_barrier_semaphore()
    for m in masks:
        pl.semaphore_signal(bar, inc=1, device_id=at(m), device_id_type=MESH)
    pl.semaphore_wait(bar, len(masks))

    def copy(src, dst, ss, rs, m):
        return pltpu.make_async_remote_copy(src, dst, ss, rs, device_id=at(m), device_id_type=MESH)

    def quarter(w, owner, q, nq, c0, nc):
        r = shards[w].shape[0]
        return fulls[w].at[pl.ds(pl.multiple_of(owner * r + q * nq, 16), nq), pl.ds(c0, nc)]

    J = len(jobs)

    def Z(i, k):
        w, nq, c0, nc = jobs[i]
        src = shards[w].at[pl.ds(pl.multiple_of(p * nq, 16), nq), pl.ds(c0, nc)]
        return copy(src, quarter(w, d, p, nq, c0, nc), zs.at[i, k], zr.at[i, k], (0, 2 * (k + 1)))

    def XY(i, k, axis):
        w, nq, c0, nc = jobs[i]
        ref = quarter(w, d ^ (2 * (k + 1)), p, nq, c0, nc)
        return copy(ref, ref, ps.at[i, k, axis], pr.at[i, k, axis], (1 + axis, 0))

    def DG(i, k, axis):
        w, nq, c0, nc = jobs[i]
        h = nc // 2
        ref = quarter(w, d ^ (2 * (k + 1)), p ^ (2 - axis), nq, c0 + axis * h, h)
        return copy(ref, ref, ps.at[i, k, 2 + axis], pr.at[i, k, 2 + axis], (1 + axis, 0))

    def S(i, k):
        w, nq, c0, nc = jobs[i]
        r = shards[w].shape[0]
        ref = fulls[w].at[pl.ds(pl.multiple_of((d ^ (2 * (k + 1))) * r, 16), r), pl.ds(c0, nc)]
        return copy(ref, ref, cs.at[i, k], cr.at[i, k], (0, 1))

    for i in range(min(AHEAD, J)):
        for k in range(3):
            Z(i, k).start()
    own = []
    for w in range(count):
        r = shards[w].shape[0]
        place = fulls[w].at[pl.ds(pl.multiple_of(d * r, 16), r)]
        pair = pltpu.make_async_copy(shards[w], place, ls.at[w]), copy(shards[w], place, os.at[w], orr.at[w], (0, 1))
        for c in pair:
            c.start()
        own.append(pair)
    targets[p] = target[...]
    named = [copy(target, targets.at[p], ts.at[m - 1], tr.at[m - 1], (m, 0)) for m in (1, 2, 3)]
    for c in named:
        c.start()
    clear_edges(pad, maps.shape[0])
    blocks = maps.shape[2] // LANES
    leaving_vmem = []

    def write_out(src, dst):
        c = pltpu.make_async_copy(src, dst, xs.at[len(leaving_vmem)])
        c.start()
        leaving_vmem.append(c)

    ready = set()

    def ensure(w):
        if w not in ready:
            ready.add(w)
            own[w][0].wait()
            own[w][1].wait_recv()

    def cell_row(row):
        side = maps.shape[0]
        return pl.ds(pl.multiple_of(row * side, 8), side)

    def pairs(value):
        blocks, half = value.shape[1] // LANES, value.shape[0] // 2
        for k in range(blocks):
            pair_sum[k] = value[:, k * LANES : (k + 1) * LANES]
        return [
            pair_sum[k, pl.ds(0, half, stride=2), :] + pair_sum[k, pl.ds(1, half, stride=2), :] for k in range(blocks)
        ]

    def expand_block(c0, nc):
        load = pltpu.make_async_copy(fulls[expand].at[:, pl.ds(c0, nc)], wide_w, ws.at[0])
        load.start()
        load.wait()

        def chunk(j, carry):
            here = pl.multiple_of(j * STEP, STEP)
            product(rows, wide_w, total, 0, here)
            stage[...] = total[...]
            low = jax.nn.gelu(total[...]).astype(jnp.bfloat16)
            active[:, pl.ds(c0 + here, STEP)] = low
            total[...] = low.astype(jnp.float32)

            def block_sums(h, inner):
                sums = pairs(total[cell_row(2 * h), :] + total[cell_row(2 * h + 1), :])
                for k, value in enumerate(sums):
                    lanes = pl.ds(pl.multiple_of(c0 + here + k * LANES, LANES), LANES)
                    block_active[h, :, lanes] = value.astype(jnp.bfloat16)
                return inner

            lax.fori_loop(0, maps.shape[0] // 2, block_sums, 0)
            out = pltpu.make_async_copy(stage, expanded.at[:, pl.ds(c0 + here, STEP)], es.at[0])
            out.start()
            out.wait()
            return carry

        lax.fori_loop(0, nc // STEP, chunk, 0)

    def reduce_block(c0, nc):
        load = pltpu.make_async_copy(fulls[reduce].at[:, pl.ds(c0, nc)], deep_w, ws.at[1])
        load.start()
        load.wait()
        cols = pl.ds(c0, nc)
        product(active, deep_w, total, 0, 0)
        side = maps.shape[0]

        def pool(h, carry):
            part = pairs(total[cell_row(2 * h), :] + total[cell_row(2 * h + 1), :])
            for k, value in enumerate(part):
                block_reduced[h, :, c0 + k * LANES : c0 + (k + 1) * LANES] = value * 0.25
            cells = pairs(maps[2 * h, :, cols].astype(jnp.float32) + maps[2 * h + 1, :, cols].astype(jnp.float32))
            for k, value in enumerate(cells):
                lanes = slice(c0 + k * LANES, c0 + (k + 1) * LANES)
                pooled[h, :, lanes] = value * 0.25 + scale[:, lanes] * block_reduced[h, :, lanes]
            return carry

        lax.fori_loop(0, side // 2, pool, 0)

    parts = maps.shape[2] // 4

    def hop(src, dst, ss, rs):
        return [copy(src.at[p ^ m], dst.at[p], ss.at[m - 1], rs.at[m - 1], (m, 0)) for m in (1, 2, 3)]

    def route_one():
        for k in range(4):
            leaving[k] = pooled[..., k * parts : (k + 1) * parts].reshape(leaving.shape[1:]).astype(jnp.bfloat16)
        met[p] = leaving[p]
        sent = hop(leaving, met, fs, fr)
        for c in sent:
            c.start()
        return sent

    def route_two(sent):
        for c in sent + named:
            c.wait()
        for k in range(4):
            chosen = jnp.zeros(met.shape[1:], jnp.float32)
            for q in range(4):
                here = targets[q, :1, :1] == k
                chosen += jnp.where(here, met[q].astype(jnp.float32), 0.0)
            sorted_maps[k] = chosen.astype(jnp.bfloat16)
        landing[p] = sorted_maps[p]
        sent = hop(sorted_maps, landing, gs, gr)
        for c in sent:
            c.start()
        return sent

    def route_three(sent):
        for c in sent:
            c.wait()
        for k in range(4):
            features[:, k * parts : (k + 1) * parts] = landing[k]

    last_reduce = max(i for i in range(J) if jobs[i][0] == reduce)
    routed = None
    for i in range(J + 3):
        if i < J:
            for k in range(3):
                Z(i, k).wait_recv()
                XY(i, k, 0).start()
                XY(i, k, 1).start()
            if i + AHEAD < J:
                for k in range(3):
                    Z(i + AHEAD, k).start()
        if 0 <= i - 1 < J:
            for k in range(3):
                XY(i - 1, k, 0).wait_recv()
                DG(i - 1, k, 1).start()
                XY(i - 1, k, 1).wait_recv()
                DG(i - 1, k, 0).start()
        if 0 <= i - 2 < J:
            for k in range(3):
                DG(i - 2, k, 0).wait_recv()
                DG(i - 2, k, 1).wait_recv()
                S(i - 2, k).start()
        if i < MIX_STEPS:
            mix_blocks(i * blocks // MIX_STEPS, (i + 1) * blocks // MIX_STEPS, maps, taps, mixed, pad)
        if i + 1 == MIX_STEPS:
            norm_all(gain, mixed, rows)
            write_out(mixed, mixed_out)
            write_out(rows, rows_out)
        if 0 <= i - 3 < J:
            for k in range(3):
                S(i - 3, k).wait_recv()
            w, _, c0, nc = jobs[i - 3]
            ensure(w)
            if w == expand:
                expand_block(c0, nc)
            if w == reduce:
                reduce_block(c0, nc)
            if i - 3 == last_reduce:
                routed = route_one()
            if i - 3 == last_reduce + 1:
                routed = route_two(routed)
            if i - 3 == last_reduce + 2:
                route_three(routed)
    for c in leaving_vmem:
        c.wait()
    for w in range(count):
        ensure(w)
        own[w][1].wait_send()
    for i in range(J):
        for k in range(3):
            Z(i, k).wait_send()
            S(i, k).wait_send()
            for a in range(2):
                XY(i, k, a).wait_send()
                DG(i, k, a).wait_send()


AHEAD = 3
MIX_STEPS = 3
GATHER_ORDER = (4, 0, 1, 5, 6, 3, 2)


def gather_weights(shards, maps, taps, gain, scale, target, expand, reduce):
    shapes = [s.shape for s in shards]
    jobs = gather_jobs(shapes)
    n, J = len(shards), len(jobs)
    side, _, channels = maps.shape
    cells, hidden = side * side, shapes[expand][1]
    wide = max(nc for w, _, _, nc in jobs if w == expand)
    low, full = jnp.bfloat16, jnp.float32
    anyspec, whole = pl.BlockSpec(memory_space=pl.ANY), pl.BlockSpec(memory_space=VMEM)
    dma = pltpu.SemaphoreType.DMA
    shape = jax.ShapeDtypeStruct
    results = pl.pallas_call(
        functools.partial(gather_kernel, jobs, n, expand, reduce),
        out_shape=[shape((8 * r, c), low) for r, c in shapes]
        + [
            shape(maps.shape, full),
            shape((cells, channels), low),
            shape((4, 8, LANES), jnp.int32),
            shape((cells, hidden), full),
            shape((side // 2, side // 2, hidden), low),
            shape((side // 2, side // 2, channels), full),
            shape((cells // 4, channels), low),
        ],
        in_specs=[anyspec] * n + [whole] * 5,
        out_specs=[anyspec] * n + [anyspec] * 2 + [whole] + [anyspec] + [whole] * 3,
        scratch_shapes=[
            VMEM((side + 2 * REACH, side + 2 * EDGE, LANES), full),
            VMEM((channels, wide), low),
            VMEM((hidden, STEP), low),
            VMEM((cells, STEP), full),
            VMEM((cells, STEP), full),
            VMEM((STEP // LANES, side, LANES), full),
            VMEM((side // 2, side // 2, channels), full),
            VMEM((4, cells // 4, channels // 4), low),
            VMEM((4, cells // 4, channels // 4), low),
            VMEM((4, cells // 4, channels // 4), low),
            VMEM((4, cells // 4, channels // 4), low),
            VMEM(maps.shape, full),
            VMEM((cells, channels), low),
            VMEM((cells, hidden), low),
        ]
        + [dma((J, 3)), dma((J, 3)), dma((J, 3, 4)), dma((J, 3, 4)), dma((J, 3)), dma((J, 3))]
        + [dma((n,)), dma((n,)), dma((n,)), dma((3,)), dma((3,)), dma((2,)), dma((1,))] + [dma((3,))] * 4 + [dma((4,))],
        compiler_params=pltpu.CompilerParams(
            collective_id=0, has_side_effects=True, vmem_limit_bytes=60 * 2**20
        ),
    )(
        *shards, maps, taps, gain.reshape(1, channels), scale.reshape(1, channels),
        jnp.broadcast_to(target, (8, LANES)),
    )
    rest = results[n:]
    return results[:n], rest[0], rest[1], rest[2][:, 0, 0], rest[3], rest[4], rest[5], rest[6]


def add_block(total, term):
    return (total.astype(jnp.float32) + term.astype(jnp.float32)).astype(jnp.bfloat16)


def scatter_kernel(
    big0, big1, land0a, land0b, land0c, land0d, t0, t1, t2, t3, small_in, grad_normed, mixed, maps, taps, gain,
    grad_maps, small_out, o0, o1, o2, o3, o4, o5, land1a, land1b,
    acc0a, acc0b, acc1a, acc1b, two0a, two0b, two1a, two1b, tmp0, tmp1,
    own0, own1, own2, own3, two0, two1, two2, two3,
    zr0, zr1, zr2, zr3, zr4, zr5, low0, low1, low2, low3, low4, low5,
    full0, full1, full2, full3, full4, full5,
    small_at, small_from, pad, grad_pad, tap_sums, ssem, rsem, lsem,
):
    p, d = lax.axis_index("path"), lax.axis_index("dev")
    up, across, height, side = p // 2, lax.rem(p, 2), d // 2, lax.rem(d, 2)
    masks = [(0, 1), (0, 2), (0, 4), (0, 6), (1, 0), (2, 0), (3, 0)]
    bar = pltpu.get_barrier_semaphore()
    for m in masks:
        pl.semaphore_signal(bar, inc=1, device_id=(p ^ m[0], d ^ m[1]), device_id_type=MESH)
    pl.semaphore_wait(bar, len(masks))

    copies = []

    def send(src, dst, m):
        n = len(copies)
        copy = pltpu.make_async_remote_copy(
            src, dst, ssem.at[n], rsem.at[n], device_id=(p ^ m[0], d ^ m[1]), device_id_type=MESH
        )
        copies.append(copy)
        copy.start()
        return copy

    local = []

    def fetch(src, dst):
        copy = pltpu.make_async_copy(src, dst, lsem.at[len(local)])
        local.append(copy)
        copy.start()
        return copy

    thin = [(t0, own0, two0, True), (t1, own1, two1, False), (t2, own2, two2, True), (t3, own3, two3, False)]
    wide = [
        (big0, (acc0a, acc0b), ((land0a, land0b), (land0c, land0d)), (two0a, two0b), tmp0),
        (big1, (acc1a, acc1b), ((land1a,), (land1b,)), (two1a, two1b), tmp1),
    ]
    outs = [o0, o1, o2, o3, o4, o5]
    zrs, lows, wholes = [zr0, zr1, zr2, zr3, zr4, zr5], [low0, low1, low2, low3, low4, low5], [full0, full1, full2, full3, full4, full5]

    def thin_two(i):
        src, own, two, upward = thin[i]
        index, mask = (up, (2, 0)) if upward else (across, (1, 0))
        loaded = fetch(src.at[:, :, index], own)
        return loaded, send(src.at[:, :, 1 - index], two, mask)

    def wide_one(w, ours):
        src, acc, land, _, _ = wide[w]
        half = src.shape[5] // 2
        a, b = pl.ds(0, half), pl.ds(half, half)
        loaded = [fetch(src.at[:, :, :, across, :, a], acc[0]), fetch(src.at[:, :, up, :, :, b], acc[1])]
        if not ours:
            return loaded
        return loaded + [
            send(src.at[:, :, :, 1 - across, :, a], land[0][0], (1, 0)),
            send(src.at[:, :, 1 - up, :, :, b], land[1][0], (2, 0)),
        ]

    def wide_two(w, started):
        src, acc, land, two, tmp = wide[w]
        started[0].wait()
        started[1].wait()
        sent = []
        for copy in started[2:]:
            copy.wait_recv()
        for k in range(2):
            each = 4 // len(land[k])
            loads = [fetch(land[k][0].at[0], tmp.at[0])]
            for z in range(4):
                if z < 3:
                    loads.append(fetch(land[k][(z + 1) // each].at[(z + 1) % each], tmp.at[(z + 1) % 2]))
                loads[z].wait()
                for c in range(2):
                    for q in range(2):
                        acc[k][z, c, q] = add_block(acc[k][z, c, q], tmp[z % 2, c, q])
            index, mask = (up, (2, 0)) if k == 0 else (across, (1, 0))
            sent.append(send(acc[k].at[:, :, 1 - index], two[k], mask))
        return sent

    def columns_of(n, parts, k):
        half = zrs[n].shape[3] // len(parts)
        return pl.ds(k * half, half)

    def heights(n, parts, k):
        cols = columns_of(n, parts, k)
        return [send(parts[k].at[height ^ m], zrs[n].at[m // 2, :, :, cols], (0, 2)) for m in (1, 3)]

    def further(n, parts, k, sent):
        for copy in sent:
            copy.wait_recv()
        cols = columns_of(n, parts, k)
        for c in range(2):
            zrs[n][1, c, :, cols] = add_block(zrs[n][1, c, :, cols], parts[k][height ^ 2, c])
        return send(zrs[n].at[1, :, :, cols], zrs[n].at[2, :, :, cols], (0, 4))

    def thin_three(i, started):
        _, own, two, _ = thin[i]
        started[0].wait()
        started[1].wait_recv()
        for z in range(4):
            for c in range(2):
                two[z, c] = add_block(two[z, c], own[z, c])
        return heights(i, [two], 0)

    def wide_three(w, sent):
        _, acc, _, two, _ = wide[w]
        for k in range(2):
            index = up if k == 0 else across
            sent[k].wait_recv()
            for z in range(4):
                for c in range(2):
                    two[k][z, c] = add_block(two[k][z, c], acc[k][z, c, index])
        return heights(4 + w, two, 0)

    def total(n, parts, k, sent):
        sent.wait_recv()
        zr, low, whole = zrs[n], lows[n], wholes[n]
        size = zr.shape[3]
        half = size // len(parts)
        cols = slice(k * half, (k + 1) * half)
        for c in range(2):
            value = parts[k][height, c].astype(jnp.float32)
            for m in (0, 2):
                value = value + zr[m, c, :, cols].astype(jnp.float32)
            low[c, :, cols] = value.astype(jnp.bfloat16)
        place = (slice(None), pl.ds(pl.multiple_of(side * size + k * half, LANES), half))
        whole[place] = low[side, :, cols]
        return send(low.at[1 - side, :, cols], whole.at[place], (0, 1))

    def spread(n, swapped, first=0, parts=1):
        swapped.wait_recv()
        size = zrs[n].shape[3]
        group = []
        for c in range(2):
            cols = pl.ds(c * size + first * (size // parts), size // parts)
            src, dst = wholes[n].at[:, cols], outs[n].at[p, :, cols]
            group.append((n, cols, fetch(src, dst), send(src, dst, (1, 0)), send(src, dst, (2, 0))))
        return group

    def relay(group):
        sent = []
        for n, cols, _, along_x, along_y in group:
            half = cols.size // 2
            for k, (copy, other, mask) in enumerate(((along_x, 1, (2, 0)), (along_y, 2, (1, 0)))):
                copy.wait_recv()
                ref = outs[n].at[p ^ other, :, pl.ds(cols.start + k * half, half)]
                sent.append(send(ref, ref, mask))
        return sent

    side_cells, _, channels = maps.shape
    count = channels // LANES

    def norm_back():
        clear_edges(pad, side_cells)
        clear_edges(grad_pad, side_cells)
        small_at[0] = small_in[...]

        def norm(h, carry):
            v = mixed[h]
            centred = v - jnp.mean(v, axis=-1, keepdims=True)
            scale = lax.rsqrt(jnp.mean(centred * centred, axis=-1, keepdims=True) + 1e-06)
            unit = centred * scale
            grad = grad_normed[h]
            small_at[0, SIDE * SIDE : SIDE * SIDE + 1, :] += jnp.sum(grad * unit, axis=0, keepdims=True)
            grad = grad * gain[...]
            grad_maps[h] = scale * (
                grad - jnp.mean(grad, axis=-1, keepdims=True) - unit * jnp.mean(grad * unit, axis=-1, keepdims=True)
            )
            return carry

        lax.fori_loop(0, side_cells, norm, 0)

    def blocks(first, last):
        def one(block, carry):
            at = lane_block(block)
            inside = (slice(REACH, REACH + side_cells), slice(EDGE, EDGE + side_cells), slice(None))
            pad[inside] = maps[:, :, at].astype(jnp.float32)
            grad_pad[inside] = grad_maps[:, :, at]
            tap_sums[...] = jnp.zeros_like(tap_sums)

            def rows(group, inner):
                base = group * GROUP
                sums = conv_rows(grad_pad, lambda t: taps[pl.ds(t, 1), at], group, True, side_cells)
                for r in range(GROUP):
                    grad_maps[base + r, :, at] = sums[r]
                for dc in range(SIDE):
                    grads = [grad_pad[base + REACH + r, EDGE : EDGE + side_cells, :] for r in range(GROUP)]
                    acc = [None] * SIDE
                    for j in range(GROUP + SIDE - 1):
                        row = pad[base + j, EDGE - REACH + dc : EDGE - REACH + dc + side_cells, :]
                        for r in range(GROUP):
                            dr = j - r
                            if 0 <= dr < SIDE:
                                term = row * grads[r]
                                acc[dr] = term if acc[dr] is None else acc[dr] + term
                    for dr in range(SIDE):
                        tap_sums[dr * SIDE + dc] += jnp.sum(acc[dr].reshape(side_cells // 8, 8, LANES), axis=0)
                return inner

            lax.fori_loop(0, side_cells // GROUP, rows, 0)
            small_at[0, : SIDE * SIDE, at] = jnp.sum(tap_sums[...], axis=1)
            return carry

        lax.fori_loop(first, last, one, 0)

    small_masks = [(0, 1), (1, 0), (2, 0), (0, 2), (0, 4), (0, 1)]
    small_half = small_in.shape[0] // 2
    small_rows = pl.ds(pl.multiple_of(side * small_half, 8), small_half)
    small_rest = pl.ds(pl.multiple_of((1 - side) * small_half, 8), small_half)

    def small_send(s, rows):
        return send(small_at.at[s, rows], small_from.at[s, rows], small_masks[s])

    def small_step(s, copy):
        copy.wait_recv()
        small_at[s + 1, small_rows] = small_at[s, small_rows] + small_from[s, small_rows]
        return small_send(s + 1, small_rows)

    def small_end(copy):
        copy.wait_recv()
        small_out[small_rows] = small_at[5, small_rows]
        small_out[small_rest] = small_from[5, small_rest]

    thin_parts = [[group[2]] for group in thin]
    parts_reduce, parts_expand = wide[0][3], wide[1][3]
    thin_sent = [thin_two(i) for i in range(4)]
    one_reduce = wide_one(0, False)
    norm_back()
    blocks(0, count // 6)
    two_reduce = wide_two(0, one_reduce)
    blocks(count // 6, count // 3)
    thin_high = [thin_three(i, thin_sent[i]) for i in range(4)]
    one_expand = wide_one(1, True)
    blocks(count // 3, count // 2)
    high_reduce = [wide_three(0, two_reduce), heights(4, parts_reduce, 1)]
    thin_high = [further(i, thin_parts[i], 0, thin_high[i]) for i in range(4)]
    blocks(count // 2, count)
    small = small_send(0, small_rest)
    small = small_step(0, small)
    high_reduce = [further(4, parts_reduce, k, high_reduce[k]) for k in range(2)]
    small = small_step(1, small)
    two_expand = wide_two(1, one_expand)
    swaps = [total(i, thin_parts[i], 0, thin_high[i]) for i in range(4)]
    small = small_step(2, small)
    small = small_step(3, small)
    high_low = wide_three(1, two_expand)
    thin_out = [spread(i, swaps[i]) for i in range(4)]
    small = small_step(4, small)
    swap_reduce = [total(4, parts_reduce, k, high_reduce[k]) for k in range(2)]
    high_low = further(5, parts_expand, 0, high_low)
    high_high = heights(5, parts_expand, 1)
    small_end(small)
    swap_reduce[0].wait_recv()
    reduce_out = spread(4, swap_reduce[1])
    last = [relay(group) for group in thin_out]
    swap_low = total(5, parts_expand, 0, high_low)
    high_high = further(5, parts_expand, 1, high_high)
    low_out = spread(5, swap_low, 0, 2)
    last.append(relay(reduce_out))
    swap_high = total(5, parts_expand, 1, high_high)
    high_out = spread(5, swap_high, 1, 2)
    last.append(relay(low_out))
    last.append(relay(high_out))
    for group in thin_out + [reduce_out, low_out, high_out]:
        for entry in group:
            entry[2].wait()
    for group in last:
        for copy in group:
            copy.wait_recv()
    for copy in copies:
        copy.wait_send()


def scatter_gradients(part_reduce, part_expand, landed, thins, small, grad_normed, mixed, maps, taps, gain):
    side, _, channels = maps.shape
    low, full = jnp.bfloat16, jnp.float32
    anyspec, whole = pl.BlockSpec(memory_space=pl.ANY), pl.BlockSpec(memory_space=VMEM)
    dma = pltpu.SemaphoreType.DMA
    finals = [(t.shape[3], t.shape[4]) for t in thins] + [w.shape[4:] for w in (part_reduce, part_expand)]
    scratch = []
    for w in (part_reduce, part_expand):
        shape = w.shape[:3] + (w.shape[4], w.shape[5] // 2)
        landing = [jax.ShapeDtypeStruct(shape, low)] * 2
        scratch += [VMEM(shape, low)] * 2
    scratch += [VMEM(w.shape[:2] + (w.shape[4], w.shape[5] // 2), low) for w in (part_reduce, part_expand) for _ in range(2)]
    scratch += [VMEM((2, 2, 2, w.shape[4], w.shape[5] // 2), low) for w in (part_reduce, part_expand)]
    scratch += [VMEM(t.shape[:2] + t.shape[3:], low) for t in thins] * 2
    scratch += [VMEM((3, 2) + f, low) for f in finals]
    scratch += [VMEM((2,) + f, low) for f in finals]
    scratch += [VMEM((f[0], 2 * f[1]), low) for f in finals]
    edge = (side + 2 * REACH, side + 2 * EDGE, LANES)
    scratch += [VMEM((6,) + small.shape, full)] * 2
    scratch += [VMEM(edge, full)] * 2 + [VMEM((SIDE * SIDE, 8, LANES), full)]
    scratch += [dma((120,)), dma((120,)), dma((48,))]
    results = pl.pallas_call(
        scatter_kernel,
        out_shape=[jax.ShapeDtypeStruct(maps.shape, full), jax.ShapeDtypeStruct(small.shape, full)]
        + [jax.ShapeDtypeStruct((4, f[0], 2 * f[1]), low) for f in finals]
        + landing,
        in_specs=[anyspec] * 10 + [whole] * 6,
        out_specs=[whole] * 2 + [anyspec] * 8,
        scratch_shapes=scratch,
        compiler_params=pltpu.CompilerParams(
            collective_id=1, has_side_effects=True, vmem_limit_bytes=60 * 2**20
        ),
    )(part_reduce, part_expand, *landed, *thins, small, grad_normed, mixed, maps, taps, gain.reshape(1, channels))
    return results[0], results[1], results[2:8]


def layer_norm(values, gain_vec):
    centred = values - jnp.mean(values, axis=-1, keepdims=True)
    spread = jnp.mean(centred * centred, axis=-1, keepdims=True)
    return centred * lax.rsqrt(spread + 1e-06) * gain_vec


def depthwise(feature_map, taps_table, kernel_side):
    half_side = kernel_side // 2
    padded = jnp.pad(feature_map, ((0, 0), (half_side, half_side), (half_side, half_side), (0, 0)))
    map_side = feature_map.shape[1]
    accum_sum = jnp.zeros(feature_map.shape, feature_map.dtype)
    for offset_row in range(kernel_side):
        for offset_col in range(kernel_side):
            window = padded[
                :, offset_row : offset_row + map_side, offset_col : offset_col + map_side, :
            ]
            accum_sum = accum_sum + window * taps_table[offset_row * kernel_side + offset_col]
    return accum_sum


def section_depthwise(grid_field, grid_kernel):
    return depthwise(grid_field, grid_kernel, 7)


def adapter_depthwise(grid_field, grid_kernel):
    return depthwise(grid_field, grid_kernel, 3)


def swap(value, axis, mask):
    size = lax.axis_size(axis)
    return lax.ppermute(value, axis, [(i, i ^ mask) for i in range(size)])


def pick(value, index, axis):
    return lax.dynamic_index_in_dim(value, index, axis, keepdims=False)


def add_low(left, right):
    return (left.astype(jnp.float32) + right.astype(jnp.float32)).astype(jnp.bfloat16)


def place():
    path, dev = lax.axis_index("path"), lax.axis_index("dev")
    return path, path // 2, lax.rem(path, 2), dev // 2, lax.rem(dev, 2)


def both_images(rows):
    return jnp.concatenate([rows, swap(rows, "dev", 1)])


def pair_halves(grads):
    side = place()[4]
    half = grads.shape[1] // 2
    low, high = grads[:, :half], grads[:, half:]
    theirs = swap(jnp.where(side == 0, high, low), "dev", 1)
    return jnp.concatenate([jnp.where(side == 0, low, high), theirs])


def pair_product(rows, grads):
    result = lax.dot_general(rows, grads, (((0,), (0,)), ((), ())), preferred_element_type=jnp.float32)
    return result.astype(jnp.bfloat16).reshape(4, 2, 2, 2, rows.shape[1] // 32, grads.shape[1])


def pair_gradient(rows, grads):
    return pair_product(rows, pair_halves(grads))


def across_half(share, axis):
    return swap(pick(share, 1 - place()[2], axis), "path", 1)


def up_half(share, axis):
    return swap(pick(share, 1 - place()[1], axis), "path", 2)


def across_sum(share, axis, other):
    return add_low(pick(share, place()[2], axis), other)


def up_sum(share, axis, other):
    return add_low(pick(share, place()[1], axis), other)


def tie(*values):
    return lax.optimization_barrier(values)


def finish(pieces):
    return pieces.reshape(-1, pieces.shape[2]).astype(jnp.float32)


def plain_sum(rows, grads):
    product = lax.dot_general(
        rows, grads, (((0,), (0,)), ((), ())), preferred_element_type=jnp.float32
    ).astype(jnp.bfloat16)
    share = lax.psum_scatter(product, "dev", scatter_dimension=0, tiled=True)
    return lax.psum(share, "path").astype(jnp.float32)


def local(
    inputs,
    hires_maps,
    target_path,
    cotangent,
    attn_gain,
    w_qkv,
    w_out,
    mlp_gain,
    w_fc1,
    w_fc2,
    w_adapter,
    adapter_kernel,
    merge_gate,
    section_kernel,
    section_gain,
    w_expand,
    w_reduce,
    layer_scale,
):
    tuned = lax.axis_size("path") == 4 and lax.axis_size("dev") == 8
    weights = (w_expand, w_reduce, w_adapter, w_qkv, w_out, w_fc1, w_fc2)
    if tuned:
        ordered, section_mixed, section_rows, spread_targets, expanded, block_active, block_reduced, features = gather_weights(
            [weights[i] for i in GATHER_ORDER],
            hires_maps[0],
            section_kernel,
            section_gain,
            layer_scale,
            target_path,
            GATHER_ORDER.index(0),
            GATHER_ORDER.index(1),
        )
        fulls = [ordered[GATHER_ORDER.index(i)] for i in range(len(weights))]
    else:
        fulls = [lax.all_gather(shard, "dev", axis=0, tiled=True) for shard in weights]
    full_expand, full_reduce, full_adapter, full_qkv, full_out, full_fc1, full_fc2 = fulls
    path_count = lax.axis_size("path")
    maps_float = hires_maps.astype(jnp.float32)
    map_side = maps_float.shape[1]
    channels = maps_float.shape[3]
    grid_side = map_side // 2
    tokens = grid_side * grid_side
    quarter_rows = tokens // path_count
    model_width = inputs.shape[2]
    head_count = model_width // HEAD_DIM
    score_scale = HEAD_DIM ** (-0.5)
    if not tuned:
        section_mixed, section_back = jax.vjp(section_depthwise, maps_float, section_kernel)
        section_normed, section_norm_back = jax.vjp(layer_norm, section_mixed, section_gain)
    if tuned:
        _, section_gelu_back = jax.vjp(jax.nn.gelu, expanded)
        block_active = block_active.reshape(tokens, -1)
        block_reduced = block_reduced.reshape(tokens, channels)
    else:
        section_rows = section_normed.reshape(-1, channels).astype(jnp.bfloat16)
        expanded = jnp.dot(section_rows, full_expand, preferred_element_type=jnp.float32)
        activated, section_gelu_back = jax.vjp(jax.nn.gelu, expanded)
        activated_low = activated.astype(jnp.bfloat16)
        reduced = jnp.dot(activated_low, full_reduce, preferred_element_type=jnp.float32).reshape(
            maps_float.shape
        )
        section_out = maps_float + layer_scale * reduced
        pooled = jnp.mean(
            section_out.reshape(grid_side, 2, grid_side, 2, channels), axis=(1, 3)
        ).reshape(tokens, channels)
    if not tuned:
        pieces = pooled.astype(jnp.bfloat16).reshape(path_count, quarter_rows, channels)
        own_target = jnp.broadcast_to(target_path, (path_count, 1))
        spread_pieces = lax.all_to_all(pieces, "path", split_axis=0, concat_axis=0, tiled=True)
        spread_targets = lax.all_to_all(own_target, "path", split_axis=0, concat_axis=0, tiled=True)
    selector = (
        jnp.arange(path_count, dtype=jnp.int32)[:, None] == spread_targets.reshape(1, path_count)
    ).astype(jnp.float32)
    if not tuned:
        routed = jnp.einsum("pq,qtc->ptc", selector, spread_pieces.astype(jnp.float32)).astype(jnp.bfloat16)
        arrived = lax.all_to_all(routed, "path", split_axis=0, concat_axis=0, tiled=True)
        features = arrived.reshape(tokens, channels)
    adapted = jnp.dot(features, full_adapter, preferred_element_type=jnp.float32)
    spread_map, adapter_back = jax.vjp(
        adapter_depthwise, adapted.reshape(1, grid_side, grid_side, model_width), adapter_kernel
    )
    spread_rows = spread_map.reshape(tokens, model_width)
    gate_factor = jnp.tanh(merge_gate)
    hidden_in = inputs[0].astype(jnp.float32) + gate_factor * spread_rows
    normed_one, norm_one_back = jax.vjp(layer_norm, hidden_in, attn_gain)
    attn_rows = normed_one.astype(jnp.bfloat16)
    projected = jnp.dot(attn_rows, full_qkv, preferred_element_type=jnp.float32).astype(
        jnp.bfloat16
    )
    queries = projected[:, :model_width].reshape(tokens, head_count, HEAD_DIM)
    key_rows = projected[:, model_width : 2 * model_width].reshape(tokens, head_count, HEAD_DIM)
    values = projected[:, 2 * model_width :].reshape(tokens, head_count, HEAD_DIM)
    scores = (
        jnp.einsum("thd,shd->hts", queries, key_rows, preferred_element_type=jnp.float32)
        * score_scale
    )
    probs = jax.nn.softmax(scores, axis=-1)
    probs_low = probs.astype(jnp.bfloat16)
    attn_mixed = jnp.einsum("hts,shd->thd", probs_low, values, preferred_element_type=jnp.float32)
    attn_mixed = attn_mixed.astype(jnp.bfloat16).reshape(tokens, model_width)
    attended = jnp.dot(attn_mixed, full_out, preferred_element_type=jnp.float32)
    hidden_mid = hidden_in + attended
    normed_two, norm_two_back = jax.vjp(layer_norm, hidden_mid, mlp_gain)
    mlp_rows = normed_two.astype(jnp.bfloat16)
    raised = jnp.dot(mlp_rows, full_fc1, preferred_element_type=jnp.float32)
    lifted_value, gelu_back = jax.vjp(jax.nn.gelu, raised)
    lifted = lifted_value.astype(jnp.bfloat16)
    lowered = jnp.dot(lifted, full_fc2, preferred_element_type=jnp.float32)
    result = (hidden_mid + lowered)[None].astype(jnp.bfloat16)
    grad_out = cotangent[0].astype(jnp.float32)
    grad_out_low = grad_out.astype(jnp.bfloat16)
    if tuned:
        part_fc2 = pair_gradient(both_images(lifted), grad_out_low)
    else:
        grad_fc2_w = plain_sum(lifted, grad_out_low)
    grad_lifted = jnp.dot(grad_out_low, full_fc2.T, preferred_element_type=jnp.float32)
    grad_raised = gelu_back(grad_lifted)[0].astype(jnp.bfloat16)
    if tuned:
        part_fc1 = pair_gradient(both_images(mlp_rows), grad_raised)
    else:
        grad_fc1_w = plain_sum(mlp_rows, grad_raised)
    grad_normed_two = jnp.dot(grad_raised, full_fc1.T, preferred_element_type=jnp.float32)
    grad_mid_norm, grad_mlp_gain = norm_two_back(grad_normed_two)
    grad_mid = grad_out + grad_mid_norm
    grad_attended = grad_mid.astype(jnp.bfloat16)
    if tuned:
        part_out = pair_gradient(both_images(attn_mixed), grad_attended)
    else:
        grad_out_w = plain_sum(attn_mixed, grad_attended)
    grad_mixed = jnp.dot(grad_attended, full_out.T, preferred_element_type=jnp.float32)
    grad_mixed = grad_mixed.astype(jnp.bfloat16).reshape(tokens, head_count, HEAD_DIM)
    grad_probs = jnp.einsum("thd,shd->hts", grad_mixed, values, preferred_element_type=jnp.float32)
    grad_values = jnp.einsum(
        "hts,thd->shd", probs_low, grad_mixed, preferred_element_type=jnp.float32
    )
    grad_scores = probs * (grad_probs - jnp.sum(grad_probs * probs, axis=-1, keepdims=True))
    grad_scores = grad_scores.astype(jnp.bfloat16)
    grad_queries = (
        jnp.einsum("hts,shd->thd", grad_scores, key_rows, preferred_element_type=jnp.float32)
        * score_scale
    )
    grad_keys = (
        jnp.einsum("hts,thd->shd", grad_scores, queries, preferred_element_type=jnp.float32)
        * score_scale
    )
    grad_projected = jnp.concatenate(
        [
            grad_queries.reshape(tokens, model_width),
            grad_keys.reshape(tokens, model_width),
            grad_values.reshape(tokens, model_width),
        ],
        axis=1,
    ).astype(jnp.bfloat16)
    if tuned:
        part_qkv = pair_gradient(both_images(attn_rows), grad_projected)
    else:
        grad_qkv_w = plain_sum(attn_rows, grad_projected)
    grad_normed_one = jnp.dot(grad_projected, full_qkv.T, preferred_element_type=jnp.float32)
    grad_in_norm, grad_attn_gain = norm_one_back(grad_normed_one)
    grad_in = grad_mid + grad_in_norm
    grad_merge = jnp.sum(grad_in * spread_rows, axis=0) * (1.0 - gate_factor * gate_factor)
    grad_spread = (grad_in * gate_factor).reshape(1, grid_side, grid_side, model_width)
    grad_adapted, grad_adapter_taps = adapter_back(grad_spread)
    grad_adapted_low = grad_adapted.reshape(tokens, model_width).astype(jnp.bfloat16)
    if tuned:
        part_adapter = pair_gradient(both_images(features), grad_adapted_low)
    else:
        grad_adapter_w = plain_sum(features, grad_adapted_low)
    grad_features = jnp.dot(grad_adapted_low, full_adapter.T, preferred_element_type=jnp.float32)
    grad_pieces = grad_features.astype(jnp.bfloat16).reshape(path_count, quarter_rows, channels)
    grad_routed = lax.all_to_all(grad_pieces, "path", split_axis=0, concat_axis=0, tiled=True)
    grad_unrouted = jnp.einsum("pq,ptc->qtc", selector, grad_routed.astype(jnp.float32)).astype(
        jnp.bfloat16
    )
    grad_home = lax.all_to_all(grad_unrouted, "path", split_axis=0, concat_axis=0, tiled=True)
    if tuned:
        part_rest = jnp.concatenate([part_out, part_adapter], axis=4)
        _, up, across, _, _ = place()
        going = [pick(part_fc2, 1 - across, 3), pick(part_fc1, 1 - up, 2), pick(part_qkv, 1 - across, 3), pick(part_rest, 1 - up, 2)]
        grad_home, part_fc2, part_fc1, part_qkv, part_rest, *going = tie(
            grad_home, part_fc2, part_fc1, part_qkv, part_rest, *going
        )
        half_fc2, half_fc1, half_qkv, half_rest = [swap(piece, "path", 1 + k % 2) for k, piece in enumerate(going)]
    grad_pooled = grad_home.astype(jnp.float32).reshape(tokens, channels)
    quarter = (grad_pooled * 0.25).reshape(1, grid_side, 1, grid_side, 1, channels)
    grad_section_out = jnp.broadcast_to(quarter, (1, grid_side, 2, grid_side, 2, channels)).reshape(
        maps_float.shape
    )
    if tuned:
        grad_scale = jnp.sum(grad_pooled * block_reduced, axis=0)
        block_grad = (grad_pooled * 0.25 * layer_scale).astype(jnp.bfloat16)
        grad_reduced = jnp.broadcast_to(
            block_grad.reshape(grid_side, 1, grid_side, 1, channels), (grid_side, 2, grid_side, 2, channels)
        ).reshape(-1, channels)
    else:
        grad_scale = jnp.sum((grad_section_out * reduced).reshape(-1, channels), axis=0)
        grad_reduced = (grad_section_out * layer_scale).reshape(-1, channels).astype(jnp.bfloat16)
    if tuned:
        part_reduce = pair_gradient(both_images(block_active), block_grad)
        columns = part_reduce.shape[5] // 2
        leaving = [
            pick(part_reduce[first : first + 2, ..., :columns], 1 - place()[2], 3) for first in (0, 2)
        ] + [pick(part_reduce[first : first + 2, ..., columns:], 1 - place()[1], 2) for first in (0, 2)]
        grad_reduced, part_reduce, *leaving = tie(grad_reduced, part_reduce, *leaving)
        landed = [swap(piece, "path", 1 + k // 2) for k, piece in enumerate(leaving)]
    else:
        grad_reduce_w = plain_sum(activated_low, grad_reduced)
    grad_activated = jnp.dot(grad_reduced, full_reduce.T, preferred_element_type=jnp.float32)
    grad_expanded = section_gelu_back(grad_activated)[0].astype(jnp.bfloat16)
    if tuned:
        grad_expanded, half_fc2, half_fc1 = tie(grad_expanded, half_fc2, half_fc1)
    else:
        grad_expand_w = plain_sum(section_rows, grad_expanded)
    grad_section_normed = jnp.dot(
        grad_expanded, full_expand.T, preferred_element_type=jnp.float32
    ).reshape(maps_float.shape)
    if tuned:
        halves_expand = pair_halves(grad_expanded)
        grad_section_normed, halves_expand, half_qkv, half_rest, landed[0], landed[2] = tie(
            grad_section_normed, halves_expand, half_qkv, half_rest, landed[0], landed[2]
        )
        part_expand = pair_product(both_images(section_rows), halves_expand)
        step_fc2, step_fc1 = across_sum(part_fc2, 3, half_fc2), up_sum(part_fc1, 2, half_fc1)
        step_qkv, step_rest = across_sum(part_qkv, 3, half_qkv), up_sum(part_rest, 2, half_rest)
        small_rows = jnp.concatenate(
            [
                jnp.zeros((section_kernel.shape[0] + 1, channels), jnp.float32),
                jnp.concatenate([grad_attn_gain, grad_mlp_gain, grad_merge, grad_adapter_taps.reshape(-1)]).reshape(-1, channels),
                grad_scale[None],
            ]
        )
        small_count = small_rows.shape[0]
        small_rows = jnp.pad(small_rows, ((0, -small_count % 16), (0, 0)))
        grad_maps, small_rows, pieces = scatter_gradients(
            part_reduce,
            part_expand,
            landed,
            [step_fc2, step_fc1, step_qkv, step_rest],
            small_rows,
            grad_section_normed[0],
            section_mixed,
            hires_maps[0],
            section_kernel,
            section_gain,
        )
        grad_maps = grad_maps[None] + grad_section_out
        split = part_out.shape[4]
        grad_fc2_w, grad_fc1_w, grad_qkv_w = [finish(piece) for piece in pieces[:3]]
        grad_out_w, grad_adapter_w = finish(pieces[3][:, :split]), finish(pieces[3][:, split:])
        grad_reduce_w, grad_expand_w = finish(pieces[4]), finish(pieces[5])
    else:
        grad_section_mixed, grad_section_gain = section_norm_back(grad_section_normed)
        grad_maps_conv, grad_section_taps = section_back(grad_section_mixed)
        grad_maps = grad_section_out + grad_maps_conv
    summed = (
        grad_qkv_w,
        grad_out_w,
        grad_fc1_w,
        grad_fc2_w,
        grad_adapter_w,
        grad_expand_w,
        grad_reduce_w,
    )
    if tuned:
        tap_count = section_kernel.shape[0]
        flat = small_rows[tap_count + 1 : small_count - 1].reshape(-1)
        small_sums = (
            flat[:model_width],
            flat[model_width : 2 * model_width],
            flat[2 * model_width : 3 * model_width],
            flat[3 * model_width :].reshape(adapter_kernel.shape),
            small_rows[tap_count],
            small_rows[:tap_count],
            small_rows[small_count - 1],
        )
    else:
        small_sums = lax.psum(
            (
                grad_attn_gain,
                grad_mlp_gain,
                grad_merge,
                grad_adapter_taps,
                grad_section_gain,
                grad_section_taps,
                grad_scale,
            ),
            ("path", "dev"),
        )
    return (
        result,
        grad_in[None],
        grad_maps,
        small_sums[0],
        summed[0],
        summed[1],
        small_sums[1],
        summed[2],
        summed[3],
        summed[4],
        small_sums[3],
        small_sums[2],
        small_sums[5],
        small_sums[4],
        summed[5],
        summed[6],
        small_sums[6],
    )


def solution(mesh):
    return jax.shard_map(
        local,
        mesh=mesh,
        in_specs=(
            P(("path", "dev"), None, None),
            P(("path", "dev"), None, None, None),
            P("path", "dev"),
            P(("path", "dev"), None, None),
            P(),
            P("dev", None),
            P("dev", None),
            P(),
            P("dev", None),
            P("dev", None),
            P("dev", None),
            P(),
            P(),
            P(),
            P(),
            P("dev", None),
            P("dev", None),
            P(),
        ),
        out_specs=(
            P(("path", "dev"), None, None),
            P(("path", "dev"), None, None),
            P(("path", "dev"), None, None, None),
            P(),
            P("dev", None),
            P("dev", None),
            P(),
            P("dev", None),
            P("dev", None),
            P("dev", None),
            P(),
            P(),
            P(),
            P(),
            P("dev", None),
            P("dev", None),
            P(),
        ),
        check_vma=False,
    )
```

```python
import functools

import jax
import jax.numpy as jnp
from jax import lax
from jax.experimental import pallas as pl
from jax.experimental.pallas import tpu as pltpu
from jax.sharding import PartitionSpec as P

HEAD_DIM = 64
MESH = pl.DeviceIdType.MESH
VMEM = pltpu.VMEM
SIDE, REACH, EDGE, GROUP, LANES = 7, 3, 8, 8, 128


def conv_rows(src, taps, group, flip, side):
    base = group * GROUP
    sums = [None] * GROUP
    for dc in range(SIDE):
        col = [taps((SIDE - 1 - dr) * SIDE + SIDE - 1 - dc if flip else dr * SIDE + dc) for dr in range(SIDE)]
        for j in range(GROUP + SIDE - 1):
            row = src[base + j, EDGE - REACH + dc : EDGE - REACH + dc + side, :]
            for r in range(GROUP):
                if 0 <= j - r < SIDE:
                    term = row * col[j - r]
                    sums[r] = term if sums[r] is None else sums[r] + term
    return sums


def clear_edges(pad, side):
    rows, columns, lanes = pad.shape[-3:]
    pad[:, :EDGE, :] = jnp.zeros((rows, EDGE, lanes), jnp.float32)
    pad[:, EDGE + side :, :] = jnp.zeros((rows, columns - EDGE - side, lanes), jnp.float32)
    pad[:REACH] = jnp.zeros((REACH, columns, lanes), jnp.float32)
    pad[REACH + side :] = jnp.zeros((rows - REACH - side, columns, lanes), jnp.float32)


def lane_block(block):
    return pl.ds(pl.multiple_of(block * LANES, LANES), LANES)


def mix_block(block, maps, taps, mixed, pad):
    side = maps.shape[0]
    at = lane_block(block)
    pad[REACH : REACH + side, EDGE : EDGE + side, :] = maps[:, :, at].astype(jnp.float32)

    def rows(group, carry):
        sums = conv_rows(pad, lambda t: taps[pl.ds(t, 1), at], group, False, side)
        for r in range(GROUP):
            mixed[group * GROUP + r, :, at] = sums[r]
        return carry

    lax.fori_loop(0, side // GROUP, rows, 0)


def mix_blocks(first, last, maps, taps, mixed, pad):
    def blocks(block, carry):
        mix_block(block, maps, taps, mixed, pad)
        return carry

    lax.fori_loop(first, last, blocks, 0)


def norm_all(gain, mixed, rows):
    side, _, channels = mixed.shape

    def norm(pair, carry):
        v = mixed[pl.ds(2 * pair, 2)].reshape(2 * side, channels)
        centred = v - jnp.mean(v, axis=-1, keepdims=True)
        scale = lax.rsqrt(jnp.mean(centred * centred, axis=-1, keepdims=True) + 1e-06)
        at = pl.ds(pl.multiple_of(pair * 2 * side, 2 * side), 2 * side)
        rows[at, :] = (centred * scale * gain[...]).astype(jnp.bfloat16)
        return carry

    lax.fori_loop(0, side // 2, norm, 0)


STEP = 512


def product(left, right, total, left_at, right_at):
    total[...] = jnp.zeros_like(total)

    def step(k, carry):
        here = pl.multiple_of(k * STEP, STEP)
        total[...] += jnp.dot(
            left[:, pl.ds(left_at + here, STEP)],
            right[pl.ds(here, STEP), pl.ds(pl.multiple_of(right_at, STEP), STEP)],
            preferred_element_type=jnp.float32,
        )
        return carry

    lax.fori_loop(0, right.shape[0] // STEP, step, 0)


def gather_jobs(shapes):
    jobs = []
    for w, (r, n) in enumerate(shapes):
        parts = max(1, round(r // 4 * n / (16 * 6144)))
        while n % (parts * STEP):
            parts -= 1
        jobs += [(w, r // 4, k * (n // parts), n // parts) for k in range(parts)]
    return jobs


def gather_kernel(jobs, count, expand, reduce, *refs):
    shards = refs[:count]
    maps, taps, gain, scale, target = refs[count : count + 5]
    fulls = refs[count + 5 : 2 * count + 5]
    mixed_out, rows_out, targets, expanded, block_active, block_reduced, features = refs[2 * count + 5 : 2 * count + 12]
    pad, wide_w, deep_w, total, stage, pair_sum, pooled, leaving, met, sorted_maps, landing = refs[2 * count + 12 : 2 * count + 23]
    mixed, rows, active = refs[2 * count + 23 : 2 * count + 26]
    zs, zr, ps, pr, cs, cr, os, orr, ls, ts, tr, ws, es, fs, fr, gs, gr, xs = refs[2 * count + 26 :]
    p, d = lax.axis_index("path"), lax.axis_index("dev")

    def at(m):
        return (p ^ m[0], d ^ m[1])

    masks = [(0, 1), (0, 2), (0, 4), (0, 6), (1, 0), (2, 0), (3, 0)]
    bar = pltpu.get_barrier_semaphore()
    for m in masks:
        pl.semaphore_signal(bar, inc=1, device_id=at(m), device_id_type=MESH)
    pl.semaphore_wait(bar, len(masks))

    def copy(src, dst, ss, rs, m):
        return pltpu.make_async_remote_copy(src, dst, ss, rs, device_id=at(m), device_id_type=MESH)

    def quarter(w, owner, q, nq, c0, nc):
        r = shards[w].shape[0]
        return fulls[w].at[pl.ds(pl.multiple_of(owner * r + q * nq, 16), nq), pl.ds(c0, nc)]

    J = len(jobs)

    def Z(i, k):
        w, nq, c0, nc = jobs[i]
        src = shards[w].at[pl.ds(pl.multiple_of(p * nq, 16), nq), pl.ds(c0, nc)]
        return copy(src, quarter(w, d, p, nq, c0, nc), zs.at[i, k], zr.at[i, k], (0, 2 * (k + 1)))

    def XY(i, k, axis):
        w, nq, c0, nc = jobs[i]
        ref = quarter(w, d ^ (2 * (k + 1)), p, nq, c0, nc)
        return copy(ref, ref, ps.at[i, k, axis], pr.at[i, k, axis], (1 + axis, 0))

    def DG(i, k, axis):
        w, nq, c0, nc = jobs[i]
        h = nc // 2
        ref = quarter(w, d ^ (2 * (k + 1)), p ^ (2 - axis), nq, c0 + axis * h, h)
        return copy(ref, ref, ps.at[i, k, 2 + axis], pr.at[i, k, 2 + axis], (1 + axis, 0))

    def S(i, k):
        w, nq, c0, nc = jobs[i]
        r = shards[w].shape[0]
        ref = fulls[w].at[pl.ds(pl.multiple_of((d ^ (2 * (k + 1))) * r, 16), r), pl.ds(c0, nc)]
        return copy(ref, ref, cs.at[i, k], cr.at[i, k], (0, 1))

    for i in range(min(AHEAD, J)):
        for k in range(3):
            Z(i, k).start()
    own = []
    for w in range(count):
        r = shards[w].shape[0]
        place = fulls[w].at[pl.ds(pl.multiple_of(d * r, 16), r)]
        pair = pltpu.make_async_copy(shards[w], place, ls.at[w]), copy(shards[w], place, os.at[w], orr.at[w], (0, 1))
        for c in pair:
            c.start()
        own.append(pair)
    targets[p] = target[...]
    named = [copy(target, targets.at[p], ts.at[m - 1], tr.at[m - 1], (m, 0)) for m in (1, 2, 3)]
    for c in named:
        c.start()
    clear_edges(pad, maps.shape[0])
    blocks = maps.shape[2] // LANES
    leaving_vmem = []

    def write_out(src, dst):
        c = pltpu.make_async_copy(src, dst, xs.at[len(leaving_vmem)])
        c.start()
        leaving_vmem.append(c)

    ready = set()

    def ensure(w):
        if w not in ready:
            ready.add(w)
            own[w][0].wait()
            own[w][1].wait_recv()

    def cell_row(row):
        side = maps.shape[0]
        return pl.ds(pl.multiple_of(row * side, 8), side)

    def pairs(value):
        blocks, half = value.shape[1] // LANES, value.shape[0] // 2
        for k in range(blocks):
            pair_sum[k] = value[:, k * LANES : (k + 1) * LANES]
        return [
            pair_sum[k, pl.ds(0, half, stride=2), :] + pair_sum[k, pl.ds(1, half, stride=2), :] for k in range(blocks)
        ]

    def expand_block(c0, nc):
        load = pltpu.make_async_copy(fulls[expand].at[:, pl.ds(c0, nc)], wide_w, ws.at[0])
        load.start()
        load.wait()

        def chunk(j, carry):
            here = pl.multiple_of(j * STEP, STEP)
            product(rows, wide_w, total, 0, here)
            stage[...] = total[...]
            low = jax.nn.gelu(total[...]).astype(jnp.bfloat16)
            active[:, pl.ds(c0 + here, STEP)] = low
            total[...] = low.astype(jnp.float32)

            def block_sums(h, inner):
                sums = pairs(total[cell_row(2 * h), :] + total[cell_row(2 * h + 1), :])
                for k, value in enumerate(sums):
                    lanes = pl.ds(pl.multiple_of(c0 + here + k * LANES, LANES), LANES)
                    block_active[h, :, lanes] = value.astype(jnp.bfloat16)
                return inner

            lax.fori_loop(0, maps.shape[0] // 2, block_sums, 0)
            out = pltpu.make_async_copy(stage, expanded.at[:, pl.ds(c0 + here, STEP)], es.at[0])
            out.start()
            out.wait()
            return carry

        lax.fori_loop(0, nc // STEP, chunk, 0)

    def reduce_block(c0, nc):
        load = pltpu.make_async_copy(fulls[reduce].at[:, pl.ds(c0, nc)], deep_w, ws.at[1])
        load.start()
        load.wait()
        cols = pl.ds(c0, nc)
        product(active, deep_w, total, 0, 0)
        side = maps.shape[0]

        def pool(h, carry):
            part = pairs(total[cell_row(2 * h), :] + total[cell_row(2 * h + 1), :])
            for k, value in enumerate(part):
                block_reduced[h, :, c0 + k * LANES : c0 + (k + 1) * LANES] = value * 0.25
            cells = pairs(maps[2 * h, :, cols].astype(jnp.float32) + maps[2 * h + 1, :, cols].astype(jnp.float32))
            for k, value in enumerate(cells):
                lanes = slice(c0 + k * LANES, c0 + (k + 1) * LANES)
                pooled[h, :, lanes] = value * 0.25 + scale[:, lanes] * block_reduced[h, :, lanes]
            return carry

        lax.fori_loop(0, side // 2, pool, 0)

    parts = maps.shape[2] // 4

    def hop(src, dst, ss, rs):
        return [copy(src.at[p ^ m], dst.at[p], ss.at[m - 1], rs.at[m - 1], (m, 0)) for m in (1, 2, 3)]

    def route_one():
        for k in range(4):
            leaving[k] = pooled[..., k * parts : (k + 1) * parts].reshape(leaving.shape[1:]).astype(jnp.bfloat16)
        met[p] = leaving[p]
        sent = hop(leaving, met, fs, fr)
        for c in sent:
            c.start()
        return sent

    def route_two(sent):
        for c in sent + named:
            c.wait()
        for k in range(4):
            chosen = jnp.zeros(met.shape[1:], jnp.float32)
            for q in range(4):
                here = targets[q, :1, :1] == k
                chosen += jnp.where(here, met[q].astype(jnp.float32), 0.0)
            sorted_maps[k] = chosen.astype(jnp.bfloat16)
        landing[p] = sorted_maps[p]
        sent = hop(sorted_maps, landing, gs, gr)
        for c in sent:
            c.start()
        return sent

    def route_three(sent):
        for c in sent:
            c.wait()
        for k in range(4):
            features[:, k * parts : (k + 1) * parts] = landing[k]

    last_reduce = max(i for i in range(J) if jobs[i][0] == reduce)
    routed = None
    for i in range(J + 3):
        if i < J:
            for k in range(3):
                Z(i, k).wait_recv()
                XY(i, k, 0).start()
                XY(i, k, 1).start()
            if i + AHEAD < J:
                for k in range(3):
                    Z(i + AHEAD, k).start()
        if 0 <= i - 1 < J:
            for k in range(3):
                XY(i - 1, k, 0).wait_recv()
                DG(i - 1, k, 1).start()
                XY(i - 1, k, 1).wait_recv()
                DG(i - 1, k, 0).start()
        if 0 <= i - 2 < J:
            for k in range(3):
                DG(i - 2, k, 0).wait_recv()
                DG(i - 2, k, 1).wait_recv()
                S(i - 2, k).start()
        if i < MIX_STEPS:
            mix_blocks(i * blocks // MIX_STEPS, (i + 1) * blocks // MIX_STEPS, maps, taps, mixed, pad)
        if i + 1 == MIX_STEPS:
            norm_all(gain, mixed, rows)
            write_out(mixed, mixed_out)
            write_out(rows, rows_out)
        if 0 <= i - 3 < J:
            for k in range(3):
                S(i - 3, k).wait_recv()
            w, _, c0, nc = jobs[i - 3]
            ensure(w)
            if w == expand:
                expand_block(c0, nc)
            if w == reduce:
                reduce_block(c0, nc)
            if i - 3 == last_reduce:
                routed = route_one()
            if i - 3 == last_reduce + 1:
                routed = route_two(routed)
            if i - 3 == last_reduce + 2:
                route_three(routed)
    for c in leaving_vmem:
        c.wait()
    for w in range(count):
        ensure(w)
        own[w][1].wait_send()
    for i in range(J):
        for k in range(3):
            Z(i, k).wait_send()
            S(i, k).wait_send()
            for a in range(2):
                XY(i, k, a).wait_send()
                DG(i, k, a).wait_send()


AHEAD = 3
MIX_STEPS = 3
GATHER_ORDER = (4, 0, 1, 5, 6, 3, 2)


def gather_weights(shards, maps, taps, gain, scale, target, expand, reduce):
    shapes = [s.shape for s in shards]
    jobs = gather_jobs(shapes)
    n, J = len(shards), len(jobs)
    side, _, channels = maps.shape
    cells, hidden = side * side, shapes[expand][1]
    wide = max(nc for w, _, _, nc in jobs if w == expand)
    low, full = jnp.bfloat16, jnp.float32
    anyspec, whole = pl.BlockSpec(memory_space=pl.ANY), pl.BlockSpec(memory_space=VMEM)
    dma = pltpu.SemaphoreType.DMA
    shape = jax.ShapeDtypeStruct
    results = pl.pallas_call(
        functools.partial(gather_kernel, jobs, n, expand, reduce),
        out_shape=[shape((8 * r, c), low) for r, c in shapes]
        + [
            shape(maps.shape, full),
            shape((cells, channels), low),
            shape((4, 8, LANES), jnp.int32),
            shape((cells, hidden), full),
            shape((side // 2, side // 2, hidden), low),
            shape((side // 2, side // 2, channels), full),
            shape((cells // 4, channels), low),
        ],
        in_specs=[anyspec] * n + [whole] * 5,
        out_specs=[anyspec] * n + [anyspec] * 2 + [whole] + [anyspec] + [whole] * 3,
        scratch_shapes=[
            VMEM((side + 2 * REACH, side + 2 * EDGE, LANES), full),
            VMEM((channels, wide), low),
            VMEM((hidden, STEP), low),
            VMEM((cells, STEP), full),
            VMEM((cells, STEP), full),
            VMEM((STEP // LANES, side, LANES), full),
            VMEM((side // 2, side // 2, channels), full),
            VMEM((4, cells // 4, channels // 4), low),
            VMEM((4, cells // 4, channels // 4), low),
            VMEM((4, cells // 4, channels // 4), low),
            VMEM((4, cells // 4, channels // 4), low),
            VMEM(maps.shape, full),
            VMEM((cells, channels), low),
            VMEM((cells, hidden), low),
        ]
        + [dma((J, 3)), dma((J, 3)), dma((J, 3, 4)), dma((J, 3, 4)), dma((J, 3)), dma((J, 3))]
        + [dma((n,)), dma((n,)), dma((n,)), dma((3,)), dma((3,)), dma((2,)), dma((1,))] + [dma((3,))] * 4 + [dma((4,))],
        compiler_params=pltpu.CompilerParams(
            collective_id=0, has_side_effects=True, vmem_limit_bytes=60 * 2**20
        ),
    )(
        *shards, maps, taps, gain.reshape(1, channels), scale.reshape(1, channels),
        jnp.broadcast_to(target, (8, LANES)),
    )
    rest = results[n:]
    return results[:n], rest[0], rest[1], rest[2][:, 0, 0], rest[3], rest[4], rest[5], rest[6]


def add_block(total, term):
    return (total.astype(jnp.float32) + term.astype(jnp.float32)).astype(jnp.bfloat16)


def scatter_kernel(
    big0, big1, land0a, land0b, land0c, land0d, t0, t1, t2, t3, small_in, grad_normed_in, mixed_in, maps_in, taps, gain,
    grad_maps, small_out, o0, o1, o2, o3, o4, o5, land1a, land1b,
    acc0a, acc0b, acc1a, acc1b, two0a, two0b, two1a, two1b, tmp0, tmp1,
    own0, own1, own2, own3, two0, two1, two2, two3,
    zr0, zr1, zr2, zr3, zr4, zr5, low0, low1, low2, low3, low4, low5,
    full0, full1, full2, full3, full4, full5,
    grad_normed, mixed, maps, small_at, small_from, pad, grad_pad, tap_sums, ssem, rsem, lsem,
):
    p, d = lax.axis_index("path"), lax.axis_index("dev")
    up, across, height, side = p // 2, lax.rem(p, 2), d // 2, lax.rem(d, 2)
    masks = [(0, 1), (0, 2), (0, 4), (0, 6), (1, 0), (2, 0), (3, 0)]
    bar = pltpu.get_barrier_semaphore()
    for m in masks:
        pl.semaphore_signal(bar, inc=1, device_id=(p ^ m[0], d ^ m[1]), device_id_type=MESH)
    pl.semaphore_wait(bar, len(masks))

    copies = []

    def send(src, dst, m):
        n = len(copies)
        copy = pltpu.make_async_remote_copy(
            src, dst, ssem.at[n], rsem.at[n], device_id=(p ^ m[0], d ^ m[1]), device_id_type=MESH
        )
        copies.append(copy)
        copy.start()
        return copy

    local = []

    def fetch(src, dst):
        copy = pltpu.make_async_copy(src, dst, lsem.at[len(local)])
        local.append(copy)
        copy.start()
        return copy

    thin = [(t0, own0, two0, True), (t1, own1, two1, False), (t2, own2, two2, True), (t3, own3, two3, False)]
    wide = [
        (big0, (acc0a, acc0b), ((land0a, land0b), (land0c, land0d)), (two0a, two0b), tmp0),
        (big1, (acc1a, acc1b), ((land1a,), (land1b,)), (two1a, two1b), tmp1),
    ]
    outs = [o0, o1, o2, o3, o4, o5]
    zrs, lows, wholes = [zr0, zr1, zr2, zr3, zr4, zr5], [low0, low1, low2, low3, low4, low5], [full0, full1, full2, full3, full4, full5]

    def thin_two(i):
        src, own, two, upward = thin[i]
        index, mask = (up, (2, 0)) if upward else (across, (1, 0))
        loaded = fetch(src.at[:, :, index], own)
        return loaded, send(src.at[:, :, 1 - index], two, mask)

    def wide_one(w, ours):
        src, acc, land, _, _ = wide[w]
        half = src.shape[5] // 2
        a, b = pl.ds(0, half), pl.ds(half, half)
        loaded = [fetch(src.at[:, :, :, across, :, a], acc[0]), fetch(src.at[:, :, up, :, :, b], acc[1])]
        if not ours:
            return loaded
        return loaded + [
            send(src.at[:, :, :, 1 - across, :, a], land[0][0], (1, 0)),
            send(src.at[:, :, 1 - up, :, :, b], land[1][0], (2, 0)),
        ]

    def wide_two(w, started):
        src, acc, land, two, tmp = wide[w]
        started[0].wait()
        started[1].wait()
        sent = []
        for copy in started[2:]:
            copy.wait_recv()
        for k in range(2):
            each = 4 // len(land[k])
            loads = [fetch(land[k][0].at[0], tmp.at[0])]
            for z in range(4):
                if z < 3:
                    loads.append(fetch(land[k][(z + 1) // each].at[(z + 1) % each], tmp.at[(z + 1) % 2]))
                loads[z].wait()
                for c in range(2):
                    for q in range(2):
                        acc[k][z, c, q] = add_block(acc[k][z, c, q], tmp[z % 2, c, q])
            index, mask = (up, (2, 0)) if k == 0 else (across, (1, 0))
            sent.append(send(acc[k].at[:, :, 1 - index], two[k], mask))
        return sent

    def columns_of(n, parts, k):
        half = zrs[n].shape[3] // len(parts)
        return pl.ds(k * half, half)

    def heights(n, parts, k):
        cols = columns_of(n, parts, k)
        return [send(parts[k].at[height ^ m], zrs[n].at[m // 2, :, :, cols], (0, 2)) for m in (1, 3)]

    def further(n, parts, k, sent):
        for copy in sent:
            copy.wait_recv()
        cols = columns_of(n, parts, k)
        for c in range(2):
            zrs[n][1, c, :, cols] = add_block(zrs[n][1, c, :, cols], parts[k][height ^ 2, c])
        return send(zrs[n].at[1, :, :, cols], zrs[n].at[2, :, :, cols], (0, 4))

    def thin_three(i, started):
        _, own, two, _ = thin[i]
        started[0].wait()
        started[1].wait_recv()
        for z in range(4):
            for c in range(2):
                two[z, c] = add_block(two[z, c], own[z, c])
        return heights(i, [two], 0)

    def wide_three(w, sent):
        _, acc, _, two, _ = wide[w]
        for k in range(2):
            index = up if k == 0 else across
            sent[k].wait_recv()
            for z in range(4):
                for c in range(2):
                    two[k][z, c] = add_block(two[k][z, c], acc[k][z, c, index])
        return heights(4 + w, two, 0)

    def total(n, parts, k, sent):
        sent.wait_recv()
        zr, low, whole = zrs[n], lows[n], wholes[n]
        size = zr.shape[3]
        half = size // len(parts)
        cols = slice(k * half, (k + 1) * half)
        for c in range(2):
            value = parts[k][height, c].astype(jnp.float32)
            for m in (0, 2):
                value = value + zr[m, c, :, cols].astype(jnp.float32)
            low[c, :, cols] = value.astype(jnp.bfloat16)
        place = (slice(None), pl.ds(pl.multiple_of(side * size + k * half, LANES), half))
        whole[place] = low[side, :, cols]
        return send(low.at[1 - side, :, cols], whole.at[place], (0, 1))

    def spread(n, swapped, first=0, parts=1):
        swapped.wait_recv()
        size = zrs[n].shape[3]
        group = []
        for c in range(2):
            cols = pl.ds(c * size + first * (size // parts), size // parts)
            src, dst = wholes[n].at[:, cols], outs[n].at[p, :, cols]
            group.append((n, cols, fetch(src, dst), send(src, dst, (1, 0)), send(src, dst, (2, 0))))
        return group

    def relay(group):
        sent = []
        for n, cols, _, along_x, along_y in group:
            half = cols.size // 2
            for k, (copy, other, mask) in enumerate(((along_x, 1, (2, 0)), (along_y, 2, (1, 0)))):
                copy.wait_recv()
                ref = outs[n].at[p ^ other, :, pl.ds(cols.start + k * half, half)]
                sent.append(send(ref, ref, mask))
        return sent

    side_cells, _, channels = maps.shape
    count = channels // LANES

    def norm_back():
        clear_edges(pad, side_cells)
        clear_edges(grad_pad, side_cells)
        small_at[0] = small_in[...]

        def norm(h, carry):
            v = mixed[h]
            centred = v - jnp.mean(v, axis=-1, keepdims=True)
            scale = lax.rsqrt(jnp.mean(centred * centred, axis=-1, keepdims=True) + 1e-06)
            unit = centred * scale
            grad = grad_normed[h]
            small_at[0, SIDE * SIDE : SIDE * SIDE + 1, :] += jnp.sum(grad * unit, axis=0, keepdims=True)
            grad = grad * gain[...]
            grad_maps[h] = scale * (
                grad - jnp.mean(grad, axis=-1, keepdims=True) - unit * jnp.mean(grad * unit, axis=-1, keepdims=True)
            )
            return carry

        lax.fori_loop(0, side_cells, norm, 0)

    def blocks(first, last):
        def one(block, carry):
            at = lane_block(block)
            inside = (slice(REACH, REACH + side_cells), slice(EDGE, EDGE + side_cells), slice(None))
            pad[inside] = maps[:, :, at].astype(jnp.float32)
            grad_pad[inside] = grad_maps[:, :, at]
            tap_sums[...] = jnp.zeros_like(tap_sums)

            def rows(group, inner):
                base = group * GROUP
                sums = conv_rows(grad_pad, lambda t: taps[pl.ds(t, 1), at], group, True, side_cells)
                for r in range(GROUP):
                    grad_maps[base + r, :, at] = sums[r]
                for dc in range(SIDE):
                    grads = [grad_pad[base + REACH + r, EDGE : EDGE + side_cells, :] for r in range(GROUP)]
                    acc = [None] * SIDE
                    for j in range(GROUP + SIDE - 1):
                        row = pad[base + j, EDGE - REACH + dc : EDGE - REACH + dc + side_cells, :]
                        for r in range(GROUP):
                            dr = j - r
                            if 0 <= dr < SIDE:
                                term = row * grads[r]
                                acc[dr] = term if acc[dr] is None else acc[dr] + term
                    for dr in range(SIDE):
                        tap_sums[dr * SIDE + dc] += jnp.sum(acc[dr].reshape(side_cells // 8, 8, LANES), axis=0)
                return inner

            lax.fori_loop(0, side_cells // GROUP, rows, 0)
            small_at[0, : SIDE * SIDE, at] = jnp.sum(tap_sums[...], axis=1)
            return carry

        lax.fori_loop(first, last, one, 0)

    small_masks = [(0, 1), (1, 0), (2, 0), (0, 2), (0, 4), (0, 1)]
    small_half = small_in.shape[0] // 2
    small_rows = pl.ds(pl.multiple_of(side * small_half, 8), small_half)
    small_rest = pl.ds(pl.multiple_of((1 - side) * small_half, 8), small_half)

    def small_send(s, rows):
        return send(small_at.at[s, rows], small_from.at[s, rows], small_masks[s])

    def small_step(s, copy):
        copy.wait_recv()
        small_at[s + 1, small_rows] = small_at[s, small_rows] + small_from[s, small_rows]
        return small_send(s + 1, small_rows)

    def small_end(copy):
        copy.wait_recv()
        small_out[small_rows] = small_at[5, small_rows]
        small_out[small_rest] = small_from[5, small_rest]

    thin_parts = [[group[2]] for group in thin]
    parts_reduce, parts_expand = wide[0][3], wide[1][3]
    thin_sent = [thin_two(i) for i in range(4)]
    arriving = [fetch(grad_normed_in, grad_normed), fetch(mixed_in, mixed), fetch(maps_in, maps)]
    one_reduce = wide_one(0, False)
    for copy in arriving:
        copy.wait()
    norm_back()
    blocks(0, count // 6)
    two_reduce = wide_two(0, one_reduce)
    blocks(count // 6, count // 3)
    thin_high = [thin_three(i, thin_sent[i]) for i in range(4)]
    one_expand = wide_one(1, True)
    blocks(count // 3, count // 2)
    high_reduce = [wide_three(0, two_reduce), heights(4, parts_reduce, 1)]
    thin_high = [further(i, thin_parts[i], 0, thin_high[i]) for i in range(4)]
    blocks(count // 2, count)
    small = small_send(0, small_rest)
    small = small_step(0, small)
    high_reduce = [further(4, parts_reduce, k, high_reduce[k]) for k in range(2)]
    small = small_step(1, small)
    two_expand = wide_two(1, one_expand)
    swaps = [total(i, thin_parts[i], 0, thin_high[i]) for i in range(4)]
    small = small_step(2, small)
    small = small_step(3, small)
    high_low = wide_three(1, two_expand)
    thin_out = [spread(i, swaps[i]) for i in range(4)]
    small = small_step(4, small)
    swap_reduce = [total(4, parts_reduce, k, high_reduce[k]) for k in range(2)]
    high_low = further(5, parts_expand, 0, high_low)
    high_high = heights(5, parts_expand, 1)
    small_end(small)
    swap_reduce[0].wait_recv()
    reduce_out = spread(4, swap_reduce[1])
    last = [relay(group) for group in thin_out]
    swap_low = total(5, parts_expand, 0, high_low)
    high_high = further(5, parts_expand, 1, high_high)
    low_out = spread(5, swap_low, 0, 2)
    last.append(relay(reduce_out))
    swap_high = total(5, parts_expand, 1, high_high)
    high_out = spread(5, swap_high, 1, 2)
    last.append(relay(low_out))
    last.append(relay(high_out))
    for group in thin_out + [reduce_out, low_out, high_out]:
        for entry in group:
            entry[2].wait()
    for group in last:
        for copy in group:
            copy.wait_recv()
    for copy in copies:
        copy.wait_send()


def scatter_gradients(part_reduce, part_expand, landed, thins, small, grad_normed, mixed, maps, taps, gain):
    side, _, channels = maps.shape
    low, full = jnp.bfloat16, jnp.float32
    anyspec, whole = pl.BlockSpec(memory_space=pl.ANY), pl.BlockSpec(memory_space=VMEM)
    dma = pltpu.SemaphoreType.DMA
    finals = [(t.shape[3], t.shape[4]) for t in thins] + [w.shape[4:] for w in (part_reduce, part_expand)]
    scratch = []
    for w in (part_reduce, part_expand):
        shape = w.shape[:3] + (w.shape[4], w.shape[5] // 2)
        landing = [jax.ShapeDtypeStruct(shape, low)] * 2
        scratch += [VMEM(shape, low)] * 2
    scratch += [VMEM(w.shape[:2] + (w.shape[4], w.shape[5] // 2), low) for w in (part_reduce, part_expand) for _ in range(2)]
    scratch += [VMEM((2, 2, 2, w.shape[4], w.shape[5] // 2), low) for w in (part_reduce, part_expand)]
    scratch += [VMEM(t.shape[:2] + t.shape[3:], low) for t in thins] * 2
    scratch += [VMEM((3, 2) + f, low) for f in finals]
    scratch += [VMEM((2,) + f, low) for f in finals]
    scratch += [VMEM((f[0], 2 * f[1]), low) for f in finals]
    edge = (side + 2 * REACH, side + 2 * EDGE, LANES)
    scratch += [VMEM(maps.shape, full)] * 2 + [VMEM(maps.shape, low)]
    scratch += [VMEM((6,) + small.shape, full)] * 2
    scratch += [VMEM(edge, full)] * 2 + [VMEM((SIDE * SIDE, 8, LANES), full)]
    scratch += [dma((120,)), dma((120,)), dma((48,))]
    results = pl.pallas_call(
        scatter_kernel,
        out_shape=[jax.ShapeDtypeStruct(maps.shape, full), jax.ShapeDtypeStruct(small.shape, full)]
        + [jax.ShapeDtypeStruct((4, f[0], 2 * f[1]), low) for f in finals]
        + landing,
        in_specs=[anyspec] * 10 + [whole] + [anyspec] * 3 + [whole] * 2,
        out_specs=[whole] * 2 + [anyspec] * 8,
        scratch_shapes=scratch,
        compiler_params=pltpu.CompilerParams(
            collective_id=1, has_side_effects=True, vmem_limit_bytes=60 * 2**20
        ),
    )(part_reduce, part_expand, *landed, *thins, small, grad_normed, mixed, maps, taps, gain.reshape(1, channels))
    return results[0], results[1], results[2:8]


def layer_norm(values, gain_vec):
    centred = values - jnp.mean(values, axis=-1, keepdims=True)
    spread = jnp.mean(centred * centred, axis=-1, keepdims=True)
    return centred * lax.rsqrt(spread + 1e-06) * gain_vec


def depthwise(feature_map, taps_table, kernel_side):
    half_side = kernel_side // 2
    padded = jnp.pad(feature_map, ((0, 0), (half_side, half_side), (half_side, half_side), (0, 0)))
    map_side = feature_map.shape[1]
    accum_sum = jnp.zeros(feature_map.shape, feature_map.dtype)
    for offset_row in range(kernel_side):
        for offset_col in range(kernel_side):
            window = padded[
                :, offset_row : offset_row + map_side, offset_col : offset_col + map_side, :
            ]
            accum_sum = accum_sum + window * taps_table[offset_row * kernel_side + offset_col]
    return accum_sum


def section_depthwise(grid_field, grid_kernel):
    return depthwise(grid_field, grid_kernel, 7)


def adapter_depthwise(grid_field, grid_kernel):
    return depthwise(grid_field, grid_kernel, 3)


def swap(value, axis, mask):
    size = lax.axis_size(axis)
    return lax.ppermute(value, axis, [(i, i ^ mask) for i in range(size)])


def pick(value, index, axis):
    return lax.dynamic_index_in_dim(value, index, axis, keepdims=False)


def add_low(left, right):
    return (left.astype(jnp.float32) + right.astype(jnp.float32)).astype(jnp.bfloat16)


def place():
    path, dev = lax.axis_index("path"), lax.axis_index("dev")
    return path, path // 2, lax.rem(path, 2), dev // 2, lax.rem(dev, 2)


def both_images(rows):
    return jnp.concatenate([rows, swap(rows, "dev", 1)])


def pair_halves(grads):
    side = place()[4]
    half = grads.shape[1] // 2
    low, high = grads[:, :half], grads[:, half:]
    theirs = swap(jnp.where(side == 0, high, low), "dev", 1)
    return jnp.concatenate([jnp.where(side == 0, low, high), theirs])


def pair_product(rows, grads):
    result = lax.dot_general(rows, grads, (((0,), (0,)), ((), ())), preferred_element_type=jnp.float32)
    return result.astype(jnp.bfloat16).reshape(4, 2, 2, 2, rows.shape[1] // 32, grads.shape[1])


def pair_gradient(rows, grads):
    return pair_product(rows, pair_halves(grads))


def across_half(share, axis):
    return swap(pick(share, 1 - place()[2], axis), "path", 1)


def up_half(share, axis):
    return swap(pick(share, 1 - place()[1], axis), "path", 2)


def across_sum(share, axis, other):
    return add_low(pick(share, place()[2], axis), other)


def up_sum(share, axis, other):
    return add_low(pick(share, place()[1], axis), other)


def tie(*values):
    return lax.optimization_barrier(values)


def finish(pieces):
    return pieces.reshape(-1, pieces.shape[2]).astype(jnp.float32)


def plain_sum(rows, grads):
    product = lax.dot_general(
        rows, grads, (((0,), (0,)), ((), ())), preferred_element_type=jnp.float32
    ).astype(jnp.bfloat16)
    share = lax.psum_scatter(product, "dev", scatter_dimension=0, tiled=True)
    return lax.psum(share, "path").astype(jnp.float32)


def local(
    inputs,
    hires_maps,
    target_path,
    cotangent,
    attn_gain,
    w_qkv,
    w_out,
    mlp_gain,
    w_fc1,
    w_fc2,
    w_adapter,
    adapter_kernel,
    merge_gate,
    section_kernel,
    section_gain,
    w_expand,
    w_reduce,
    layer_scale,
):
    tuned = lax.axis_size("path") == 4 and lax.axis_size("dev") == 8
    weights = (w_expand, w_reduce, w_adapter, w_qkv, w_out, w_fc1, w_fc2)
    if tuned:
        ordered, section_mixed, section_rows, spread_targets, expanded, block_active, block_reduced, features = gather_weights(
            [weights[i] for i in GATHER_ORDER],
            hires_maps[0],
            section_kernel,
            section_gain,
            layer_scale,
            target_path,
            GATHER_ORDER.index(0),
            GATHER_ORDER.index(1),
        )
        fulls = [ordered[GATHER_ORDER.index(i)] for i in range(len(weights))]
    else:
        fulls = [lax.all_gather(shard, "dev", axis=0, tiled=True) for shard in weights]
    full_expand, full_reduce, full_adapter, full_qkv, full_out, full_fc1, full_fc2 = fulls
    path_count = lax.axis_size("path")
    maps_float = hires_maps.astype(jnp.float32)
    map_side = maps_float.shape[1]
    channels = maps_float.shape[3]
    grid_side = map_side // 2
    tokens = grid_side * grid_side
    quarter_rows = tokens // path_count
    model_width = inputs.shape[2]
    head_count = model_width // HEAD_DIM
    score_scale = HEAD_DIM ** (-0.5)
    if not tuned:
        section_mixed, section_back = jax.vjp(section_depthwise, maps_float, section_kernel)
        section_normed, section_norm_back = jax.vjp(layer_norm, section_mixed, section_gain)
    if tuned:
        _, section_gelu_back = jax.vjp(jax.nn.gelu, expanded)
        block_active = block_active.reshape(tokens, -1)
        block_reduced = block_reduced.reshape(tokens, channels)
    else:
        section_rows = section_normed.reshape(-1, channels).astype(jnp.bfloat16)
        expanded = jnp.dot(section_rows, full_expand, preferred_element_type=jnp.float32)
        activated, section_gelu_back = jax.vjp(jax.nn.gelu, expanded)
        activated_low = activated.astype(jnp.bfloat16)
        reduced = jnp.dot(activated_low, full_reduce, preferred_element_type=jnp.float32).reshape(
            maps_float.shape
        )
        section_out = maps_float + layer_scale * reduced
        pooled = jnp.mean(
            section_out.reshape(grid_side, 2, grid_side, 2, channels), axis=(1, 3)
        ).reshape(tokens, channels)
    if not tuned:
        pieces = pooled.astype(jnp.bfloat16).reshape(path_count, quarter_rows, channels)
        own_target = jnp.broadcast_to(target_path, (path_count, 1))
        spread_pieces = lax.all_to_all(pieces, "path", split_axis=0, concat_axis=0, tiled=True)
        spread_targets = lax.all_to_all(own_target, "path", split_axis=0, concat_axis=0, tiled=True)
    selector = (
        jnp.arange(path_count, dtype=jnp.int32)[:, None] == spread_targets.reshape(1, path_count)
    ).astype(jnp.float32)
    if not tuned:
        routed = jnp.einsum("pq,qtc->ptc", selector, spread_pieces.astype(jnp.float32)).astype(jnp.bfloat16)
        arrived = lax.all_to_all(routed, "path", split_axis=0, concat_axis=0, tiled=True)
        features = arrived.reshape(tokens, channels)
    adapted = jnp.dot(features, full_adapter, preferred_element_type=jnp.float32)
    spread_map, adapter_back = jax.vjp(
        adapter_depthwise, adapted.reshape(1, grid_side, grid_side, model_width), adapter_kernel
    )
    spread_rows = spread_map.reshape(tokens, model_width)
    gate_factor = jnp.tanh(merge_gate)
    hidden_in = inputs[0].astype(jnp.float32) + gate_factor * spread_rows
    normed_one, norm_one_back = jax.vjp(layer_norm, hidden_in, attn_gain)
    attn_rows = normed_one.astype(jnp.bfloat16)
    projected = jnp.dot(attn_rows, full_qkv, preferred_element_type=jnp.float32).astype(
        jnp.bfloat16
    )
    queries = projected[:, :model_width].reshape(tokens, head_count, HEAD_DIM)
    key_rows = projected[:, model_width : 2 * model_width].reshape(tokens, head_count, HEAD_DIM)
    values = projected[:, 2 * model_width :].reshape(tokens, head_count, HEAD_DIM)
    scores = (
        jnp.einsum("thd,shd->hts", queries, key_rows, preferred_element_type=jnp.float32)
        * score_scale
    )
    probs = jax.nn.softmax(scores, axis=-1)
    probs_low = probs.astype(jnp.bfloat16)
    attn_mixed = jnp.einsum("hts,shd->thd", probs_low, values, preferred_element_type=jnp.float32)
    attn_mixed = attn_mixed.astype(jnp.bfloat16).reshape(tokens, model_width)
    attended = jnp.dot(attn_mixed, full_out, preferred_element_type=jnp.float32)
    hidden_mid = hidden_in + attended
    normed_two, norm_two_back = jax.vjp(layer_norm, hidden_mid, mlp_gain)
    mlp_rows = normed_two.astype(jnp.bfloat16)
    raised = jnp.dot(mlp_rows, full_fc1, preferred_element_type=jnp.float32)
    lifted_value, gelu_back = jax.vjp(jax.nn.gelu, raised)
    lifted = lifted_value.astype(jnp.bfloat16)
    lowered = jnp.dot(lifted, full_fc2, preferred_element_type=jnp.float32)
    result = (hidden_mid + lowered)[None].astype(jnp.bfloat16)
    grad_out = cotangent[0].astype(jnp.float32)
    grad_out_low = grad_out.astype(jnp.bfloat16)
    if tuned:
        part_fc2 = pair_gradient(both_images(lifted), grad_out_low)
    else:
        grad_fc2_w = plain_sum(lifted, grad_out_low)
    grad_lifted = jnp.dot(grad_out_low, full_fc2.T, preferred_element_type=jnp.float32)
    grad_raised = gelu_back(grad_lifted)[0].astype(jnp.bfloat16)
    if tuned:
        part_fc1 = pair_gradient(both_images(mlp_rows), grad_raised)
    else:
        grad_fc1_w = plain_sum(mlp_rows, grad_raised)
    grad_normed_two = jnp.dot(grad_raised, full_fc1.T, preferred_element_type=jnp.float32)
    grad_mid_norm, grad_mlp_gain = norm_two_back(grad_normed_two)
    grad_mid = grad_out + grad_mid_norm
    grad_attended = grad_mid.astype(jnp.bfloat16)
    if tuned:
        part_out = pair_gradient(both_images(attn_mixed), grad_attended)
    else:
        grad_out_w = plain_sum(attn_mixed, grad_attended)
    grad_mixed = jnp.dot(grad_attended, full_out.T, preferred_element_type=jnp.float32)
    grad_mixed = grad_mixed.astype(jnp.bfloat16).reshape(tokens, head_count, HEAD_DIM)
    grad_probs = jnp.einsum("thd,shd->hts", grad_mixed, values, preferred_element_type=jnp.float32)
    grad_values = jnp.einsum(
        "hts,thd->shd", probs_low, grad_mixed, preferred_element_type=jnp.float32
    )
    grad_scores = probs * (grad_probs - jnp.sum(grad_probs * probs, axis=-1, keepdims=True))
    grad_scores = grad_scores.astype(jnp.bfloat16)
    grad_queries = (
        jnp.einsum("hts,shd->thd", grad_scores, key_rows, preferred_element_type=jnp.float32)
        * score_scale
    )
    grad_keys = (
        jnp.einsum("hts,thd->shd", grad_scores, queries, preferred_element_type=jnp.float32)
        * score_scale
    )
    grad_projected = jnp.concatenate(
        [
            grad_queries.reshape(tokens, model_width),
            grad_keys.reshape(tokens, model_width),
            grad_values.reshape(tokens, model_width),
        ],
        axis=1,
    ).astype(jnp.bfloat16)
    if tuned:
        part_qkv = pair_gradient(both_images(attn_rows), grad_projected)
    else:
        grad_qkv_w = plain_sum(attn_rows, grad_projected)
    grad_normed_one = jnp.dot(grad_projected, full_qkv.T, preferred_element_type=jnp.float32)
    grad_in_norm, grad_attn_gain = norm_one_back(grad_normed_one)
    grad_in = grad_mid + grad_in_norm
    grad_merge = jnp.sum(grad_in * spread_rows, axis=0) * (1.0 - gate_factor * gate_factor)
    grad_spread = (grad_in * gate_factor).reshape(1, grid_side, grid_side, model_width)
    grad_adapted, grad_adapter_taps = adapter_back(grad_spread)
    grad_adapted_low = grad_adapted.reshape(tokens, model_width).astype(jnp.bfloat16)
    if tuned:
        part_adapter = pair_gradient(both_images(features), grad_adapted_low)
    else:
        grad_adapter_w = plain_sum(features, grad_adapted_low)
    grad_features = jnp.dot(grad_adapted_low, full_adapter.T, preferred_element_type=jnp.float32)
    grad_pieces = grad_features.astype(jnp.bfloat16).reshape(path_count, quarter_rows, channels)
    grad_routed = lax.all_to_all(grad_pieces, "path", split_axis=0, concat_axis=0, tiled=True)
    grad_unrouted = jnp.einsum("pq,ptc->qtc", selector, grad_routed.astype(jnp.float32)).astype(
        jnp.bfloat16
    )
    grad_home = lax.all_to_all(grad_unrouted, "path", split_axis=0, concat_axis=0, tiled=True)
    if tuned:
        part_rest = jnp.concatenate([part_out, part_adapter], axis=4)
        _, up, across, _, _ = place()
        going = [pick(part_fc2, 1 - across, 3), pick(part_fc1, 1 - up, 2), pick(part_qkv, 1 - across, 3), pick(part_rest, 1 - up, 2)]
        grad_home, part_fc2, part_fc1, part_qkv, part_rest, *going = tie(
            grad_home, part_fc2, part_fc1, part_qkv, part_rest, *going
        )
        half_fc2, half_fc1, half_qkv, half_rest = [swap(piece, "path", 1 + k % 2) for k, piece in enumerate(going)]
    grad_pooled = grad_home.astype(jnp.float32).reshape(tokens, channels)
    quarter = (grad_pooled * 0.25).reshape(1, grid_side, 1, grid_side, 1, channels)
    grad_section_out = jnp.broadcast_to(quarter, (1, grid_side, 2, grid_side, 2, channels)).reshape(
        maps_float.shape
    )
    if tuned:
        grad_scale = jnp.sum(grad_pooled * block_reduced, axis=0)
        block_grad = (grad_pooled * 0.25 * layer_scale).astype(jnp.bfloat16)
        grad_reduced = jnp.broadcast_to(
            block_grad.reshape(grid_side, 1, grid_side, 1, channels), (grid_side, 2, grid_side, 2, channels)
        ).reshape(-1, channels)
    else:
        grad_scale = jnp.sum((grad_section_out * reduced).reshape(-1, channels), axis=0)
        grad_reduced = (grad_section_out * layer_scale).reshape(-1, channels).astype(jnp.bfloat16)
    if tuned:
        part_reduce = pair_gradient(both_images(block_active), block_grad)
        columns = part_reduce.shape[5] // 2
        leaving = [
            pick(part_reduce[first : first + 2, ..., :columns], 1 - place()[2], 3) for first in (0, 2)
        ] + [pick(part_reduce[first : first + 2, ..., columns:], 1 - place()[1], 2) for first in (0, 2)]
        grad_reduced, part_reduce, *leaving = tie(grad_reduced, part_reduce, *leaving)
        landed = [swap(piece, "path", 1 + k // 2) for k, piece in enumerate(leaving)]
    else:
        grad_reduce_w = plain_sum(activated_low, grad_reduced)
    grad_activated = jnp.dot(grad_reduced, full_reduce.T, preferred_element_type=jnp.float32)
    grad_expanded = section_gelu_back(grad_activated)[0].astype(jnp.bfloat16)
    if tuned:
        grad_expanded, half_fc2, half_fc1 = tie(grad_expanded, half_fc2, half_fc1)
    else:
        grad_expand_w = plain_sum(section_rows, grad_expanded)
    grad_section_normed = jnp.dot(
        grad_expanded, full_expand.T, preferred_element_type=jnp.float32
    ).reshape(maps_float.shape)
    if tuned:
        halves_expand = pair_halves(grad_expanded)
        grad_section_normed, halves_expand, half_qkv, half_rest, landed[0], landed[2] = tie(
            grad_section_normed, halves_expand, half_qkv, half_rest, landed[0], landed[2]
        )
        part_expand = pair_product(both_images(section_rows), halves_expand)
        step_fc2, step_fc1 = across_sum(part_fc2, 3, half_fc2), up_sum(part_fc1, 2, half_fc1)
        step_qkv, step_rest = across_sum(part_qkv, 3, half_qkv), up_sum(part_rest, 2, half_rest)
        small_rows = jnp.concatenate(
            [
                jnp.zeros((section_kernel.shape[0] + 1, channels), jnp.float32),
                jnp.concatenate([grad_attn_gain, grad_mlp_gain, grad_merge, grad_adapter_taps.reshape(-1)]).reshape(-1, channels),
                grad_scale[None],
            ]
        )
        small_count = small_rows.shape[0]
        small_rows = jnp.pad(small_rows, ((0, -small_count % 16), (0, 0)))
        grad_maps, small_rows, pieces = scatter_gradients(
            part_reduce,
            part_expand,
            landed,
            [step_fc2, step_fc1, step_qkv, step_rest],
            small_rows,
            grad_section_normed[0],
            section_mixed,
            hires_maps[0],
            section_kernel,
            section_gain,
        )
        grad_maps = grad_maps[None] + grad_section_out
        split = part_out.shape[4]
        grad_fc2_w, grad_fc1_w, grad_qkv_w = [finish(piece) for piece in pieces[:3]]
        grad_out_w, grad_adapter_w = finish(pieces[3][:, :split]), finish(pieces[3][:, split:])
        grad_reduce_w, grad_expand_w = finish(pieces[4]), finish(pieces[5])
    else:
        grad_section_mixed, grad_section_gain = section_norm_back(grad_section_normed)
        grad_maps_conv, grad_section_taps = section_back(grad_section_mixed)
        grad_maps = grad_section_out + grad_maps_conv
    summed = (
        grad_qkv_w,
        grad_out_w,
        grad_fc1_w,
        grad_fc2_w,
        grad_adapter_w,
        grad_expand_w,
        grad_reduce_w,
    )
    if tuned:
        tap_count = section_kernel.shape[0]
        flat = small_rows[tap_count + 1 : small_count - 1].reshape(-1)
        small_sums = (
            flat[:model_width],
            flat[model_width : 2 * model_width],
            flat[2 * model_width : 3 * model_width],
            flat[3 * model_width :].reshape(adapter_kernel.shape),
            small_rows[tap_count],
            small_rows[:tap_count],
            small_rows[small_count - 1],
        )
    else:
        small_sums = lax.psum(
            (
                grad_attn_gain,
                grad_mlp_gain,
                grad_merge,
                grad_adapter_taps,
                grad_section_gain,
                grad_section_taps,
                grad_scale,
            ),
            ("path", "dev"),
        )
    return (
        result,
        grad_in[None],
        grad_maps,
        small_sums[0],
        summed[0],
        summed[1],
        small_sums[1],
        summed[2],
        summed[3],
        summed[4],
        small_sums[3],
        small_sums[2],
        small_sums[5],
        small_sums[4],
        summed[5],
        summed[6],
        small_sums[6],
    )


def solution(mesh):
    return jax.shard_map(
        local,
        mesh=mesh,
        in_specs=(
            P(("path", "dev"), None, None),
            P(("path", "dev"), None, None, None),
            P("path", "dev"),
            P(("path", "dev"), None, None),
            P(),
            P("dev", None),
            P("dev", None),
            P(),
            P("dev", None),
            P("dev", None),
            P("dev", None),
            P(),
            P(),
            P(),
            P(),
            P("dev", None),
            P("dev", None),
            P(),
        ),
        out_specs=(
            P(("path", "dev"), None, None),
            P(("path", "dev"), None, None),
            P(("path", "dev"), None, None, None),
            P(),
            P("dev", None),
            P("dev", None),
            P(),
            P("dev", None),
            P("dev", None),
            P("dev", None),
            P(),
            P(),
            P(),
            P(),
            P("dev", None),
            P("dev", None),
            P(),
        ),
        check_vma=False,
    )
```
